256 devices in a mesh: row: 8 (over x, core), col: 32 (over z, y).
Axes of the slice: x: 4, y: 4, z: 8, core: 2. Of those that a mesh axis runs over, the one named last changes fastest.
Arguments:
- start_block: float32 [32, 256, 4096], P(None, 'row', 'col'), may hold values from -6 to 6
- sea_mask: int32 [256, 4096], P('row', 'col'), may hold values 0 or 1
- depth_levels: int32 [256, 4096], P('row', 'col'), may hold values from 1 to 50
Outputs:
- basis: float32 [128, 256, 4096], P(None, 'row', 'col')
- alphas: float32 [3, 32, 32], replicated
- betas: float32 [3, 32, 32], replicated
The draws below stay inside these ranges and needn't reach their ends.
All inputs are finite; a program needn't handle non-finite values. No bound on the sum of `sea_mask` on one device may be relied on, other than what follows from the above.
Results may differ from the reference program's by a relative error of at most 0.00075.
Values sent between devices are 32-bit elements; how exact they have to be, the bound alone decides.
No kernel may reach another device: no remote copies, remote signals or barrier semaphores. Data moves between devices by JAX's collectives and lax.ppermute only.
A program may use at most 64 MiB of HBM per device.

```python
import math
import jax
import jax.numpy as jnp
from jax import lax

B = 32
ITERS = 3
LEVELS = 50
NLAT = 256
NLON = 4096


def draw_start_block(key, part):
    key = jax.random.fold_in(key, 11)
    subkeys = jax.random.split(key, 4)
    lat_angle = (jnp.arange(NLAT, dtype=jnp.float32) + 0.5) * (math.pi / NLAT)
    lon_angle = jnp.arange(NLON, dtype=jnp.float32) * (2.0 * math.pi / NLON)
    lat_phase = jax.random.uniform(subkeys[0], (B, 4, 5), jnp.float32, -math.pi, math.pi)
    lon_phase = jax.random.uniform(subkeys[1], (B, 4, 5), jnp.float32, -math.pi, math.pi)
    amplitude = jax.random.uniform(subkeys[2], (B, 4, 5), jnp.float32, -0.28, 0.28)
    background = jnp.clip(jax.random.normal(subkeys[3], (B, NLAT, NLON), jnp.float32), -4.0, 4.0) * 0.009
    result = background
    for lat_wave in range(4):
        for lon_wave in range(5):
            lat_part = jnp.cos(lat_wave * lat_angle[None, :] + lat_phase[:, lat_wave, lon_wave][:, None])
            lon_part = jnp.cos(lon_wave * lon_angle[None, :] + lon_phase[:, lat_wave, lon_wave][:, None])
            result = result + amplitude[:, lat_wave, lon_wave][:, None, None] * lat_part[:, :, None] * lon_part[:, None, :]
    return result


def place_ends(entries, own_key, least, high):
    longest = entries.shape.index(max(entries.shape))
    spots = []
    for shift in (0, 1):
        where = [jax.random.randint(jax.random.fold_in(own_key, axis), (), 0, length) for axis, length in enumerate(entries.shape)]
        where[longest] = (where[longest] + shift) % entries.shape[longest]
        spots.append(tuple(where))
    return entries.at[spots[0]].set(least).at[spots[1]].set(high)


def setup_inputs(seed: int = 0) -> dict:
    arg_keys = jax.random.split(jax.random.key(seed), 4)
    start_block = draw_start_block(jax.random.fold_in(arg_keys[3], 71), 0)
    sea_mask = place_ends((jax.random.randint(arg_keys[1], (NLAT, NLON), 0, 10) < 7).astype(jnp.int32), jax.random.fold_in(arg_keys[1], 1), 0, 1)
    depth_levels = place_ends(jax.random.randint(arg_keys[2], (NLAT, NLON), 1, LEVELS + 1), jax.random.fold_in(arg_keys[2], 1), 1, LEVELS).astype(jnp.int32)
    return dict(start_block=start_block, sea_mask=sea_mask, depth_levels=depth_levels)


HIGH = lax.Precision.HIGHEST
KAPPA = 1.5

def operate(block, mask, depth):
    lat_face = jnp.minimum(depth[:-1], depth[1:])
    lat_flux = lat_face[None] * (block[:, :-1] - block[:, 1:])
    zero_row = jnp.zeros((block.shape[0], 1, block.shape[2]), jnp.float32)
    total = jnp.concatenate([lat_flux, zero_row], axis=1) - jnp.concatenate([zero_row, lat_flux], axis=1)
    lon_face = jnp.minimum(depth, jnp.roll(depth, -1, axis=1))
    lon_flux = lon_face[None] * (block - jnp.roll(block, -1, axis=2))
    total = total + lon_flux - jnp.roll(lon_flux, 1, axis=2)
    return mask[None] * block + KAPPA * total

def factorize(flat, cells):
    gram = jnp.dot(flat.astype(jnp.float32), flat.T.astype(jnp.float32), precision=HIGH, preferred_element_type=jnp.float32) / cells
    lower = jnp.linalg.cholesky(gram)
    return (jax.scipy.linalg.solve_triangular(lower, flat, lower=True), lower.T)

def reference(start_block, sea_mask, depth_levels):
    mask = sea_mask.astype(jnp.float32)
    depth = mask * depth_levels.astype(jnp.float32) / LEVELS
    cells = float(NLAT * NLON)
    flat = (mask[None] * start_block).reshape(B, NLAT * NLON)
    first, unused = factorize(flat, cells)
    stacked = first
    alpha_list = []
    beta_list = []
    for step in range(ITERS):
        current = stacked[step * B:(step + 1) * B]
        image = operate(current.reshape(B, NLAT, NLON), mask, depth).reshape(B, NLAT * NLON)
        coeffs = jnp.dot(stacked.astype(jnp.float32), image.T.astype(jnp.float32), precision=HIGH, preferred_element_type=jnp.float32) / cells
        alpha_list.append(coeffs[step * B:(step + 1) * B])
        image = image - jnp.dot(coeffs.T.astype(jnp.float32), stacked.astype(jnp.float32), precision=HIGH, preferred_element_type=jnp.float32)
        fresh, upper = factorize(image, cells)
        beta_list.append(upper)
        stacked = jnp.concatenate([stacked, fresh], axis=0)
    return (stacked.reshape((ITERS + 1) * B, NLAT, NLON), jnp.stack(alpha_list), jnp.stack(beta_list))
```

```python
import jax
import jax.numpy as jnp
from jax import lax
from jax.sharding import Mesh, PartitionSpec as P

ITERS = 3
LEVELS = 50


HIGH = lax.Precision.HIGHEST
KAPPA = 1.5


def extended(block, sides, width, periodic):
    for axis, dim in sides:
        count = lax.axis_size(axis)
        forward = [(i, i + 1) for i in range(count - 1)]
        if periodic:
            forward.append((count - 1, 0))
        backward = [(target, source) for source, target in forward]
        low = lax.ppermute(
            lax.slice_in_dim(block, block.shape[dim] - width, None, axis=dim), axis, forward
        )
        high = lax.ppermute(lax.slice_in_dim(block, 0, width, axis=dim), axis, backward)
        block = jnp.concatenate([low, block, high], axis=dim)
    return block


def widen(field):
    rimmed = extended(field, ((("x", "core"), 1),), 1, False)
    return extended(rimmed, ((("z", "y"), 2),), 1, True)


def spread_sum(part, axes):
    count = lax.axis_size(axes)
    copies = jnp.broadcast_to(part[None], (count, *part.shape))
    return jnp.sum(lax.all_to_all(copies, axes, 0, 0), axis=0)


def total_sum(part):
    return spread_sum(spread_sum(part, ("x", "y")), ("core", "z"))


def inner(left, right, cells):
    return jnp.dot(left, right.T, precision=HIGH, preferred_element_type=jnp.float32) / cells


def lower_solve(lower, values):
    return jax.scipy.linalg.solve_triangular(lower, values, lower=True)


def finish(flat, gram):
    lower = jnp.linalg.cholesky(gram)
    return (lower_solve(lower, flat), lower.T)


def factorize(flat, cells):
    gram = total_sum(inner(flat, flat, cells))
    return finish(flat, gram)


def body(start_block, sea_mask, depth_levels):
    blocks, lats, lons = start_block.shape
    cells = float(lats * lons * lax.axis_size(("x", "core", "z", "y")))
    mask = sea_mask.astype(jnp.float32)
    depth = (mask * depth_levels.astype(jnp.float32) / LEVELS)[None]
    depth_wide = widen(depth)
    centre = depth_wide[:, 1:-1, 1:-1]
    weight_north = jnp.minimum(centre, depth_wide[:, :-2, 1:-1])
    weight_south = jnp.minimum(centre, depth_wide[:, 2:, 1:-1])
    weight_west = jnp.minimum(centre, depth_wide[:, 1:-1, :-2])
    weight_east = jnp.minimum(centre, depth_wide[:, 1:-1, 2:])
    flat = (mask[None] * start_block).reshape(blocks, lats * lons)
    alpha_list = []
    beta_list = []
    stacked, unused = factorize(flat, cells)
    for step in range(ITERS):
        current = stacked[step * blocks : (step + 1) * blocks]
        wide = widen(current.reshape(blocks, lats, lons))
        middle = wide[:, 1:-1, 1:-1]
        total = weight_north * (middle - wide[:, :-2, 1:-1]) + weight_south * (
            middle - wide[:, 2:, 1:-1]
        )
        total = (
            total
            + weight_west * (middle - wide[:, 1:-1, :-2])
            + weight_east * (middle - wide[:, 1:-1, 2:])
        )
        image = (mask[None] * middle + KAPPA * total).reshape(blocks, lats * lons)
        coeffs = total_sum(inner(stacked, image, cells))
        image = image - jnp.dot(
            coeffs.T, stacked, precision=HIGH, preferred_element_type=jnp.float32
        )
        fresh, upper = factorize(image, cells)
        alpha_list.append(coeffs[step * blocks : (step + 1) * blocks])
        beta_list.append(upper)
        stacked = jnp.concatenate([stacked, fresh], axis=0)
    return (
        stacked.reshape((ITERS + 1) * blocks, lats, lons),
        jnp.stack(alpha_list),
        jnp.stack(beta_list),
    )


def solution(mesh):
    torus = Mesh(mesh.devices.reshape(4, 2, 8, 4), ("x", "core", "z", "y"))
    row, col = ("x", "core"), ("z", "y")
    in_specs = (P(None, row, col), P(row, col), P(row, col))
    out_specs = (P(None, row, col), P(), P())
    return jax.shard_map(body, mesh=torus, in_specs=in_specs, out_specs=out_specs, check_vma=False)
```

```python
import jax
import jax.numpy as jnp
from jax import lax
from jax.experimental import pallas as pl
from jax.experimental.pallas import tpu as pltpu
from jax.sharding import Mesh, PartitionSpec as P

ITERS = 3
LEVELS = 50.0
KAPPA = 1.5
SHIFT = 3.0
CELLS = 1048576.0

B = 32
LAT = 32
LON = 128
RIM = 3
ROWS = LAT + 2 * RIM
WIDE = 2 * LON
ALL = (ITERS + 1) * B
HIGH = lax.Precision.HIGHEST
ROW, COL = ("x", "core"), ("z", "y")
NT = (((1,), (1,)), ((), ()))
PARAMS = pltpu.CompilerParams(vmem_limit_bytes=48 * 1024 * 1024)


def lanes_of(rows):
    return lax.broadcasted_iota(jnp.int32, (rows, LON), 1)


def call(kernel, outs, scratch=(), flops=0, moved=0):
    return pl.pallas_call(
        kernel,
        out_shape=tuple(jax.ShapeDtypeStruct(s, jnp.float32) for s in outs),
        scratch_shapes=list(scratch),
        compiler_params=PARAMS,
        cost_estimate=pl.CostEstimate(flops=flops, bytes_accessed=moved, transcendentals=0),
    )


def masked_row(lat, x_ref, mask_ref, depth_ref):
    mask = mask_ref[pl.ds(lat, 1), :].astype(jnp.float32)
    depth = mask * depth_ref[pl.ds(lat, 1), :].astype(jnp.float32) / LEVELS
    row = x_ref[pl.ds(lat, B, stride=LAT), :] * mask
    return jnp.concatenate([row, jnp.broadcast_to(depth, (8, LON))], axis=0)


def edge_rows(x_ref, mask_ref, depth_ref, top_ref, bottom_ref):
    for i in range(RIM):
        top_ref[i] = masked_row(i, x_ref, mask_ref, depth_ref)
        bottom_ref[i] = masked_row(LAT - RIM + i, x_ref, mask_ref, depth_ref)


def pack_sides(row, r, west, east):
    lane = lanes_of(B + 8)
    here = (lane >= RIM * r) & (lane < RIM * r + RIM)
    west = jnp.where(here, pltpu.roll(row, (RIM * r) % LON, 1), west)
    east = jnp.where(here, pltpu.roll(row, (RIM * r + RIM) % LON, 1), east)
    return west, east


def core_rows(x_ref, mask_ref, depth_ref, core_ref, west_ref, east_ref):
    west = east = jnp.zeros((B + 8, LON), jnp.float32)
    for i in range(LAT):
        row = masked_row(i, x_ref, mask_ref, depth_ref)
        core_ref[i] = row
        west, east = pack_sides(row, i + RIM, west, east)
    west_ref[...] = west
    east_ref[...] = east


def side_columns(north_ref, south_ref, part_west_ref, part_east_ref, west_ref, east_ref):
    west, east = part_west_ref[...], part_east_ref[...]
    for i in range(RIM):
        west, east = pack_sides(north_ref[i], i, west, east)
        west, east = pack_sides(south_ref[i], i + RIM + LAT, west, east)
    west_ref[...] = west
    east_ref[...] = east


def four(field):
    return jnp.concatenate([field] * (B // 8), axis=0)


def krylov(core_ref, north_ref, south_ref, west_ref, east_ref, s_ref, gram_ref,
           x_ref, k1_ref, k2_ref, h_ref, down_ref, right_ref):
    lane = lanes_of(B + 8)
    from_west, from_east = west_ref[...], east_ref[...]
    for r in range(ROWS):
        if r < RIM:
            row = north_ref[r]
        elif r < RIM + LAT:
            row = core_ref[r - RIM]
        else:
            row = south_ref[r - RIM - LAT]
        beyond = jnp.where(lane < RIM, pltpu.roll(from_east, (-RIM * r) % LON, 1), 0.0)
        beyond = jnp.where(lane >= LON - RIM, pltpu.roll(from_west, (LON - RIM - RIM * r) % LON, 1), beyond)
        full = jnp.concatenate([row, beyond], axis=1)
        x_ref[r] = full[:B]
        h_ref[r] = full[B:]
    for r in range(ROWS):
        h = h_ref[r]
        if r + 1 < ROWS:
            down_ref[r] = KAPPA * jnp.minimum(h, h_ref[r + 1])
        right_ref[r] = KAPPA * jnp.minimum(h, pltpu.roll(h, WIDE - 1, 1))
    for i in range(LAT):
        s_ref[i, :B, :] = x_ref[i + RIM][:, :LON]
    levels = ((x_ref, k1_ref, 1.0), (k1_ref, k2_ref, 1.0 + SHIFT), (k2_ref, None, 1.0 + SHIFT))
    for step, (source, target, shift) in enumerate(levels):
        first, last = step + 1, ROWS - 2 - step
        flux = four(down_ref[first - 1]) * (source[first - 1] - source[first])
        for r in range(first, last + 1):
            v = source[r]
            centre = jnp.where(h_ref[r] > 0.0, 1.0 - shift, -shift)
            down = four(down_ref[r]) * (v - source[r + 1])
            right = four(right_ref[r]) * (v - pltpu.roll(v, WIDE - 1, 1))
            new = four(centre) * v + ((down - flux) + (right - pltpu.roll(right, 1, 1)))
            flux = down
            if target is not None:
                target[r] = new
            if RIM <= r < RIM + LAT:
                s_ref[r - RIM, (step + 1) * B:(step + 2) * B, :] = new[:, :LON]
    total = jnp.zeros((ALL, ALL), jnp.float32)
    for i in range(0, LAT, 2):
        pair = jnp.concatenate([s_ref[i], s_ref[i + 1]], axis=1)
        total += lax.dot_general(pair, pair, NT, precision=HIGH, preferred_element_type=jnp.float32)
    gram_ref[...] = total


def spread(parts_ref, out_ref):
    total = parts_ref[0]
    for i in range(1, parts_ref.shape[0]):
        total += parts_ref[i]
    for i in range(out_ref.shape[0]):
        out_ref[i] = total


def basis(parts_ref, s_ref, q_ref, alpha_ref, beta_ref):
    total = parts_ref[0]
    for i in range(1, parts_ref.shape[0]):
        total += parts_ref[i]
    work = total * (1.0 / CELLS)
    lane = lax.broadcasted_iota(jnp.int32, (ALL, ALL), 1)
    sub = lax.broadcasted_iota(jnp.int32, (ALL, ALL), 0)
    for j in range(ALL):
        base = (j // 8) * 8
        low = work[base:]
        pivot = work[j:j + 1, j:j + 1]
        row = jnp.where(lane[:1] == j, 1.0, work[j:j + 1])
        ratio = jnp.where(sub[base:, :1] > j, low[:, j:j + 1] * (1.0 / pivot), 0.0)
        kept = jnp.where((lane[base:] == j) & (sub[base:] > j), 0.0, low)
        low = kept - ratio * row
        work = low if base == 0 else jnp.concatenate([work[:base], low], axis=0)
    pivots = jnp.sum(jnp.where(lane == sub, work, 0.0), axis=1, keepdims=True)
    scale = lax.rsqrt(pivots)
    inverse = scale * jnp.where(lane < sub, work, jnp.where(lane == sub, 1.0, 0.0))
    upper = scale * jnp.where(lane >= sub, work, 0.0)
    own = jnp.where(lane < B, 1.0, jnp.where(lane < ITERS * B, 1.0 + SHIFT, 0.0))
    image = inverse * own + jnp.where(lane >= B, pltpu.roll(inverse, B, 1), 0.0)
    coeffs = lax.dot_general(upper, image, NT, precision=HIGH, preferred_element_type=jnp.float32)
    for k in range(ITERS):
        here, after = slice(k * B, (k + 1) * B), slice((k + 1) * B, (k + 2) * B)
        alpha_ref[k] = coeffs[here, here]
        beta_ref[k] = coeffs[after, here]
    for i in range(0, LAT, 2):
        pair = jnp.concatenate([s_ref[i], s_ref[i + 1]], axis=1)
        new = jnp.dot(inverse, pair, precision=HIGH, preferred_element_type=jnp.float32)
        q_ref[pl.ds(i, ALL, stride=LAT), :] = new[:, :LON]
        q_ref[pl.ds(i + 1, ALL, stride=LAT), :] = new[:, LON:]


def body(start_block, sea_mask, depth_levels):
    x = start_block.reshape(B * LAT, LON)
    edge = (RIM, B + 8, LON)
    side = (B + 8, LON)
    top, bottom = call(edge_rows, (edge, edge))(x, sea_mask, depth_levels)
    down = [(i, i + 1) for i in range(7)]
    up = [(i + 1, i) for i in range(7)]
    north = lax.ppermute(bottom, ROW, down)
    south = lax.ppermute(top, ROW, up)
    core, part_west, part_east = call(core_rows, ((LAT, B + 8, LON), side, side), flops=1 << 22, moved=1 << 20)(
        x, sea_mask, depth_levels
    )
    west, east = call(side_columns, (side, side))(north, south, part_west, part_east)
    from_east = lax.ppermute(west, COL, [((i + 1) % 32, i) for i in range(32)])
    from_west = lax.ppermute(east, COL, [(i, (i + 1) % 32) for i in range(32)])
    wide = (ROWS, B, WIDE)
    thin = (ROWS, 8, WIDE)
    s, gram = call(
        krylov,
        ((LAT, ALL, LON), (ALL, ALL)),
        [pltpu.VMEM(wide, jnp.float32)] * 3 + [pltpu.VMEM(thin, jnp.float32)] * 3,
    )(core, north, south, from_west, from_east)
    pair = lax.all_gather(gram, "core")
    copies = call(spread, ((16, ALL, ALL),))(pair)[0]
    parts = lax.all_to_all(copies, ("x", "y"), 0, 0)
    copies = call(spread, ((8, ALL, ALL),))(parts)[0]
    parts = lax.all_to_all(copies, "z", 0, 0)
    q, alphas, betas = call(basis, ((ALL * LAT, LON), (ITERS, B, B), (ITERS, B, B)))(parts, s)
    return q.reshape(ALL, LAT, LON), alphas, betas


def solution(mesh):
    torus = Mesh(mesh.devices.reshape(4, 2, 8, 4), ("x", "core", "z", "y"))
    in_specs = (P(None, ROW, COL), P(ROW, COL), P(ROW, COL))
    out_specs = (P(None, ROW, COL), P(), P())
    return jax.shard_map(body, mesh=torus, in_specs=in_specs, out_specs=out_specs, check_vma=False)
```

```python
import jax
import jax.numpy as jnp
from jax import lax
from jax.experimental import pallas as pl
from jax.experimental.pallas import tpu as pltpu
from jax.sharding import Mesh, PartitionSpec as P

ITERS = 3
LEVELS = 50.0
KAPPA = 1.5
SHIFT = 3.0
CELLS = 1048576.0

B = 32
LAT = 32
LON = 128
RIM = 3
ROWS = LAT + 2 * RIM
WIDE = 2 * LON
ALL = (ITERS + 1) * B
HIGH = lax.Precision.HIGHEST
ROW, COL = ("x", "core"), ("z", "y")
NT = (((1,), (1,)), ((), ()))
PARAMS = pltpu.CompilerParams(vmem_limit_bytes=48 * 1024 * 1024)


def lanes_of(rows):
    return lax.broadcasted_iota(jnp.int32, (rows, LON), 1)


def call(kernel, outs, scratch=(), flops=0, moved=0, **specs):
    return pl.pallas_call(
        kernel,
        **specs,
        out_shape=tuple(jax.ShapeDtypeStruct(s, jnp.float32) for s in outs),
        scratch_shapes=list(scratch),
        compiler_params=PARAMS,
        cost_estimate=pl.CostEstimate(flops=flops, bytes_accessed=moved, transcendentals=0),
    )


def masked_row(lat, x_ref, mask_ref, depth_ref):
    mask = mask_ref[pl.ds(lat, 1), :].astype(jnp.float32)
    depth = mask * depth_ref[pl.ds(lat, 1), :].astype(jnp.float32) / LEVELS
    row = x_ref[pl.ds(lat, B, stride=LAT), :] * mask
    return jnp.concatenate([row, jnp.broadcast_to(depth, (8, LON))], axis=0)


def edge_rows(x_hbm, mask_hbm, depth_hbm, top_ref, bottom_ref, x_ref, mask_ref, depth_ref, sems):
    pairs = ((x_hbm, x_ref), (mask_hbm, mask_ref), (depth_hbm, depth_ref))
    copies = [pltpu.make_async_copy(source, target, sems.at[i]) for i, (source, target) in enumerate(pairs)]
    for copy in copies:
        copy.start()
    for copy in copies:
        copy.wait()
    for i in range(RIM):
        top_ref[i] = masked_row(i, x_ref, mask_ref, depth_ref)
        bottom_ref[i] = masked_row(LAT - RIM + i, x_ref, mask_ref, depth_ref)


def pack_sides(row, r, west, east):
    lane = lanes_of(B + 8)
    here = (lane >= RIM * r) & (lane < RIM * r + RIM)
    west = jnp.where(here, pltpu.roll(row, (RIM * r) % LON, 1), west)
    east = jnp.where(here, pltpu.roll(row, (RIM * r + RIM) % LON, 1), east)
    return west, east


def core_rows(x_ref, mask_ref, depth_ref, core_ref, west_ref, east_ref):
    west = east = jnp.zeros((B + 8, LON), jnp.float32)
    for i in range(LAT):
        row = masked_row(i, x_ref, mask_ref, depth_ref)
        core_ref[i] = row
        west, east = pack_sides(row, i + RIM, west, east)
    west_ref[...] = west
    east_ref[...] = east


def side_columns(north_ref, south_ref, part_west_ref, part_east_ref, west_ref, east_ref):
    west, east = part_west_ref[...], part_east_ref[...]
    for i in range(RIM):
        west, east = pack_sides(north_ref[i], i, west, east)
        west, east = pack_sides(south_ref[i], i + RIM + LAT, west, east)
    west_ref[...] = west
    east_ref[...] = east


def split(value):
    high = value.astype(jnp.bfloat16)
    rest = value - high.astype(jnp.float32)
    middle = rest.astype(jnp.bfloat16)
    low = (rest - middle.astype(jnp.float32)).astype(jnp.bfloat16)
    return high, middle, low


def four(field):
    return jnp.concatenate([field] * (B // 8), axis=0)


def krylov(core_ref, north_ref, south_ref, west_ref, east_ref, s_ref, gram_ref,
           x_ref, k1_ref, k2_ref, h_ref, down_ref, right_ref):
    lane = lanes_of(B + 8)
    from_west, from_east = west_ref[...], east_ref[...]
    for r in range(ROWS):
        if r < RIM:
            row = north_ref[r]
        elif r < RIM + LAT:
            row = core_ref[r - RIM]
        else:
            row = south_ref[r - RIM - LAT]
        beyond = jnp.where(lane < RIM, pltpu.roll(from_east, (-RIM * r) % LON, 1), 0.0)
        beyond = jnp.where(lane >= LON - RIM, pltpu.roll(from_west, (LON - RIM - RIM * r) % LON, 1), beyond)
        full = jnp.concatenate([row, beyond], axis=1)
        x_ref[r] = full[:B]
        h_ref[r] = full[B:]
    for r in range(ROWS):
        h = h_ref[r]
        if r + 1 < ROWS:
            down_ref[r] = KAPPA * jnp.minimum(h, h_ref[r + 1])
        right_ref[r] = KAPPA * jnp.minimum(h, pltpu.roll(h, WIDE - 1, 1))
    for i in range(LAT):
        s_ref[i, :B, :] = x_ref[i + RIM][:, :LON]
    levels = ((x_ref, k1_ref, 1.0), (k1_ref, k2_ref, 1.0 + SHIFT), (k2_ref, None, 1.0 + SHIFT))
    for step, (source, target, shift) in enumerate(levels):
        first, last = step + 1, ROWS - 2 - step
        flux = four(down_ref[first - 1]) * (source[first - 1] - source[first])
        for r in range(first, last + 1):
            v = source[r]
            centre = jnp.where(h_ref[r] > 0.0, 1.0 - shift, -shift)
            down = four(down_ref[r]) * (v - source[r + 1])
            right = four(right_ref[r]) * (v - pltpu.roll(v, WIDE - 1, 1))
            new = four(centre) * v + ((down - flux) + (right - pltpu.roll(right, 1, 1)))
            flux = down
            if target is not None:
                target[r] = new
            if RIM <= r < RIM + LAT:
                s_ref[r - RIM, (step + 1) * B:(step + 2) * B, :] = new[:, :LON]
    outer = lambda left, right: lax.dot_general(left, right, NT, preferred_element_type=jnp.float32)
    large = small = jnp.zeros((ALL, 2 * ALL), jnp.float32)
    for i in range(0, LAT, 2):
        high, middle, low = split(jnp.concatenate([s_ref[i], s_ref[i + 1]], axis=1))
        large += outer(high, jnp.concatenate([high, middle], axis=0))
        small += jnp.concatenate([outer(high, low), outer(middle, middle)], axis=1)
    half = large[:, ALL:] + small[:, :ALL]
    gram = large[:, :ALL] + small[:, ALL:] + half + half.T
    row = lax.broadcasted_iota(jnp.int32, (B, LON), 0)
    lane = lax.broadcasted_iota(jnp.int32, (B, LON), 1)
    packed = diagonal = jnp.zeros((B, LON), jnp.float32)
    for k in range(ITERS + 1):
        own = gram[k * B:(k + 1) * B]
        after = pltpu.roll(own, LON - B, 1)
        here = (lane >= k * B) & (lane < (k + 1) * B)
        packed = jnp.where(here, jnp.where(lane - k * B >= row, own, after), packed)
        diagonal = jnp.where(here & (lane - k * B == row), after, diagonal)
    gram_ref[:B] = packed
    gram_ref[B:] = (diagonal[:8] + diagonal[8:16]) + (diagonal[16:24] + diagonal[24:])


def spread(parts_ref, out_ref):
    total = parts_ref[0]
    for i in range(1, parts_ref.shape[0]):
        total += parts_ref[i]
    for i in range(out_ref.shape[0]):
        out_ref[i] = total


def unpack(total):
    row = lax.broadcasted_iota(jnp.int32, (B, LON), 0)
    lane = lax.broadcasted_iota(jnp.int32, (B, LON), 1)
    block, place = lane // B, lane % B
    turned = jnp.concatenate([total[:B], jnp.zeros((LON - B, LON), jnp.float32)], axis=0).T
    mirror = jnp.zeros((B, LON), jnp.float32)
    for k in range(ITERS + 1):
        part = turned[k * B:(k + 1) * B]
        mirror = jnp.where(block == k, pltpu.roll(part, k * B, 1) if k else part, mirror)
    even = jnp.where(place >= row, total[:B], mirror)
    odd = jnp.where(place < row, total[:B], mirror)
    odd = jnp.where(place == row, jnp.sum(total[B:], axis=0, keepdims=True), odd)
    move = lambda field, k: pltpu.roll(field, (k * B) % LON, 1)
    even1, even2, odd1, odd2, odd3 = move(even, 1), move(even, -1), move(odd, 1), move(odd, 2), move(odd, 3)
    pick = lambda a, b, c, d: jnp.where(block == 0, a, jnp.where(block == 1, b, jnp.where(block == 2, c, d)))
    corner = move(odd, -1)
    return jnp.concatenate(
        [
            pick(even, odd1, even1 - SHIFT * odd2, odd2 - SHIFT * (move(even, 2) - SHIFT * odd3)),
            pick(odd, even, odd1, even1),
            pick(even2 - SHIFT * odd, odd, even, odd1),
            pick(corner - SHIFT * (even2 - SHIFT * odd), even2, odd, even),
        ],
        axis=0,
    )


def factor(gram):
    groups = ALL // 8
    lane = lax.broadcasted_iota(jnp.int32, (8, ALL), 1)
    sub = lax.broadcasted_iota(jnp.int32, (8, ALL), 0)
    full = lambda value: jnp.broadcast_to(value, (8, ALL))
    tree = lambda p: ((p[0] + p[1]) + (p[2] + p[3])) + ((p[4] + p[5]) + (p[6] + p[7]))
    left = [gram[8 * g:8 * g + 8] for g in range(groups)]
    right = [jnp.where(lane == sub + 8 * g, 1.0, 0.0) for g in range(groups)]
    uppers, inverses = [], []
    for g in range(groups):
        columns = [full(left[g][:, 8 * g + t:8 * g + t + 1]) for t in range(8)]
        d = {(s, t): full(columns[t][s:s + 1]) for t in range(8) for s in range(t, 8)}
        a = [full(left[g][t:t + 1]) for t in range(8)]
        b = [full(right[g][t:t + 1]) for t in range(8)]
        ratio, recip = {}, []
        for t in range(8):
            recip.append(1.0 / d[t, t])
            for s in range(t + 1, 8):
                ratio[s, t] = d[s, t] * recip[t]
            for s in range(t + 1, 8):
                for u in range(t + 1, s + 1):
                    d[s, u] = d[s, u] - ratio[s, t] * d[u, t]
                a[s] = a[s] - ratio[s, t] * a[t]
                b[s] = b[s] - ratio[s, t] * b[t]
        upper = inverse = jnp.zeros((8, ALL), jnp.float32)
        for t in range(8):
            scale = lax.rsqrt(d[t, t])
            upper = jnp.where(sub == t, a[t] * scale, upper)
            inverse = jnp.where(sub == t, b[t] * scale, inverse)
        uppers.append(jnp.where(lane >= sub + 8 * g, upper, 0.0))
        inverses.append(inverse)
        a = [a[t] * recip[t] for t in range(8)]
        b = [b[t] * recip[t] for t in range(8)]
        for t in range(7, 0, -1):
            for s in range(t):
                a[s] = a[s] - ratio[t, s] * a[t]
                b[s] = b[s] - ratio[t, s] * b[t]
        for k in range(g + 1, groups):
            below = [full(left[k][:, 8 * g + t:8 * g + t + 1]) for t in range(8)]
            left[k] = left[k] - tree([below[t] * a[t] for t in range(8)])
            right[k] = right[k] - tree([below[t] * b[t] for t in range(8)])
    return jnp.concatenate(inverses, axis=0), jnp.concatenate(uppers, axis=0)


def swap(rows, sub):
    for k in (4, 2, 1):
        low, new = (sub & k) == 0, list(rows)
        for i in range(8):
            if not i & k:
                new[i] = jnp.where(low, rows[i], pltpu.roll(rows[i | k], k, 0))
                new[i | k] = jnp.where(low, pltpu.roll(rows[i], 8 - k, 0), rows[i | k])
        rows = new
    return rows


def basis(parts_ref, s_ref, q_hbm, alpha_ref, beta_ref, q_ref, sems):
    total = parts_ref[0]
    for i in range(1, parts_ref.shape[0]):
        total += parts_ref[i]
    inverse, upper = factor(unpack(total * (1.0 / CELLS)))
    lane = lax.broadcasted_iota(jnp.int32, (ALL, ALL), 1)
    own = jnp.where(lane < B, 1.0, jnp.where(lane < ITERS * B, 1.0 + SHIFT, 0.0))
    image = inverse * own + jnp.where(lane >= B, pltpu.roll(inverse, B, 1), 0.0)
    coeffs = lax.dot_general(upper, image, NT, precision=HIGH, preferred_element_type=jnp.float32)
    for k in range(ITERS):
        here, after = slice(k * B, (k + 1) * B), slice((k + 1) * B, (k + 2) * B)
        alpha_ref[k] = coeffs[here, here]
        beta_ref[k] = coeffs[after, here]
    high, middle, low = split(inverse)
    two = jnp.concatenate([high, middle], axis=1)
    three = jnp.concatenate([high, middle, low], axis=1)
    dot = lambda a, b: jnp.dot(a, b, preferred_element_type=jnp.float32)
    sub = lax.broadcasted_iota(jnp.int32, (8, LON), 0)
    copies = []
    for g in range(LAT // 8):
        rows = []
        for i in range(8 * g, 8 * g + 8, 2):
            a, b, c = split(jnp.concatenate([s_ref[i], s_ref[i + 1]], axis=1))
            new = dot(three, jnp.concatenate([a, a, a], axis=0)) + dot(two, jnp.concatenate([b, b], axis=0)) + dot(high, c)
            rows += [new[:, :LON], new[:, LON:]]
        for v in range(0, ALL, 8):
            for t, tile in enumerate(swap([row[v:v + 8] for row in rows], sub)):
                q_ref[v + t, 8 * g:8 * g + 8, :] = tile
        chunk = pl.ds(8 * g, 8)
        copies.append(pltpu.make_async_copy(q_ref.at[:, chunk, :], q_hbm.at[:, chunk, :], sems.at[g]))
        copies[-1].start()
    for copy in copies:
        copy.wait()


def body(start_block, sea_mask, depth_levels):
    x = start_block.reshape(B * LAT, LON)
    edge = (RIM, B + 8, LON)
    side = (B + 8, LON)
    anywhere = pl.BlockSpec(memory_space=pl.ANY)
    small = pltpu.VMEM((LAT, LON), jnp.int32)
    top, bottom = call(
        edge_rows,
        (edge, edge),
        [pltpu.VMEM((B * LAT, LON), jnp.float32), small, small, pltpu.SemaphoreType.DMA((3,))],
        in_specs=[anywhere] * 3,
    )(x, sea_mask, depth_levels)
    down = [(i, i + 1) for i in range(7)]
    up = [(i + 1, i) for i in range(7)]
    north = lax.ppermute(bottom, ROW, down)
    south = lax.ppermute(top, ROW, up)
    core, part_west, part_east = call(core_rows, ((LAT, B + 8, LON), side, side), flops=1 << 22, moved=1 << 20)(
        x, sea_mask, depth_levels
    )
    west, east = call(side_columns, (side, side))(north, south, part_west, part_east)
    from_east = lax.ppermute(west, COL, [((i + 1) % 32, i) for i in range(32)])
    from_west = lax.ppermute(east, COL, [(i, (i + 1) % 32) for i in range(32)])
    wide = (ROWS, B, WIDE)
    thin = (ROWS, 8, WIDE)
    s, gram = call(
        krylov,
        ((LAT, ALL, LON), (B + 8, LON)),
        [pltpu.VMEM(wide, jnp.float32)] * 3 + [pltpu.VMEM(thin, jnp.float32)] * 3,
    )(core, north, south, from_west, from_east)
    pair = lax.all_gather(gram, "core")
    copies = call(spread, ((16, B + 8, LON),))(pair)[0]
    parts = lax.all_to_all(copies, ("x", "y"), 0, 0)
    copies = call(spread, ((8, B + 8, LON),))(parts)[0]
    parts = lax.all_to_all(copies, "z", 0, 0)
    vmem = pl.BlockSpec(memory_space=pltpu.VMEM)
    return call(
        basis,
        ((ALL, LAT, LON), (ITERS, B, B), (ITERS, B, B)),
        [pltpu.VMEM((ALL, LAT, LON), jnp.float32), pltpu.SemaphoreType.DMA((LAT // 8,))],
        out_specs=(anywhere, vmem, vmem),
    )(parts, s)


def solution(mesh):
    torus = Mesh(mesh.devices.reshape(4, 2, 8, 4), ("x", "core", "z", "y"))
    in_specs = (P(None, ROW, COL), P(ROW, COL), P(ROW, COL))
    out_specs = (P(None, ROW, COL), P(), P())
    return jax.shard_map(body, mesh=torus, in_specs=in_specs, out_specs=out_specs, check_vma=False)
```

```python
import jax
import jax.numpy as jnp
from jax import lax
from jax.experimental import pallas as pl
from jax.experimental.pallas import tpu as pltpu
from jax.sharding import Mesh, PartitionSpec as P

ITERS = 3
LEVELS = 50.0
KAPPA = 1.5
SHIFT = 3.0
CELLS = 1048576.0

B = 32
LAT = 32
LON = 128
RIM = 3
ROWS = LAT + 2 * RIM
WIDE = 2 * LON
ALL = (ITERS + 1) * B
HIGH = lax.Precision.HIGHEST
ROW, COL = ("x", "core"), ("z", "y")
NT = (((1,), (1,)), ((), ()))
PARAMS = pltpu.CompilerParams(vmem_limit_bytes=48 * 1024 * 1024)


def lanes_of(rows):
    return lax.broadcasted_iota(jnp.int32, (rows, LON), 1)


def call(kernel, outs, scratch=(), flops=0, moved=0, **specs):
    return pl.pallas_call(
        kernel,
        **specs,
        out_shape=tuple(jax.ShapeDtypeStruct(s, jnp.float32) for s in outs),
        scratch_shapes=list(scratch),
        compiler_params=PARAMS,
        cost_estimate=pl.CostEstimate(flops=flops, bytes_accessed=moved, transcendentals=0),
    )


def masked_row(lat, x_ref, mask_ref, depth_ref):
    mask = mask_ref[pl.ds(lat, 1), :].astype(jnp.float32)
    depth = mask * depth_ref[pl.ds(lat, 1), :].astype(jnp.float32) / LEVELS
    row = x_ref[pl.ds(lat, B, stride=LAT), :] * mask
    return jnp.concatenate([row, jnp.broadcast_to(depth, (8, LON))], axis=0)


def load(sources, targets, sems):
    copies = [pltpu.make_async_copy(a, b, sems.at[i]) for i, (a, b) in enumerate(zip(sources, targets))]
    for copy in copies:
        copy.start()
    for copy in copies:
        copy.wait()


def edge_rows(x_hbm, mask_hbm, depth_hbm, near_ref, far_ref, x_ref, mask_ref, depth_ref, sems):
    load((x_hbm, mask_hbm, depth_hbm), (x_ref, mask_ref, depth_ref), sems)
    odd = lax.axis_index("core") == 1
    for i in range(RIM):
        top = masked_row(i, x_ref, mask_ref, depth_ref)
        bottom = masked_row(LAT - RIM + i, x_ref, mask_ref, depth_ref)
        near_ref[i] = jnp.where(odd, top, bottom)
        far_ref[i] = jnp.where(odd, bottom, top)


def pack_sides(row, r, west, east):
    lane = lanes_of(B + 8)
    here = (lane >= RIM * r) & (lane < RIM * r + RIM)
    west = jnp.where(here, pltpu.roll(row, (RIM * r) % LON, 1), west)
    east = jnp.where(here, pltpu.roll(row, (RIM * r + RIM) % LON, 1), east)
    return west, east


def core_rows(x_hbm, mask_hbm, depth_hbm, core_ref, west_ref, east_ref, x_ref, mask_ref, depth_ref, sems):
    load((x_hbm, mask_hbm, depth_hbm), (x_ref, mask_ref, depth_ref), sems)
    west = east = jnp.zeros((B + 8, LON), jnp.float32)
    for i in range(LAT):
        row = masked_row(i, x_ref, mask_ref, depth_ref)
        core_ref[i] = row
        west, east = pack_sides(row, i + RIM, west, east)
    west_ref[...] = west
    east_ref[...] = east


def side_columns(near_ref, far_ref, part_west_ref, part_east_ref, near_out, far_out, north_ref, south_ref):
    odd = lax.axis_index("core") == 1
    west, east = part_west_ref[...], part_east_ref[...]
    for i in range(RIM):
        north = jnp.where(odd, near_ref[i], far_ref[i])
        south = jnp.where(odd, far_ref[i], near_ref[i])
        north_ref[i] = north
        south_ref[i] = south
        west, east = pack_sides(north, i, west, east)
        west, east = pack_sides(south, i + RIM + LAT, west, east)
    odd = lax.axis_index("y") % 2 == 1
    near_out[...] = jnp.where(odd, west, east)
    far_out[...] = jnp.where(odd, east, west)


def split(value):
    high = value.astype(jnp.bfloat16)
    rest = value - high.astype(jnp.float32)
    middle = rest.astype(jnp.bfloat16)
    low = (rest - middle.astype(jnp.float32)).astype(jnp.bfloat16)
    return high, middle, low


def four(field):
    return jnp.concatenate([field] * (B // 8), axis=0)


def krylov(core_ref, north_ref, south_ref, near_ref, far_ref, s_ref, gram_ref,
           x_ref, k1_ref, k2_ref, h_ref, down_ref, right_ref):
    lane = lanes_of(B + 8)
    odd = lax.axis_index("y") % 2 == 1
    near, far = near_ref[...], far_ref[...]
    from_west, from_east = jnp.where(odd, near, far), jnp.where(odd, far, near)
    for r in range(ROWS):
        if r < RIM:
            row = north_ref[r]
        elif r < RIM + LAT:
            row = core_ref[r - RIM]
        else:
            row = south_ref[r - RIM - LAT]
        beyond = jnp.where(lane < RIM, pltpu.roll(from_east, (-RIM * r) % LON, 1), 0.0)
        beyond = jnp.where(lane >= LON - RIM, pltpu.roll(from_west, (LON - RIM - RIM * r) % LON, 1), beyond)
        full = jnp.concatenate([row, beyond], axis=1)
        x_ref[r] = full[:B]
        h_ref[r] = full[B:]
        if RIM <= r < RIM + LAT:
            s_ref[r - RIM, :B, :] = row[:B]

    for r in range(ROWS - 1):
        h = h_ref[r]
        down_ref[r] = KAPPA * jnp.minimum(h, h_ref[r + 1])
        right_ref[r] = KAPPA * jnp.minimum(h, pltpu.roll(h, WIDE - 1, 1))
    levels = ((x_ref, k1_ref, 1.0), (k1_ref, k2_ref, 1.0 + SHIFT), (k2_ref, None, 1.0 + SHIFT))
    for step, (source, target, shift) in enumerate(levels):
        first, last = step + 1, ROWS - 2 - step
        flux = four(down_ref[first - 1]) * (source[first - 1] - source[first])
        for r in range(first, last + 1):
            v = source[r]
            centre = jnp.where(h_ref[r] > 0.0, 1.0 - shift, -shift)
            down = four(down_ref[r]) * (v - source[r + 1])
            right = four(right_ref[r]) * (v - pltpu.roll(v, WIDE - 1, 1))
            new = four(centre) * v + ((down - flux) + (right - pltpu.roll(right, 1, 1)))
            flux = down
            if target is not None:
                target[r] = new
            if RIM <= r < RIM + LAT:
                s_ref[r - RIM, (step + 1) * B:(step + 2) * B, :] = new[:, :LON]
    outer = lambda left, right: lax.dot_general(left, right, NT, preferred_element_type=jnp.float32)
    large = small = jnp.zeros((ALL, 2 * ALL), jnp.float32)
    for i in range(0, LAT, 2):
        high, middle, low = split(jnp.concatenate([s_ref[i], s_ref[i + 1]], axis=1))
        large += outer(high, jnp.concatenate([high, middle], axis=0))
        small += jnp.concatenate([outer(high, low), outer(middle, middle)], axis=1)
    half = large[:, ALL:] + small[:, :ALL]
    gram = large[:, :ALL] + small[:, ALL:] + half + half.T
    row = lax.broadcasted_iota(jnp.int32, (B, LON), 0)
    lane = lax.broadcasted_iota(jnp.int32, (B, LON), 1)
    packed = diagonal = jnp.zeros((B, LON), jnp.float32)
    for k in range(ITERS + 1):
        own = gram[k * B:(k + 1) * B]
        after = pltpu.roll(own, LON - B, 1)
        here = (lane >= k * B) & (lane < (k + 1) * B)
        packed = jnp.where(here, jnp.where(lane - k * B >= row, own, after), packed)
        diagonal = jnp.where(here & (lane - k * B == row), after, diagonal)
    gram_ref[:B] = packed
    gram_ref[B:] = (diagonal[:8] + diagonal[8:16]) + (diagonal[16:24] + diagonal[24:])


def spread(parts_ref, out_ref):
    total = parts_ref[0]
    for i in range(1, parts_ref.shape[0]):
        total += parts_ref[i]
    for i in range(out_ref.shape[0]):
        out_ref[i] = total


def unpack(total):
    row = lax.broadcasted_iota(jnp.int32, (B, LON), 0)
    lane = lax.broadcasted_iota(jnp.int32, (B, LON), 1)
    block, place = lane // B, lane % B
    turned = jnp.concatenate([total[:B], jnp.zeros((LON - B, LON), jnp.float32)], axis=0).T
    mirror = jnp.zeros((B, LON), jnp.float32)
    for k in range(ITERS + 1):
        part = turned[k * B:(k + 1) * B]
        mirror = jnp.where(block == k, pltpu.roll(part, k * B, 1) if k else part, mirror)
    even = jnp.where(place >= row, total[:B], mirror)
    odd = jnp.where(place < row, total[:B], mirror)
    odd = jnp.where(place == row, jnp.sum(total[B:], axis=0, keepdims=True), odd)
    move = lambda field, k: pltpu.roll(field, (k * B) % LON, 1)
    even1, even2, odd1, odd2, odd3 = move(even, 1), move(even, -1), move(odd, 1), move(odd, 2), move(odd, 3)
    pick = lambda a, b, c, d: jnp.where(block == 0, a, jnp.where(block == 1, b, jnp.where(block == 2, c, d)))
    corner = move(odd, -1)
    return jnp.concatenate(
        [
            pick(even, odd1, even1 - SHIFT * odd2, odd2 - SHIFT * (move(even, 2) - SHIFT * odd3)),
            pick(odd, even, odd1, even1),
            pick(even2 - SHIFT * odd, odd, even, odd1),
            pick(corner - SHIFT * (even2 - SHIFT * odd), even2, odd, even),
        ],
        axis=0,
    )


def factor(gram):
    groups = ALL // 8
    lane = lax.broadcasted_iota(jnp.int32, (8, ALL), 1)
    sub = lax.broadcasted_iota(jnp.int32, (8, ALL), 0)
    full = lambda value: jnp.broadcast_to(value, (8, ALL))
    tree = lambda p: ((p[0] + p[1]) + (p[2] + p[3])) + ((p[4] + p[5]) + (p[6] + p[7]))
    left = [gram[8 * g:8 * g + 8] for g in range(groups)]
    right = [jnp.where(lane == sub + 8 * g, 1.0, 0.0) for g in range(groups)]
    uppers, inverses = [], []
    for g in range(groups):
        columns = [full(left[g][:, 8 * g + t:8 * g + t + 1]) for t in range(8)]
        d = {(s, t): full(columns[t][s:s + 1]) for t in range(8) for s in range(t, 8)}
        a = [full(left[g][t:t + 1]) for t in range(8)]
        b = [full(right[g][t:t + 1]) for t in range(8)]
        ratio, recip = {}, []
        for t in range(8):
            recip.append(1.0 / d[t, t])
            for s in range(t + 1, 8):
                ratio[s, t] = d[s, t] * recip[t]
            for s in range(t + 1, 8):
                for u in range(t + 1, s + 1):
                    d[s, u] = d[s, u] - ratio[s, t] * d[u, t]
                a[s] = a[s] - ratio[s, t] * a[t]
                b[s] = b[s] - ratio[s, t] * b[t]
        upper = inverse = jnp.zeros((8, ALL), jnp.float32)
        for t in range(8):
            scale = lax.rsqrt(d[t, t])
            upper = jnp.where(sub == t, a[t] * scale, upper)
            inverse = jnp.where(sub == t, b[t] * scale, inverse)
        uppers.append(jnp.where(lane >= sub + 8 * g, upper, 0.0))
        inverses.append(inverse)
        a = [a[t] * recip[t] for t in range(8)]
        b = [b[t] * recip[t] for t in range(8)]
        for t in range(7, 0, -1):
            for s in range(t):
                a[s] = a[s] - ratio[t, s] * a[t]
                b[s] = b[s] - ratio[t, s] * b[t]
        for k in range(g + 1, groups):
            below = [full(left[k][:, 8 * g + t:8 * g + t + 1]) for t in range(8)]
            left[k] = left[k] - tree([below[t] * a[t] for t in range(8)])
            right[k] = right[k] - tree([below[t] * b[t] for t in range(8)])
    return jnp.concatenate(inverses, axis=0), jnp.concatenate(uppers, axis=0)


def swap(rows, sub):
    for k in (4, 2, 1):
        low, new = (sub & k) == 0, list(rows)
        for i in range(8):
            if not i & k:
                new[i] = jnp.where(low, rows[i], pltpu.roll(rows[i | k], k, 0))
                new[i | k] = jnp.where(low, pltpu.roll(rows[i], 8 - k, 0), rows[i | k])
        rows = new
    return rows


def basis(parts_ref, s_ref, q_hbm, alpha_ref, beta_ref, q_ref, sems):
    total = parts_ref[0]
    for i in range(1, parts_ref.shape[0]):
        total += parts_ref[i]
    inverse, upper = factor(unpack(total * (1.0 / CELLS)))
    lane = lax.broadcasted_iota(jnp.int32, (ALL, ALL), 1)
    own = jnp.where(lane < B, 1.0, jnp.where(lane < ITERS * B, 1.0 + SHIFT, 0.0))
    image = inverse * own + jnp.where(lane >= B, pltpu.roll(inverse, B, 1), 0.0)
    coeffs = lax.dot_general(upper, image, NT, precision=HIGH, preferred_element_type=jnp.float32)
    for k in range(ITERS):
        here, after = slice(k * B, (k + 1) * B), slice((k + 1) * B, (k + 2) * B)
        alpha_ref[k] = coeffs[here, here]
        beta_ref[k] = coeffs[after, here]
    high, middle, low = split(inverse)
    two = jnp.concatenate([high, middle], axis=1)
    three = jnp.concatenate([high, middle, low], axis=1)
    dot = lambda a, b: jnp.dot(a, b, preferred_element_type=jnp.float32)
    sub = lax.broadcasted_iota(jnp.int32, (8, LON), 0)
    copies = []
    for g in range(LAT // 8):
        rows = []
        for i in range(8 * g, 8 * g + 8, 2):
            a, b, c = split(jnp.concatenate([s_ref[i], s_ref[i + 1]], axis=1))
            new = dot(three, jnp.concatenate([a, a, a], axis=0)) + dot(two, jnp.concatenate([b, b], axis=0)) + dot(high, c)
            rows += [new[:, :LON], new[:, LON:]]
        for v in range(0, ALL, 8):
            for t, tile in enumerate(swap([row[v:v + 8] for row in rows], sub)):
                q_ref[v + t, 8 * g:8 * g + 8, :] = tile
        chunk = pl.ds(8 * g, 8)
        copies.append(pltpu.make_async_copy(q_ref.at[:, chunk, :], q_hbm.at[:, chunk, :], sems.at[g]))
        copies[-1].start()
    for copy in copies:
        copy.wait()


def body(start_block, sea_mask, depth_levels):
    x = start_block.reshape(B * LAT, LON)
    edge = (RIM, B + 8, LON)
    side = (B + 8, LON)
    anywhere = pl.BlockSpec(memory_space=pl.ANY)
    small = pltpu.VMEM((LAT, LON), jnp.int32)
    inputs = dict(in_specs=[pl.BlockSpec(memory_space=pltpu.HBM)] * 3)
    room = [pltpu.VMEM((B * LAT, LON), jnp.float32), small, small, pltpu.SemaphoreType.DMA((3,))]
    near, far = call(edge_rows, (edge, edge), room, **inputs)(x, sea_mask, depth_levels)
    near = lax.ppermute(near, ROW, [(i, i ^ 1) for i in range(8)])
    far = lax.ppermute(far, ROW, [(i, ((i + 1) ^ 1) - 1) for i in range(1, 7)])
    core, part_west, part_east = call(
        core_rows, ((LAT, B + 8, LON), side, side), room, flops=1 << 22, moved=1 << 20, **inputs
    )(x, sea_mask, depth_levels)
    near, far, north, south = call(side_columns, (side, side, edge, edge))(near, far, part_west, part_east)
    near = lax.ppermute(near, COL, [(i, i ^ 1) for i in range(32)])
    far = lax.ppermute(far, COL, [(i, (((i + 1) ^ 1) - 1) % 32) for i in range(32)])
    wide = (ROWS, B, WIDE)
    thin = (ROWS, 8, WIDE)
    s, gram = call(
        krylov,
        ((LAT, ALL, LON), (B + 8, LON)),
        [pltpu.VMEM(wide, jnp.float32)] * 3 + [pltpu.VMEM(thin, jnp.float32)] * 3,
    )(core, north, south, near, far)
    pair = lax.all_gather(gram, "core")
    copies = call(spread, ((16, B + 8, LON),))(pair)[0]
    parts = lax.all_to_all(copies, ("x", "y"), 0, 0)
    copies = call(spread, ((8, B + 8, LON),))(parts)[0]
    parts = lax.all_to_all(copies, "z", 0, 0)
    vmem = pl.BlockSpec(memory_space=pltpu.VMEM)
    return call(
        basis,
        ((ALL, LAT, LON), (ITERS, B, B), (ITERS, B, B)),
        [pltpu.VMEM((ALL, LAT, LON), jnp.float32), pltpu.SemaphoreType.DMA((LAT // 8,))],
        out_specs=(anywhere, vmem, vmem),
    )(parts, s)


def solution(mesh):
    torus = Mesh(mesh.devices.reshape(4, 2, 8, 4), ("x", "core", "z", "y"))
    in_specs = (P(None, ROW, COL), P(ROW, COL), P(ROW, COL))
    out_specs = (P(None, ROW, COL), P(), P())
    return jax.shard_map(body, mesh=torus, in_specs=in_specs, out_specs=out_specs, check_vma=False)
```

```python
import jax
import jax.numpy as jnp
from jax import lax
from jax.experimental import pallas as pl
from jax.experimental.pallas import tpu as pltpu
from jax.sharding import Mesh, PartitionSpec as P

ITERS = 3
LEVELS = 50.0
KAPPA = 1.5
SHIFT = 3.0
CELLS = 1048576.0

B = 32
LAT = 32
LON = 128
RIM = 3
ROWS = LAT + 2 * RIM
SPAN = 3 * RIM
FLAT = 3 * LON
ALL = (ITERS + 1) * B
HIGH = lax.Precision.HIGHEST
ROW, COL = ("x", "core"), ("z", "y")
NT = (((1,), (1,)), ((), ()))
PARAMS = pltpu.CompilerParams(vmem_limit_bytes=48 * 1024 * 1024)


def lanes_of(rows):
    return lax.broadcasted_iota(jnp.int32, (rows, LON), 1)


def call(kernel, outs, scratch=(), flops=0, moved=0, **specs):
    return pl.pallas_call(
        kernel,
        **specs,
        out_shape=tuple(jax.ShapeDtypeStruct(s, jnp.float32) for s in outs),
        scratch_shapes=list(scratch),
        compiler_params=PARAMS,
        cost_estimate=pl.CostEstimate(flops=flops, bytes_accessed=moved, transcendentals=0),
    )


def masked_row(lat, x_ref, mask_ref, depth_ref):
    mask = mask_ref[pl.ds(lat, 1), :].astype(jnp.float32)
    depth = mask * depth_ref[pl.ds(lat, 1), :].astype(jnp.float32) / LEVELS
    row = x_ref[pl.ds(lat, B, stride=LAT), :] * mask
    return jnp.concatenate([row, jnp.broadcast_to(depth, (8, LON))], axis=0)


def load(sources, targets, sems):
    copies = [pltpu.make_async_copy(a, b, sems.at[i]) for i, (a, b) in enumerate(zip(sources, targets))]
    for copy in copies:
        copy.start()
    for copy in copies:
        copy.wait()


def edge_rows(x_hbm, mask_hbm, depth_hbm, near_ref, far_ref, x_ref, mask_ref, depth_ref, sems):
    load((x_hbm, mask_hbm, depth_hbm), (x_ref, mask_ref, depth_ref), sems)
    odd = lax.axis_index("core") == 1
    for i in range(RIM):
        top = masked_row(i, x_ref, mask_ref, depth_ref)
        bottom = masked_row(LAT - RIM + i, x_ref, mask_ref, depth_ref)
        near_ref[i] = jnp.where(odd, top, bottom)
        far_ref[i] = jnp.where(odd, bottom, top)


def pack_sides(row, r, west, east):
    lane = lanes_of(B + 8)
    for sides, source, target in ((west, 0, SPAN * r + RIM), (east, LON - 2 * RIM, SPAN * r)):
        moved = pltpu.roll(row, (target - source) % LON, 1)
        for k in range(target // LON, (target + 2 * RIM - 1) // LON + 1):
            place = lane + k * LON
            sides[k] = jnp.where((place >= target) & (place < target + 2 * RIM), moved, sides[k])


def chunks(flat):
    return [flat[:, k * LON:(k + 1) * LON] for k in range(FLAT // LON)]


def core_rows(x_hbm, mask_hbm, depth_hbm, core_ref, west_ref, east_ref, x_ref, mask_ref, depth_ref, sems):
    load((x_hbm, mask_hbm, depth_hbm), (x_ref, mask_ref, depth_ref), sems)
    west, east = chunks(jnp.zeros((B + 8, FLAT), jnp.float32)), chunks(jnp.zeros((B + 8, FLAT), jnp.float32))
    for i in range(LAT):
        row = masked_row(i, x_ref, mask_ref, depth_ref)
        core_ref[i] = row
        pack_sides(row, i + RIM, west, east)
    west_ref[...] = jnp.concatenate(west, axis=1)
    east_ref[...] = jnp.concatenate(east, axis=1)


def side_columns(near_ref, far_ref, part_west_ref, part_east_ref,
                 near_out, far_out, north_ref, south_ref, west_ref, east_ref):
    odd = lax.axis_index("core") == 1
    west, east = chunks(part_west_ref[...]), chunks(part_east_ref[...])
    for i in range(RIM):
        north = jnp.where(odd, near_ref[i], far_ref[i])
        south = jnp.where(odd, far_ref[i], near_ref[i])
        north_ref[i] = north
        south_ref[i] = south
        pack_sides(north, i, west, east)
        pack_sides(south, i + RIM + LAT, west, east)
    west, east = jnp.concatenate(west, axis=1), jnp.concatenate(east, axis=1)
    west_ref[...] = west
    east_ref[...] = east
    to_west, to_east = pltpu.roll(west, RIM, 1), pltpu.roll(east, FLAT - RIM, 1)
    odd = lax.axis_index("y") % 2 == 1
    near_out[...] = jnp.where(odd, to_west, to_east)
    far_out[...] = jnp.where(odd, to_east, to_west)


def split(value):
    high = value.astype(jnp.bfloat16)
    rest = value - high.astype(jnp.float32)
    middle = rest.astype(jnp.bfloat16)
    low = (rest - middle.astype(jnp.float32)).astype(jnp.bfloat16)
    return high, middle, low


def four(field):
    return jnp.concatenate([field] * (B // 8), axis=0)


def outer(left, right):
    return lax.dot_general(left, right, NT, preferred_element_type=jnp.float32)


def products(value):
    high, middle, low = split(value)
    both = outer(high, jnp.concatenate([high, middle], axis=0))
    return both[:, :ALL] + outer(middle, middle), both[:, ALL:] + outer(high, low)


def inside(core_ref, north_ref, south_ref, s_ref, even_ref, half_ref, k1_ref, k2_ref, down_ref, right_ref, centre_ref):
    def base(r):
        if r < RIM:
            return north_ref[r]
        return core_ref[r - RIM] if r < RIM + LAT else south_ref[r - RIM - LAT]

    for r in range(ROWS - 1):
        h = base(r)[B:]
        down_ref[r] = KAPPA * jnp.minimum(h, base(r + 1)[B:])
        right_ref[r] = KAPPA * jnp.minimum(h, pltpu.roll(h, LON - 1, 1))
        centre_ref[r] = jnp.where(h > 0.0, 0.0, -1.0)
    levels = (
        (lambda r: base(r)[:B], k1_ref, 0.0),
        (lambda r: k1_ref[r], k2_ref, SHIFT),
        (lambda r: k2_ref[r], None, SHIFT),
    )
    for step, (source, target, shift) in enumerate(levels):
        first, last = step + 1, ROWS - 2 - step
        v, after = source(first - 1), source(first)
        flux = four(down_ref[first - 1]) * (v - after)
        for r in range(first, last + 1):
            v, after = after, source(r + 1)
            down = four(down_ref[r]) * (v - after)
            right = four(right_ref[r]) * (v - pltpu.roll(v, LON - 1, 1))
            new = four(centre_ref[r] - shift) * v + ((down - flux) + (right - pltpu.roll(right, 1, 1)))
            flux = down
            if target is not None:
                target[r] = new
            if RIM <= r < RIM + LAT:
                s_ref[r - RIM, (step + 1) * B:(step + 2) * B, :] = new
    lane = lanes_of(ALL)
    clean = (lane >= RIM) & (lane < LON - RIM)
    even = half = jnp.zeros((ALL, ALL), jnp.float32)
    for i in range(0, LAT, 2):
        rows = []
        for j in (i, i + 1):
            s_ref[j, :B, :] = core_ref[j, :B]
            rows.append(jnp.where(clean, s_ref[j], 0.0))
        one, two = products(jnp.concatenate(rows, axis=1))
        even += one
        half += two
    even_ref[...] = even
    half_ref[...] = half


def border(near_ref, far_ref, own_west_ref, own_east_ref, even_ref, half_ref, gram_ref, west_ref, east_ref):
    odd = lax.axis_index("y") % 2 == 1
    near, far = near_ref[...], far_ref[...]
    lane = lax.broadcasted_iota(jnp.int32, (B + 8, FLAT), 1)
    line = (lane * 7282) >> 16
    place = lane - line * SPAN
    west = jnp.where(place < RIM, jnp.where(odd, near, far), own_west_ref[...])
    east = jnp.where(place >= 2 * RIM, jnp.where(odd, far, near), own_east_ref[...])
    joint = place[:8] < SPAN - 1
    kept = (place[:1] >= RIM) & (place[:1] < 2 * RIM) & (line[:1] >= RIM) & (line[:1] < RIM + LAT)
    fields = []
    for start, out_ref in ((west, west_ref), (east, east_ref)):
        h = start[B:]
        down = four(KAPPA * jnp.minimum(h, pltpu.roll(h, FLAT - SPAN, 1)))
        right = four(jnp.where(joint, KAPPA * jnp.minimum(h, pltpu.roll(h, FLAT - 1, 1)), 0.0))
        centre = jnp.where(h > 0.0, 0.0, -1.0)
        v = start[:B]
        found = [v]
        for shift in (0.0, SHIFT, SHIFT):
            flow = down * (v - pltpu.roll(v, FLAT - SPAN, 1))
            side = right * (v - pltpu.roll(v, FLAT - 1, 1))
            v = four(centre - shift) * v + (
                (flow - pltpu.roll(flow, SPAN, 1)) + (side - pltpu.roll(side, 1, 1))
            )
            found.append(v)
        out_ref[...] = jnp.concatenate(found[1:], axis=0)
        fields.append(jnp.where(kept, jnp.concatenate(found, axis=0), 0.0))
    even, half = products(jnp.concatenate(fields, axis=1))
    even += even_ref[...]
    half += half_ref[...]
    gram = even + half + half.T
    row = lax.broadcasted_iota(jnp.int32, (B, LON), 0)
    lane = lax.broadcasted_iota(jnp.int32, (B, LON), 1)
    packed = diagonal = jnp.zeros((B, LON), jnp.float32)
    for k in range(ITERS + 1):
        own = gram[k * B:(k + 1) * B]
        after = pltpu.roll(own, LON - B, 1)
        here = (lane >= k * B) & (lane < (k + 1) * B)
        packed = jnp.where(here, jnp.where(lane - k * B >= row, own, after), packed)
        diagonal = jnp.where(here & (lane - k * B == row), after, diagonal)
    gram_ref[:B] = packed
    gram_ref[B:] = (diagonal[:8] + diagonal[8:16]) + (diagonal[16:24] + diagonal[24:])


def spread(parts_ref, out_ref):
    total = parts_ref[0]
    for i in range(1, parts_ref.shape[0]):
        total += parts_ref[i]
    for i in range(out_ref.shape[0]):
        out_ref[i] = total


def unpack(total):
    row = lax.broadcasted_iota(jnp.int32, (B, LON), 0)
    lane = lax.broadcasted_iota(jnp.int32, (B, LON), 1)
    block, place = lane // B, lane % B
    turned = jnp.concatenate([total[:B], jnp.zeros((LON - B, LON), jnp.float32)], axis=0).T
    mirror = jnp.zeros((B, LON), jnp.float32)
    for k in range(ITERS + 1):
        part = turned[k * B:(k + 1) * B]
        mirror = jnp.where(block == k, pltpu.roll(part, k * B, 1) if k else part, mirror)
    even = jnp.where(place >= row, total[:B], mirror)
    odd = jnp.where(place < row, total[:B], mirror)
    odd = jnp.where(place == row, jnp.sum(total[B:], axis=0, keepdims=True), odd)
    move = lambda field, k: pltpu.roll(field, (k * B) % LON, 1)
    even1, even2, odd1, odd2, odd3 = move(even, 1), move(even, -1), move(odd, 1), move(odd, 2), move(odd, 3)
    pick = lambda a, b, c, d: jnp.where(block == 0, a, jnp.where(block == 1, b, jnp.where(block == 2, c, d)))
    corner = move(odd, -1)
    return jnp.concatenate(
        [
            pick(even, odd1, even1 - SHIFT * odd2, odd2 - SHIFT * (move(even, 2) - SHIFT * odd3)),
            pick(odd, even, odd1, even1),
            pick(even2 - SHIFT * odd, odd, even, odd1),
            pick(corner - SHIFT * (even2 - SHIFT * odd), even2, odd, even),
        ],
        axis=0,
    )


def reciprocal(value):
    return 1.0 / value


def factor(gram):
    groups = ALL // 8
    lane = lax.broadcasted_iota(jnp.int32, (8, ALL), 1)
    sub = lax.broadcasted_iota(jnp.int32, (8, ALL), 0)
    full = lambda value: jnp.broadcast_to(value, (8, ALL))
    tree = lambda p: ((p[0] + p[1]) + (p[2] + p[3])) + ((p[4] + p[5]) + (p[6] + p[7]))
    left = [gram[8 * g:8 * g + 8] for g in range(groups)]
    right = [jnp.where(lane == sub + 8 * g, 1.0, 0.0) for g in range(groups)]
    diagonal = sum(jnp.where(lane == sub + 8 * g, left[g], 0.0) for g in range(groups))
    guess = full(reciprocal(jnp.sum(diagonal, axis=0, keepdims=True)))
    uppers, inverses = [], []
    for g in range(groups):
        columns = [full(left[g][:, 8 * g + t:8 * g + t + 1]) for t in range(8)]
        d = {(s, t): full(columns[t][s:s + 1]) for t in range(8) for s in range(t, 8)}
        a = [full(left[g][t:t + 1]) for t in range(8)]
        b = [full(right[g][t:t + 1]) for t in range(8)]
        following = [full(left[g + 1][:, 8 * g + t:8 * g + t + 1]) for t in range(8)] if g + 1 < groups else None
        ratio, recip = {}, [None] * 8
        for t in range(8):
            if recip[t] is None:
                recip[t] = reciprocal(d[t, t])
            if t % 2 == 0:
                unit = full(guess[:, 8 * g + t:8 * g + t + 1])
                near = d[t, t] * unit
                recip[t + 1] = near * reciprocal(near * d[t + 1, t + 1] - d[t + 1, t] * (d[t + 1, t] * unit))
            for s in range(t + 1, 8):
                ratio[s, t] = d[s, t] * recip[t]
            for s in range(t + 1, 8):
                for u in range(t + 1, s + 1):
                    d[s, u] = d[s, u] - ratio[s, t] * d[u, t]
                a[s] = a[s] - ratio[s, t] * a[t]
                b[s] = b[s] - ratio[s, t] * b[t]
                if following:
                    following[s] = following[s] - ratio[s, t] * following[t]
        upper = inverse = jnp.zeros((8, ALL), jnp.float32)
        for t in range(8):
            scale = lax.rsqrt(d[t, t])
            upper = jnp.where(sub == t, a[t] * scale, upper)
            inverse = jnp.where(sub == t, b[t] * scale, inverse)
        uppers.append(jnp.where(lane >= sub + 8 * g, upper, 0.0))
        inverses.append(inverse)
        a = [a[t] * recip[t] for t in range(8)]
        b = [b[t] * recip[t] for t in range(8)]
        if following:
            left[g + 1] = left[g + 1] - tree([following[t] * a[t] for t in range(8)])
            right[g + 1] = right[g + 1] - tree([following[t] * b[t] for t in range(8)])
        for t in range(7, 0, -1):
            for s in range(t):
                a[s] = a[s] - ratio[t, s] * a[t]
                b[s] = b[s] - ratio[t, s] * b[t]
        for k in range(g + (2 if following else 1), groups):
            below = [full(left[k][:, 8 * g + t:8 * g + t + 1]) for t in range(8)]
            left[k] = left[k] - tree([below[t] * a[t] for t in range(8)])
            right[k] = right[k] - tree([below[t] * b[t] for t in range(8)])
    return jnp.concatenate(inverses, axis=0), jnp.concatenate(uppers, axis=0)


def swap(rows, sub):
    for k in (4, 2, 1):
        low, new = (sub & k) == 0, list(rows)
        for i in range(8):
            if not i & k:
                new[i] = jnp.where(low, rows[i], pltpu.roll(rows[i | k], k, 0))
                new[i | k] = jnp.where(low, pltpu.roll(rows[i], 8 - k, 0), rows[i | k])
        rows = new
    return rows


def whole_row(i, s_ref, west_ref, east_ref):
    lane = lanes_of(ALL - B)
    row = s_ref[i, B:, :]
    start = SPAN * (i + RIM) + RIM
    for ref, target in ((west_ref, 0), (east_ref, LON - RIM)):
        k = start // LON
        side = ref[:, k * LON:(k + 1) * LON]
        if (start + RIM - 1) // LON > k:
            side = jnp.where(lane < start - k * LON, ref[:, (k + 1) * LON:(k + 2) * LON], side)
        side = pltpu.roll(side, (target - start) % LON, 1)
        row = jnp.where((lane >= target) & (lane < target + RIM), side, row)
    return jnp.concatenate([s_ref[i, :B, :], row], axis=0)


def basis(parts_ref, s_ref, west_ref, east_ref, q_hbm, alpha_ref, beta_ref, q_ref, high_ref, middle_ref, low_ref, sems):
    for i in range(0, LAT, 2):
        pair = [whole_row(j, s_ref, west_ref, east_ref) for j in (i, i + 1)]
        a, b, c = split(jnp.concatenate(pair, axis=1))
        high_ref[i // 2] = a
        middle_ref[i // 2] = b
        low_ref[i // 2] = c
    total = parts_ref[0]
    for i in range(1, parts_ref.shape[0]):
        total += parts_ref[i]
    inverse, upper = factor(unpack(total * (1.0 / CELLS)))
    lane = lax.broadcasted_iota(jnp.int32, (ALL, ALL), 1)
    own = jnp.where(lane < B, 1.0, jnp.where(lane < ITERS * B, 1.0 + SHIFT, 0.0))
    image = inverse * own + jnp.where(lane >= B, pltpu.roll(inverse, B, 1), 0.0)
    coeffs = lax.dot_general(upper, image, NT, precision=HIGH, preferred_element_type=jnp.float32)
    for k in range(ITERS):
        here, after = slice(k * B, (k + 1) * B), slice((k + 1) * B, (k + 2) * B)
        alpha_ref[k] = coeffs[here, here]
        beta_ref[k] = coeffs[after, here]
    high, middle, low = split(inverse)
    two = jnp.concatenate([high, middle], axis=1)
    three = jnp.concatenate([high, middle, low], axis=1)
    dot = lambda a, b: jnp.dot(a, b, preferred_element_type=jnp.float32)
    sub = lax.broadcasted_iota(jnp.int32, (8, LON), 0)
    copies = []
    for g in range(LAT // 8):
        rows = []
        for i in range(8 * g, 8 * g + 8, 2):
            a, b, c = high_ref[i // 2], middle_ref[i // 2], low_ref[i // 2]
            new = dot(three, jnp.concatenate([a, a, a], axis=0)) + dot(two, jnp.concatenate([b, b], axis=0)) + dot(high, c)
            rows += [new[:, :LON], new[:, LON:]]
        for v in range(0, ALL, 8):
            for t, tile in enumerate(swap([row[v:v + 8] for row in rows], sub)):
                q_ref[v + t, 8 * g:8 * g + 8, :] = tile
        chunk = pl.ds(8 * g, 8)
        copies.append(pltpu.make_async_copy(q_ref.at[:, chunk, :], q_hbm.at[:, chunk, :], sems.at[g]))
        copies[-1].start()
    for copy in copies:
        copy.wait()


def body(start_block, sea_mask, depth_levels):
    x = start_block.reshape(B * LAT, LON)
    x, sea_mask, depth_levels = [pltpu.with_memory_space_constraint(v, pltpu.HBM) for v in (x, sea_mask, depth_levels)]
    edge = (RIM, B + 8, LON)
    anywhere = pl.BlockSpec(memory_space=pl.ANY)
    small = pltpu.VMEM((LAT, LON), jnp.int32)
    inputs = dict(in_specs=[pl.BlockSpec(memory_space=pltpu.HBM)] * 3)
    room = [pltpu.VMEM((B * LAT, LON), jnp.float32), small, small, pltpu.SemaphoreType.DMA((3,))]
    near, far = call(edge_rows, (edge, edge), room, **inputs)(x, sea_mask, depth_levels)
    far = lax.ppermute(far, ROW, [(i, ((i + 1) ^ 1) - 1) for i in range(1, 7)])
    near = lax.ppermute(near, ROW, [(i, i ^ 1) for i in range(8)])
    flat = (B + 8, FLAT)
    core, part_west, part_east = call(
        core_rows, ((LAT, B + 8, LON), flat, flat), room, flops=1 << 22, moved=1 << 20, **inputs
    )(x, sea_mask, depth_levels)
    near, far, north, south, own_west, own_east = call(side_columns, (flat, flat, edge, edge, flat, flat))(
        near, far, part_west, part_east
    )
    far = lax.ppermute(far, COL, [(i, (((i + 1) ^ 1) - 1) % 32) for i in range(32)])
    near = lax.ppermute(near, COL, [(i, i ^ 1) for i in range(32)])
    wide = pltpu.VMEM((ROWS, B, LON), jnp.float32)
    thin = pltpu.VMEM((ROWS, 8, LON), jnp.float32)
    square = (ALL, ALL)
    s, even, half = call(
        inside, ((LAT, ALL, LON), square, square), [wide, wide, thin, thin, thin], flops=1 << 28, moved=1 << 23
    )(core, north, south)
    rim = (ALL - B, FLAT)
    gram, west, east = call(border, ((B + 8, LON), rim, rim))(near, far, own_west, own_east, even, half)
    pair = lax.all_gather(gram, "core")
    copies = call(spread, ((16, B + 8, LON),))(pair)[0]
    parts = lax.all_to_all(copies, ("x", "y"), 0, 0)
    copies = call(spread, ((8, B + 8, LON),))(parts)[0]
    parts = lax.all_to_all(copies, "z", 0, 0)
    vmem = pl.BlockSpec(memory_space=pltpu.VMEM)
    return call(
        basis,
        ((ALL, LAT, LON), (ITERS, B, B), (ITERS, B, B)),
        [pltpu.VMEM((ALL, LAT, LON), jnp.float32)] + [pltpu.VMEM((LAT // 2, ALL, 2 * LON), jnp.bfloat16)] * 3
        + [pltpu.SemaphoreType.DMA((LAT // 8,))],
        out_specs=(anywhere, vmem, vmem),
    )(parts, s, west, east)


def solution(mesh):
    torus = Mesh(mesh.devices.reshape(4, 2, 8, 4), ("x", "core", "z", "y"))
    in_specs = (P(None, ROW, COL), P(ROW, COL), P(ROW, COL))
    out_specs = (P(None, ROW, COL), P(), P())
    return jax.shard_map(body, mesh=torus, in_specs=in_specs, out_specs=out_specs, check_vma=False)
```

```python
import jax
import jax.numpy as jnp
from jax import lax
from jax.experimental import pallas as pl
from jax.experimental.pallas import tpu as pltpu
from jax.sharding import Mesh, PartitionSpec as P

ITERS = 3
LEVELS = 50.0
KAPPA = 1.5
SHIFT = 3.0
CELLS = 1048576.0

B = 32
LAT = 32
LON = 128
RIM = 3
ROWS = LAT + 2 * RIM
SPAN = 3 * RIM
FLAT = 3 * LON
ALL = (ITERS + 1) * B
HALF = B // 2
PIECE = 64
HALVES = [(k, part) for k in range(ITERS) for part in range(2)]
HIGH = lax.Precision.HIGHEST
ROW, COL = ("x", "core"), ("z", "y")
NT = (((1,), (1,)), ((), ()))
PARAMS = pltpu.CompilerParams(vmem_limit_bytes=48 * 1024 * 1024)


def lanes_of(rows):
    return lax.broadcasted_iota(jnp.int32, (rows, LON), 1)


def call(kernel, outs, scratch=(), flops=0, moved=0, **specs):
    return pl.pallas_call(
        kernel,
        **specs,
        out_shape=tuple(jax.ShapeDtypeStruct(s, jnp.float32) for s in outs),
        scratch_shapes=list(scratch),
        compiler_params=PARAMS,
        cost_estimate=pl.CostEstimate(flops=flops, bytes_accessed=moved, transcendentals=0),
    )


def edge_rows(x_hbm, mask_hbm, depth_hbm, far_ref, near_ref, x_ref, h_ref, mask_ref, depth_ref, sems):
    pairs = ((x_hbm, x_ref), (mask_hbm, mask_ref), (depth_hbm, depth_ref))
    copies = [pltpu.make_async_copy(a, b, sems.at[i]) for i, (a, b) in enumerate(pairs)]
    for copy in copies:
        copy.start()
    for copy in copies[1:]:
        copy.wait()
    h_ref[...] = mask_ref[...].astype(jnp.float32) * depth_ref[...].astype(jnp.float32) / LEVELS
    copies[0].wait()
    odd = lax.axis_index("core") == 1
    for i in range(RIM):
        top = masked_row(i, x_ref, h_ref)
        bottom = masked_row(LAT - RIM + i, x_ref, h_ref)
        near_ref[i] = jnp.where(odd, top, bottom)
        far_ref[i] = jnp.where(odd, bottom, top)


def masked_row(lat, x_ref, h_ref):
    depth = h_ref[pl.ds(lat, 1), :]
    row = jnp.where(depth > 0.0, x_ref[pl.ds(lat, B, stride=LAT), :], 0.0)
    return jnp.concatenate([row, jnp.broadcast_to(depth, (8, LON))], axis=0)


def pack_sides(row, r, west, east):
    lane = lanes_of(B + 8)
    for sides, source, target in ((west, 0, SPAN * r + RIM), (east, LON - 2 * RIM, SPAN * r)):
        moved = pltpu.roll(row, (target - source) % LON, 1)
        for k in range(target // LON, (target + 2 * RIM - 1) // LON + 1):
            place = lane + k * LON
            sides[k] = jnp.where((place >= target) & (place < target + 2 * RIM), moved, sides[k])


def chunks(flat):
    return [flat[:, k * LON:(k + 1) * LON] for k in range(FLAT // LON)]


def core_rows(x_ref, h_ref, core_ref, west_ref, east_ref):
    west, east = chunks(jnp.zeros((B + 8, FLAT), jnp.float32)), chunks(jnp.zeros((B + 8, FLAT), jnp.float32))
    for i in range(LAT):
        row = masked_row(i, x_ref, h_ref)
        core_ref[i] = row
        pack_sides(row, i + RIM, west, east)
    west_ref[...] = jnp.concatenate(west, axis=1)
    east_ref[...] = jnp.concatenate(east, axis=1)


def side_columns(near_ref, far_ref, part_west_ref, part_east_ref,
                 far_out, near_out, north_ref, south_ref, west_ref, east_ref):
    odd = lax.axis_index("core") == 1
    west, east = chunks(part_west_ref[...]), chunks(part_east_ref[...])
    for i in range(RIM):
        north = jnp.where(odd, near_ref[i], far_ref[i])
        south = jnp.where(odd, far_ref[i], near_ref[i])
        north_ref[i] = north
        south_ref[i] = south
        pack_sides(north, i, west, east)
        pack_sides(south, i + RIM + LAT, west, east)
    west, east = jnp.concatenate(west, axis=1), jnp.concatenate(east, axis=1)
    west_ref[...] = west
    east_ref[...] = east
    to_west, to_east = pltpu.roll(west, RIM, 1), pltpu.roll(east, FLAT - RIM, 1)
    odd = lax.axis_index("y") % 2 == 1
    near_out[...] = jnp.where(odd, to_west, to_east)
    far_out[...] = jnp.where(odd, to_east, to_west)


def split(value):
    high = value.astype(jnp.bfloat16)
    rest = value - high.astype(jnp.float32)
    middle = rest.astype(jnp.bfloat16)
    low = (rest - middle.astype(jnp.float32)).astype(jnp.bfloat16)
    return high, middle, low


def four(field):
    return jnp.concatenate([field] * (B // 8), axis=0)


def outer(left, right):
    return lax.dot_general(left, right, NT, preferred_element_type=jnp.float32)


def products(value):
    high, middle, low = split(value)
    both = outer(high, jnp.concatenate([high, middle], axis=0))
    return both[:, :ALL] + outer(middle, middle), both[:, ALL:] + outer(high, low)


def inside(core_ref, north_ref, south_ref, s_ref, even_ref, half_ref, k1_ref, k2_ref, down_ref, right_ref, centre_ref):
    def base(r):
        if r < RIM:
            return north_ref[r]
        return core_ref[r - RIM] if r < RIM + LAT else south_ref[r - RIM - LAT]

    for r in range(ROWS - 1):
        h = base(r)[B:]
        down_ref[r] = KAPPA * jnp.minimum(h, base(r + 1)[B:])
        right_ref[r] = KAPPA * jnp.minimum(h, pltpu.roll(h, LON - 1, 1))
        centre_ref[r] = jnp.where(h > 0.0, 0.0, -1.0)
    levels = (
        (lambda r: base(r)[:B], k1_ref, 0.0),
        (lambda r: k1_ref[r], k2_ref, SHIFT),
        (lambda r: k2_ref[r], None, SHIFT),
    )
    for step, (source, target, shift) in enumerate(levels):
        first, last = step + 1, ROWS - 2 - step
        v, after = source(first - 1), source(first)
        flux = four(down_ref[first - 1]) * (v - after)
        for r in range(first, last + 1):
            v, after = after, source(r + 1)
            down = four(down_ref[r]) * (v - after)
            right = four(right_ref[r]) * (v - pltpu.roll(v, LON - 1, 1))
            new = four(centre_ref[r] - shift) * v + ((down - flux) + (right - pltpu.roll(right, 1, 1)))
            flux = down
            if target is not None:
                target[r] = new
            if RIM <= r < RIM + LAT:
                s_ref[r - RIM, (step + 1) * B:(step + 2) * B, :] = new
    lane = lanes_of(ALL)
    clean = (lane >= RIM) & (lane < LON - RIM)
    even = half = jnp.zeros((ALL, ALL), jnp.float32)
    for i in range(0, LAT, 2):
        rows = []
        for j in (i, i + 1):
            s_ref[j, :B, :] = core_ref[j, :B]
            rows.append(jnp.where(clean, s_ref[j], 0.0))
        one, two = products(jnp.concatenate(rows, axis=1))
        even += one
        half += two
    even_ref[...] = even
    half_ref[...] = half


def border(near_ref, far_ref, own_west_ref, own_east_ref, even_ref, half_ref, gram_ref, west_ref, east_ref):
    odd = lax.axis_index("y") % 2 == 1
    near, far = near_ref[...], far_ref[...]
    lane = lax.broadcasted_iota(jnp.int32, (B + 8, FLAT), 1)
    line = (lane * 7282) >> 16
    place = lane - line * SPAN
    west = jnp.where(place < RIM, jnp.where(odd, near, far), own_west_ref[...])
    east = jnp.where(place >= 2 * RIM, jnp.where(odd, far, near), own_east_ref[...])
    joint = place[:8] < SPAN - 1
    kept = (place[:1] >= RIM) & (place[:1] < 2 * RIM) & (line[:1] >= RIM) & (line[:1] < RIM + LAT)
    fields = []
    for start, out_ref in ((west, west_ref), (east, east_ref)):
        h = start[B:]
        down = four(KAPPA * jnp.minimum(h, pltpu.roll(h, FLAT - SPAN, 1)))
        right = four(jnp.where(joint, KAPPA * jnp.minimum(h, pltpu.roll(h, FLAT - 1, 1)), 0.0))
        centre = jnp.where(h > 0.0, 0.0, -1.0)
        v = start[:B]
        found = [v]
        for shift in (0.0, SHIFT, SHIFT):
            flow = down * (v - pltpu.roll(v, FLAT - SPAN, 1))
            side = right * (v - pltpu.roll(v, FLAT - 1, 1))
            v = four(centre - shift) * v + (
                (flow - pltpu.roll(flow, SPAN, 1)) + (side - pltpu.roll(side, 1, 1))
            )
            found.append(v)
        out_ref[...] = jnp.concatenate(found[1:], axis=0)
        fields.append(jnp.where(kept, jnp.concatenate(found, axis=0), 0.0))
    even, half = products(jnp.concatenate(fields, axis=1))
    even += even_ref[...]
    half += half_ref[...]
    gram = even + half + half.T
    row = lax.broadcasted_iota(jnp.int32, (B, LON), 0)
    lane = lax.broadcasted_iota(jnp.int32, (B, LON), 1)
    packed = diagonal = jnp.zeros((B, LON), jnp.float32)
    for k in range(ITERS + 1):
        own = gram[k * B:(k + 1) * B]
        after = pltpu.roll(own, LON - B, 1)
        here = (lane >= k * B) & (lane < (k + 1) * B)
        packed = jnp.where(here, jnp.where(lane - k * B >= row, own, after), packed)
        diagonal = jnp.where(here & (lane - k * B == row), after, diagonal)
    line = jnp.sum(diagonal, axis=0, keepdims=True)
    for n, (k, part) in enumerate(HALVES):
        there = (row == B - 1 - n) & (lane >= ITERS * B) & (lane < ITERS * B + HALF)
        packed = jnp.where(there, pltpu.roll(line, (ITERS * B - k * B - part * HALF) % LON, 1), packed)
    gram_ref[...] = packed


def spread(parts_ref, out_ref):
    total = parts_ref[0]
    for i in range(1, parts_ref.shape[0]):
        total += parts_ref[i]
    for i in range(out_ref.shape[0]):
        out_ref[i] = total


def unpack(total):
    row = lax.broadcasted_iota(jnp.int32, (B, LON), 0)
    lane = lax.broadcasted_iota(jnp.int32, (B, LON), 1)
    block, place = lane >> 5, lane & (B - 1)
    turned = jnp.concatenate([total, jnp.zeros((LON - B, LON), jnp.float32)], axis=0).T
    mirror = jnp.zeros((B, LON), jnp.float32)
    for k in range(ITERS + 1):
        part = turned[k * B:(k + 1) * B]
        mirror = jnp.where(block == k, pltpu.roll(part, k * B, 1) if k else part, mirror)
    even = jnp.where(place >= row, total, mirror)
    odd = jnp.where(place < row, total, mirror)
    line = jnp.zeros((1, LON), jnp.float32)
    for n, (k, part) in enumerate(HALVES):
        target = k * B + part * HALF
        moved = pltpu.roll(total[B - 1 - n:B - n], (target - ITERS * B) % LON, 1)
        line = jnp.where((lane[:1] >= target) & (lane[:1] < target + HALF), moved, line)
    odd = jnp.where(place == row, line, odd)
    move = lambda field, k: pltpu.roll(field, (k * B) % LON, 1)
    even1, even2, odd1, odd2, odd3 = move(even, 1), move(even, -1), move(odd, 1), move(odd, 2), move(odd, 3)
    pick = lambda a, b, c, d: jnp.where(block == 0, a, jnp.where(block == 1, b, jnp.where(block == 2, c, d)))
    corner = move(odd, -1)
    return jnp.concatenate(
        [
            pick(even, odd1, even1 - SHIFT * odd2, odd2 - SHIFT * (move(even, 2) - SHIFT * odd3)),
            pick(odd, even, odd1, even1),
            pick(even2 - SHIFT * odd, odd, even, odd1),
            pick(corner - SHIFT * (even2 - SHIFT * odd), even2, odd, even),
        ],
        axis=0,
    )


def reciprocal(value):
    return 1.0 / value


def factor(gram):
    groups = ALL // 8
    lane = lax.broadcasted_iota(jnp.int32, (8, ALL), 1)
    sub = lax.broadcasted_iota(jnp.int32, (8, ALL), 0)
    full = lambda value: jnp.broadcast_to(value, (8, ALL))
    line = lambda value, t: full(value[t:t + 1])
    tree = lambda p: ((p[0] + p[1]) + (p[2] + p[3])) + ((p[4] + p[5]) + (p[6] + p[7]))
    weigh = lambda p, q: tree([p[t] * q[t] for t in range(8)])
    work = [gram[8 * g:8 * g + 8] for g in range(groups)]
    columns = lambda k, g: [full(work[k][:, 8 * g + t:8 * g + t + 1]) for t in range(8)] if k < groups else None
    diagonal = sum(jnp.where(lane == sub + 8 * g, work[g], 0.0) for g in range(groups))
    guess = full(reciprocal(jnp.sum(diagonal, axis=0, keepdims=True)))
    uppers, inverses = [], []
    own, after = columns(0, 0), columns(1, 0)
    for g in range(groups):
        later, coming = columns(g + 2, g), columns(g + 1, g + 1)
        a = work[g]
        b = jnp.where(lane == sub + 8 * g, 1.0, jnp.where(lane < 8 * g, work[g], 0.0))
        recip, ratio, pivot = [None] * 8, {}, []
        for t in range(8):
            pivot.append(line(own[t], t))
            if recip[t] is None:
                recip[t] = reciprocal(pivot[t])
            if t % 2 == 0 and g > 0:
                unit = full(guess[:, 8 * g + t:8 * g + t + 1])
                near, cross = pivot[t] * unit, line(own[t], t + 1)
                recip[t + 1] = near * reciprocal(near * line(own[t + 1], t + 1) - cross * (cross * unit))
            column = jnp.where(sub > t, own[t] * recip[t], 0.0)
            for s in range(t + 1, 8):
                ratio[s, t] = line(column, s)
                own[s] = own[s] - column * line(own[t], s)
            if t < 7:
                a = a - column * line(a, t)
                b = b - column * line(b, t)
                for ahead in (after, later):
                    for s in range(t + 1, 8) if ahead else ():
                        ahead[s] = ahead[s] - ratio[s, t] * ahead[t]
        pivots = inverted = jnp.zeros((8, ALL), jnp.float32)
        for t in range(8):
            pivots = jnp.where(sub == t, pivot[t], pivots)
            inverted = jnp.where(sub == t, recip[t], inverted)
        scale = lax.rsqrt(pivots)
        uppers.append(jnp.where(lane >= sub + 8 * g, a * scale, 0.0))
        inverses.append(b * scale)
        if g + 1 == groups:
            break
        c = jnp.where(lane < 8 * g + 8, b, a) * inverted
        c = [line(c, t) for t in range(8)]
        scaled = [after[t] * recip[t] for t in range(8)]
        own = [coming[u] - weigh(after, [line(scaled[t], u) for t in range(8)]) for u in range(8)]
        block = (lane >= 8 * g) & (lane < 8 * g + 8)
        for k, ahead in ((g + 1, after), (g + 2, later)):
            if ahead:
                work[k] = jnp.where(block, 0.0, work[k]) - weigh(ahead, c)
        after = columns(g + 2, g + 1)
        for t in range(7, 0, -1):
            for s in range(t):
                c[s] = c[s] - ratio[t, s] * c[t]
        for k in range(g + 3, groups):
            work[k] = jnp.where(block, 0.0, work[k]) - weigh(columns(k, g), c)
    return jnp.concatenate(inverses, axis=0), jnp.concatenate(uppers, axis=0)


def swap(rows, sub):
    for k in (4, 2, 1):
        low, new = (sub & k) == 0, list(rows)
        for i in range(8):
            if not i & k:
                new[i] = jnp.where(low, rows[i], pltpu.roll(rows[i | k], k, 0))
                new[i | k] = jnp.where(low, pltpu.roll(rows[i], 8 - k, 0), rows[i | k])
        rows = new
    return rows


def whole_row(i, s_ref, west_ref, east_ref):
    lane = lanes_of(ALL - B)
    row = s_ref[i, B:, :]
    start = SPAN * (i + RIM) + RIM
    for ref, target in ((west_ref, 0), (east_ref, LON - RIM)):
        k = start // LON
        side = ref[:, k * LON:(k + 1) * LON]
        if (start + RIM - 1) // LON > k:
            side = jnp.where(lane < start - k * LON, ref[:, (k + 1) * LON:(k + 2) * LON], side)
        side = pltpu.roll(side, (target - start) % LON, 1)
        row = jnp.where((lane >= target) & (lane < target + RIM), side, row)
    return jnp.concatenate([s_ref[i, :B, :], row], axis=0)


def basis(parts_ref, s_ref, west_ref, east_ref, q_hbm, alpha_hbm, beta_hbm,
          q_ref, alpha_ref, beta_ref, high_ref, middle_ref, low_ref, sems):
    for i in range(0, LAT, 2):
        pair = [whole_row(j, s_ref, west_ref, east_ref) for j in (i, i + 1)]
        a, b, c = split(jnp.concatenate(pair, axis=1))
        high_ref[i // 2] = a
        middle_ref[i // 2] = b
        low_ref[i // 2] = c
    total = parts_ref[0]
    for i in range(1, parts_ref.shape[0]):
        total += parts_ref[i]
    inverse, upper = factor(unpack(total * (1.0 / CELLS)))
    lane = lax.broadcasted_iota(jnp.int32, (ALL, ALL), 1)
    own = jnp.where(lane < B, 1.0, jnp.where(lane < ITERS * B, 1.0 + SHIFT, 0.0))
    image = inverse * own + jnp.where(lane >= B, pltpu.roll(inverse, B, 1), 0.0)
    coeffs = lax.dot_general(upper, image, NT, precision=HIGH, preferred_element_type=jnp.float32)
    for k in range(ITERS):
        here, after = slice(k * B, (k + 1) * B), slice((k + 1) * B, (k + 2) * B)
        alpha_ref[k] = coeffs[here, here]
        beta_ref[k] = coeffs[after, here]
    copies = [
        pltpu.make_async_copy(alpha_ref, alpha_hbm, sems.at[0]),
        pltpu.make_async_copy(beta_ref, beta_hbm, sems.at[1]),
    ]
    for copy in copies:
        copy.start()
    high, middle, low = split(inverse)
    two = jnp.concatenate([high, middle], axis=1)
    three = jnp.concatenate([high, middle, low], axis=1)
    dot = lambda a, b: jnp.dot(a, b, preferred_element_type=jnp.float32)
    sub = lax.broadcasted_iota(jnp.int32, (8, LON), 0)
    for g in range(LAT // 8):
        rows = []
        for i in range(8 * g, 8 * g + 8, 2):
            a, b, c = high_ref[i // 2], middle_ref[i // 2], low_ref[i // 2]
            new = dot(three, jnp.concatenate([a, a, a], axis=0)) + dot(two, jnp.concatenate([b, b], axis=0)) + dot(high, c)
            rows += [new[:, :LON], new[:, LON:]]
        chunk = pl.ds(8 * g, 8)
        for v in range(0, ALL, 8):
            for t, tile in enumerate(swap([row[v:v + 8] for row in rows], sub)):
                q_ref[v + t, 8 * g:8 * g + 8, :] = tile
            if v % PIECE == PIECE - 8:
                block = pl.ds(v + 8 - PIECE, PIECE)
                sem = sems.at[len(copies)]
                copies.append(pltpu.make_async_copy(q_ref.at[block, chunk, :], q_hbm.at[block, chunk, :], sem))
                copies[-1].start()
    for copy in copies:
        copy.wait()


def body(start_block, sea_mask, depth_levels):
    x = start_block.reshape(B * LAT, LON)
    x, sea_mask, depth_levels = [pltpu.with_memory_space_constraint(v, pltpu.HBM) for v in (x, sea_mask, depth_levels)]
    edge = (RIM, B + 8, LON)
    anywhere = pl.BlockSpec(memory_space=pl.ANY)
    small = pltpu.VMEM((LAT, LON), jnp.int32)
    far, near, x, h = call(
        edge_rows,
        (edge, edge, (B * LAT, LON), (LAT, LON)),
        [small, small, pltpu.SemaphoreType.DMA((3,))],
        in_specs=[pl.BlockSpec(memory_space=pltpu.HBM)] * 3,
    )(x, sea_mask, depth_levels)
    far = lax.ppermute(far, ROW, [(i, ((i + 1) ^ 1) - 1) for i in range(1, 7)])
    near = lax.ppermute(near, ROW, [(i, i ^ 1) for i in range(8)])
    flat = (B + 8, FLAT)
    core, part_west, part_east = call(
        core_rows, ((LAT, B + 8, LON), flat, flat), flops=1 << 22, moved=1 << 20
    )(x, h)
    far, near, north, south, own_west, own_east = call(side_columns, (flat, flat, edge, edge, flat, flat))(
        near, far, part_west, part_east
    )
    far = lax.ppermute(far, COL, [(i, (((i + 1) ^ 1) - 1) % 32) for i in range(32)])
    near = lax.ppermute(near, COL, [(i, i ^ 1) for i in range(32)])
    wide = pltpu.VMEM((ROWS, B, LON), jnp.float32)
    thin = pltpu.VMEM((ROWS, 8, LON), jnp.float32)
    square = (ALL, ALL)
    s, even, half = call(
        inside, ((LAT, ALL, LON), square, square), [wide, wide, thin, thin, thin], flops=1 << 28, moved=1 << 23
    )(core, north, south)
    rim = (ALL - B, FLAT)
    gram, west, east = call(border, ((B, LON), rim, rim))(near, far, own_west, own_east, even, half)
    pair = lax.all_gather(gram, "core")
    copies = call(spread, ((16, B, LON),))(pair)[0]
    parts = lax.all_to_all(copies, ("x", "y"), 0, 0)
    copies = call(spread, ((8, B, LON),))(parts)[0]
    parts = lax.all_to_all(copies, "z", 0, 0)
    table = (ITERS, B, B)
    results = ((ALL, LAT, LON), table, table)
    return call(
        basis,
        results,
        [pltpu.VMEM(shape, jnp.float32) for shape in results]
        + [pltpu.VMEM((LAT // 2, ALL, 2 * LON), jnp.bfloat16)] * 3
        + [pltpu.SemaphoreType.DMA((2 + (LAT // 8) * (ALL // PIECE),))],
        out_specs=(anywhere,) * 3,
    )(parts, s, west, east)


def solution(mesh):
    torus = Mesh(mesh.devices.reshape(4, 2, 8, 4), ("x", "core", "z", "y"))
    in_specs = (P(None, ROW, COL), P(ROW, COL), P(ROW, COL))
    out_specs = (P(None, ROW, COL), P(), P())
    return jax.shard_map(body, mesh=torus, in_specs=in_specs, out_specs=out_specs, check_vma=False)
```

```python
import jax
import jax.numpy as jnp
from jax import lax
from jax.experimental import pallas as pl
from jax.experimental.pallas import tpu as pltpu
from jax.sharding import Mesh, PartitionSpec as P

ITERS = 3
LEVELS = 50.0
KAPPA = 1.5
CELLS = 1048576.0

B = 32
LAT = 32
LON = 128
RIM = 3
ROWS = LAT + 2 * RIM
SPAN = 3 * RIM
FLAT = 3 * LON
ALL = (ITERS + 1) * B
HALF = B // 2
PIECE = 64
HALVES = [(k, part) for k in range(ITERS) for part in range(2)]
HIGH = lax.Precision.HIGHEST
ROW, COL = ("x", "core"), ("z", "y")
NT = (((1,), (1,)), ((), ()))
PARAMS = pltpu.CompilerParams(vmem_limit_bytes=48 * 1024 * 1024)


def lanes_of(rows):
    return lax.broadcasted_iota(jnp.int32, (rows, LON), 1)


def call(kernel, outs, scratch=(), flops=0, moved=0, **specs):
    return pl.pallas_call(
        kernel,
        **specs,
        out_shape=tuple(jax.ShapeDtypeStruct(s, jnp.float32) for s in outs),
        scratch_shapes=list(scratch),
        compiler_params=PARAMS,
        cost_estimate=pl.CostEstimate(flops=flops, bytes_accessed=moved, transcendentals=0),
    )


def edge_rows(x_hbm, mask_hbm, depth_hbm, far_ref, near_ref, x_ref, h_ref, mask_ref, depth_ref, sems):
    pairs = ((x_hbm, x_ref), (mask_hbm, mask_ref), (depth_hbm, depth_ref))
    copies = [pltpu.make_async_copy(a, b, sems.at[i]) for i, (a, b) in enumerate(pairs)]
    for copy in copies:
        copy.start()
    for copy in copies[1:]:
        copy.wait()
    h_ref[...] = mask_ref[...].astype(jnp.float32) * depth_ref[...].astype(jnp.float32) / LEVELS
    copies[0].wait()
    odd = lax.axis_index("core") == 1
    for i in range(RIM):
        top = masked_row(i, x_ref, h_ref)
        bottom = masked_row(LAT - RIM + i, x_ref, h_ref)
        near_ref[i] = jnp.where(odd, top, bottom)
        far_ref[i] = jnp.where(odd, bottom, top)


def masked_row(lat, x_ref, h_ref):
    depth = h_ref[pl.ds(lat, 1), :]
    row = jnp.where(depth > 0.0, x_ref[pl.ds(lat, B, stride=LAT), :], 0.0)
    return jnp.concatenate([row, jnp.broadcast_to(depth, (8, LON))], axis=0)


def pack_sides(row, r, west, east):
    lane = lanes_of(B + 8)
    for sides, source, target in ((west, 0, SPAN * r + RIM), (east, LON - 2 * RIM, SPAN * r)):
        moved = pltpu.roll(row, (target - source) % LON, 1)
        for k in range(target // LON, (target + 2 * RIM - 1) // LON + 1):
            place = lane + k * LON
            sides[k] = jnp.where((place >= target) & (place < target + 2 * RIM), moved, sides[k])


def chunks(flat):
    return [flat[:, k * LON:(k + 1) * LON] for k in range(FLAT // LON)]


def core_rows(x_ref, h_ref, core_ref, west_ref, east_ref):
    west, east = chunks(jnp.zeros((B + 8, FLAT), jnp.float32)), chunks(jnp.zeros((B + 8, FLAT), jnp.float32))
    for i in range(LAT):
        row = masked_row(i, x_ref, h_ref)
        core_ref[i] = row
        pack_sides(row, i + RIM, west, east)
    west_ref[...] = jnp.concatenate(west, axis=1)
    east_ref[...] = jnp.concatenate(east, axis=1)


def side_columns(far_ref, near_ref, part_west_ref, part_east_ref,
                 far_out, near_out, north_ref, south_ref, west_ref, east_ref):
    odd = lax.axis_index("core") == 1
    west, east = chunks(part_west_ref[...]), chunks(part_east_ref[...])
    for i in range(RIM):
        north = jnp.where(odd, near_ref[i], far_ref[i])
        south = jnp.where(odd, far_ref[i], near_ref[i])
        north_ref[i] = north
        south_ref[i] = south
        pack_sides(north, i, west, east)
        pack_sides(south, i + RIM + LAT, west, east)
    west, east = jnp.concatenate(west, axis=1), jnp.concatenate(east, axis=1)
    west_ref[...] = west
    east_ref[...] = east
    to_west, to_east = pltpu.roll(west, RIM, 1), pltpu.roll(east, FLAT - RIM, 1)
    odd = lax.axis_index("y") % 2 == 1
    near_out[...] = jnp.where(odd, to_west, to_east)
    far_out[...] = jnp.where(odd, to_east, to_west)


def split(value):
    high = value.astype(jnp.bfloat16)
    rest = value - high.astype(jnp.float32)
    middle = rest.astype(jnp.bfloat16)
    low = (rest - middle.astype(jnp.float32)).astype(jnp.bfloat16)
    return high, middle, low


def four(field):
    return jnp.concatenate([field] * (B // 8), axis=0)


def outer(left, right):
    return lax.dot_general(left, right, NT, preferred_element_type=jnp.float32)


def products(value):
    high, middle, low = split(value)
    both = outer(high, jnp.concatenate([high, middle], axis=0))
    return both[:, :ALL] + outer(middle, middle), both[:, ALL:] + outer(high, low)


def inside(core_ref, north_ref, south_ref, s_ref, own_ref, k1_ref, k2_ref, down_ref, right_ref, centre_ref):
    def base(r):
        if r < RIM:
            return north_ref[r]
        return core_ref[r - RIM] if r < RIM + LAT else south_ref[r - RIM - LAT]

    for r in range(ROWS - 1):
        h = base(r)[B:]
        down_ref[r] = KAPPA * jnp.minimum(h, base(r + 1)[B:])
        right_ref[r] = KAPPA * jnp.minimum(h, pltpu.roll(h, LON - 1, 1))
        centre_ref[r] = jnp.where(h > 0.0, 0.0, -1.0)
    levels = (
        (lambda r: base(r)[:B], k1_ref),
        (lambda r: k1_ref[r], k2_ref),
        (lambda r: k2_ref[r], None),
    )
    for step, (source, target) in enumerate(levels):
        first, last = step + 1, ROWS - 2 - step
        v, after = source(first - 1), source(first)
        flux = four(down_ref[first - 1]) * (v - after)
        for r in range(first, last + 1):
            v, after = after, source(r + 1)
            down = four(down_ref[r]) * (v - after)
            right = four(right_ref[r]) * (v - pltpu.roll(v, LON - 1, 1))
            new = four(centre_ref[r]) * v + ((down - flux) + (right - pltpu.roll(right, 1, 1)))
            flux = down
            if target is not None:
                target[r] = new
            if RIM <= r < RIM + LAT:
                s_ref[r - RIM, (step + 1) * B:(step + 2) * B, :] = new
    lane = lanes_of(ALL)
    clean = (lane >= RIM) & (lane < LON - RIM)
    even = half = jnp.zeros((ALL, ALL), jnp.float32)
    for i in range(0, LAT, 2):
        rows = []
        for j in (i, i + 1):
            s_ref[j, :B, :] = core_ref[j, :B]
            rows.append(jnp.where(clean, s_ref[j], 0.0))
        one, two = products(jnp.concatenate(rows, axis=1))
        even += one
        half += two
    own_ref[...] = even + half + half.T


def border(far_ref, near_ref, own_west_ref, own_east_ref, own_ref, gram_ref, west_ref, east_ref):
    odd = lax.axis_index("y") % 2 == 1
    near, far = near_ref[...], far_ref[...]
    lane = lax.broadcasted_iota(jnp.int32, (B + 8, FLAT), 1)
    line = (lane * 7282) >> 16
    place = lane - line * SPAN
    west = jnp.where(place < RIM, jnp.where(odd, near, far), own_west_ref[...])
    east = jnp.where(place >= 2 * RIM, jnp.where(odd, far, near), own_east_ref[...])
    joint = place[:8] < SPAN - 1
    kept = (place[:1] >= RIM) & (place[:1] < 2 * RIM) & (line[:1] >= RIM) & (line[:1] < RIM + LAT)
    fields = []
    for start, out_ref in ((west, west_ref), (east, east_ref)):
        h = start[B:]
        south = KAPPA * jnp.minimum(h, pltpu.roll(h, FLAT - SPAN, 1))
        right = jnp.where(joint, KAPPA * jnp.minimum(h, pltpu.roll(h, FLAT - 1, 1)), 0.0)
        north, left = four(pltpu.roll(south, SPAN, 1)), four(pltpu.roll(right, 1, 1))
        south, right = four(south), four(right)
        centre = four(jnp.where(h > 0.0, 0.0, -1.0))
        v = start[:B]
        found = [v]
        for step in range(ITERS):
            down = south * (v - pltpu.roll(v, FLAT - SPAN, 1)) + north * (v - pltpu.roll(v, SPAN, 1))
            over = right * (v - pltpu.roll(v, FLAT - 1, 1)) + left * (v - pltpu.roll(v, 1, 1))
            v = centre * v + (down + over)
            found.append(v)
        out_ref[...] = jnp.concatenate(found[1:], axis=0)
        fields.append(jnp.where(kept, jnp.concatenate(found, axis=0), 0.0))
    even, half = products(jnp.concatenate(fields, axis=1))
    gram = (own_ref[...] + even) + (half + half.T)
    row = lax.broadcasted_iota(jnp.int32, (B, LON), 0)
    lane = lax.broadcasted_iota(jnp.int32, (B, LON), 1)
    packed = diagonal = jnp.zeros((B, LON), jnp.float32)
    for k in range(ITERS + 1):
        own = gram[k * B:(k + 1) * B]
        after = pltpu.roll(own, LON - B, 1)
        here = (lane >= k * B) & (lane < (k + 1) * B)
        packed = jnp.where(here, jnp.where(lane - k * B >= row, own, after), packed)
        diagonal = jnp.where(here & (lane - k * B == row), after, diagonal)
    line = jnp.sum(diagonal, axis=0, keepdims=True)
    for n, (k, part) in enumerate(HALVES):
        there = (row == B - 1 - n) & (lane >= ITERS * B) & (lane < ITERS * B + HALF)
        packed = jnp.where(there, pltpu.roll(line, (ITERS * B - k * B - part * HALF) % LON, 1), packed)
    gram_ref[...] = packed


def spread(parts_ref, out_ref):
    total = parts_ref[0]
    for i in range(1, parts_ref.shape[0]):
        total += parts_ref[i]
    for i in range(out_ref.shape[0]):
        out_ref[i] = total


def join(own_ref, other_ref, out_ref):
    total = own_ref[...] + other_ref[...]
    for i in range(out_ref.shape[0]):
        out_ref[i] = total


def unpack(total):
    row = lax.broadcasted_iota(jnp.int32, (B, LON), 0)
    lane = lax.broadcasted_iota(jnp.int32, (B, LON), 1)
    block, place = lane >> 5, lane & (B - 1)
    turned = jnp.concatenate([jnp.where(block == k, total, 0.0) for k in range(ITERS + 1)], axis=0).T
    mirror = (turned[:B] + turned[B:2 * B]) + (turned[2 * B:3 * B] + turned[3 * B:])
    even = jnp.where(place >= row, total, mirror)
    odd = jnp.where(place < row, total, mirror)
    line = jnp.zeros((1, LON), jnp.float32)
    for n, (k, part) in enumerate(HALVES):
        target = k * B + part * HALF
        moved = pltpu.roll(total[B - 1 - n:B - n], (target - ITERS * B) % LON, 1)
        line = jnp.where((lane[:1] >= target) & (lane[:1] < target + HALF), moved, line)
    odd = jnp.where(place == row, line, odd)
    move = lambda field, k: pltpu.roll(field, (k * B) % LON, 1)
    pick = lambda a, b, c, d: jnp.where(block == 0, a, jnp.where(block == 1, b, jnp.where(block == 2, c, d)))
    even_on, even_back, odd_on, odd_back = move(even, 1), move(even, -1), move(odd, 1), move(odd, -1)
    rows = [
        pick(even, odd_on, even_on, move(odd, 2)),
        pick(odd, even, odd_on, even_on),
        pick(even_back, odd, even, odd_on),
        pick(odd_back, even_back, odd, even),
    ]
    return even, jnp.concatenate(rows, axis=0)


def reciprocal(value):
    return 1.0 / value


def factor(first, gram):
    groups = ALL // 8
    lane = lax.broadcasted_iota(jnp.int32, (8, ALL), 1)
    sub = lax.broadcasted_iota(jnp.int32, (8, ALL), 0)
    full = lambda value: jnp.broadcast_to(value, (8, ALL))
    line = lambda value, t: full(value[t:t + 1])
    tree = lambda p: ((p[0] + p[1]) + (p[2] + p[3])) + ((p[4] + p[5]) + (p[6] + p[7]))
    weigh = lambda p, q: tree([p[t] * q[t] for t in range(8)])
    work = [gram[8 * g:8 * g + 8] for g in range(groups)]
    columns = lambda k, g: [full(work[k][:, 8 * g + t:8 * g + t + 1]) for t in range(8)] if k < groups else None
    diagonal = sum(jnp.where(lane == sub + 8 * g, work[g], 0.0) for g in range(groups))
    guess = full(reciprocal(jnp.sum(diagonal, axis=0, keepdims=True)))
    uppers, inverses = [], []
    own, after = [[full(first[8 * k:8 * k + 8, t:t + 1]) for t in range(8)] for k in range(2)]
    for g in range(groups):
        later, coming = columns(g + 2, g), columns(g + 1, g + 1)
        a = work[g]
        b = jnp.where(lane == sub + 8 * g, 1.0, jnp.where(lane < 8 * g, work[g], 0.0))
        recip, ratio, pivot = [None] * 8, {}, []
        for t in range(8):
            pivot.append(line(own[t], t))
            if recip[t] is None:
                recip[t] = reciprocal(pivot[t])
            if t % 2 == 0 and g > 0:
                unit = full(guess[:, 8 * g + t:8 * g + t + 1])
                near, cross = pivot[t] * unit, line(own[t], t + 1)
                recip[t + 1] = near * reciprocal(near * line(own[t + 1], t + 1) - cross * (cross * unit))
            column = jnp.where(sub > t, own[t] * recip[t], 0.0)
            for s in range(t + 1, 8):
                ratio[s, t] = line(column, s)
                own[s] = own[s] - column * line(own[t], s)
            if t < 7:
                a = a - column * line(a, t)
                b = b - column * line(b, t)
                for ahead in (after, later):
                    for s in range(t + 1, 8) if ahead else ():
                        ahead[s] = ahead[s] - ratio[s, t] * ahead[t]
        pivots = inverted = jnp.zeros((8, ALL), jnp.float32)
        for t in range(8):
            pivots = jnp.where(sub == t, pivot[t], pivots)
            inverted = jnp.where(sub == t, recip[t], inverted)
        scale = lax.rsqrt(pivots)
        uppers.append(jnp.where(lane >= sub + 8 * g, a * scale, 0.0))
        inverses.append(b * scale)
        if g + 1 == groups:
            break
        c = jnp.where(lane < 8 * g + 8, b, a) * inverted
        c = [line(c, t) for t in range(8)]
        scaled = [after[t] * recip[t] for t in range(8)]
        own = [coming[u] - weigh(after, [line(scaled[t], u) for t in range(8)]) for u in range(8)]
        block = (lane >= 8 * g) & (lane < 8 * g + 8)
        for k, ahead in ((g + 1, after), (g + 2, later)):
            if ahead:
                work[k] = jnp.where(block, 0.0, work[k]) - weigh(ahead, c)
        after = columns(g + 2, g + 1)
        for t in range(7, 0, -1):
            for s in range(t):
                c[s] = c[s] - ratio[t, s] * c[t]
        for k in range(g + 3, groups):
            work[k] = jnp.where(block, 0.0, work[k]) - weigh(columns(k, g), c)
    return jnp.concatenate(inverses, axis=0), jnp.concatenate(uppers, axis=0)


def swap(rows, sub):
    for k in (4, 2, 1):
        low, new = (sub & k) == 0, list(rows)
        for i in range(8):
            if not i & k:
                new[i] = jnp.where(low, rows[i], pltpu.roll(rows[i | k], k, 0))
                new[i | k] = jnp.where(low, pltpu.roll(rows[i], 8 - k, 0), rows[i | k])
        rows = new
    return rows


def whole_row(i, s_ref, west_ref, east_ref):
    lane = lanes_of(ALL - B)
    row = s_ref[i, B:, :]
    start = SPAN * (i + RIM) + RIM
    for ref, target in ((west_ref, 0), (east_ref, LON - RIM)):
        k = start // LON
        side = ref[:, k * LON:(k + 1) * LON]
        if (start + RIM - 1) // LON > k:
            side = jnp.where(lane < start - k * LON, ref[:, (k + 1) * LON:(k + 2) * LON], side)
        side = pltpu.roll(side, (target - start) % LON, 1)
        row = jnp.where((lane >= target) & (lane < target + RIM), side, row)
    return jnp.concatenate([s_ref[i, :B, :], row], axis=0)


def basis(parts_ref, s_ref, west_ref, east_ref, q_hbm, alpha_hbm, beta_hbm,
          q_ref, alpha_ref, beta_ref, high_ref, middle_ref, low_ref, sems):
    for i in range(0, LAT, 2):
        pair = [whole_row(j, s_ref, west_ref, east_ref) for j in (i, i + 1)]
        a, b, c = split(jnp.concatenate(pair, axis=1))
        high_ref[i // 2] = a
        middle_ref[i // 2] = b
        low_ref[i // 2] = c
    total = parts_ref[0]
    for i in range(1, parts_ref.shape[0]):
        total += parts_ref[i]
    inverse, upper = factor(*unpack(total * (1.0 / CELLS)))
    lane = lax.broadcasted_iota(jnp.int32, (ALL, ALL), 1)
    image = jnp.where(lane < ITERS * B, inverse, 0.0) + jnp.where(lane >= B, pltpu.roll(inverse, B, 1), 0.0)
    coeffs = lax.dot_general(upper, image, NT, precision=HIGH, preferred_element_type=jnp.float32)
    for k in range(ITERS):
        here, after = slice(k * B, (k + 1) * B), slice((k + 1) * B, (k + 2) * B)
        alpha_ref[k] = coeffs[here, here]
        beta_ref[k] = coeffs[after, here]
    copies = [
        pltpu.make_async_copy(alpha_ref, alpha_hbm, sems.at[0]),
        pltpu.make_async_copy(beta_ref, beta_hbm, sems.at[1]),
    ]
    for copy in copies:
        copy.start()
    high, middle, low = split(inverse)
    two = jnp.concatenate([high, middle], axis=1)
    three = jnp.concatenate([high, middle, low], axis=1)
    dot = lambda a, b: jnp.dot(a, b, preferred_element_type=jnp.float32)
    sub = lax.broadcasted_iota(jnp.int32, (8, LON), 0)
    for g in range(LAT // 8):
        rows = []
        for i in range(8 * g, 8 * g + 8, 2):
            a, b, c = high_ref[i // 2], middle_ref[i // 2], low_ref[i // 2]
            new = dot(three, jnp.concatenate([a, a, a], axis=0)) + dot(two, jnp.concatenate([b, b], axis=0)) + dot(high, c)
            rows += [new[:, :LON], new[:, LON:]]
        chunk = pl.ds(8 * g, 8)
        for v in range(0, ALL, 8):
            for t, tile in enumerate(swap([row[v:v + 8] for row in rows], sub)):
                q_ref[v + t, 8 * g:8 * g + 8, :] = tile
            if v % PIECE == PIECE - 8:
                block = pl.ds(v + 8 - PIECE, PIECE)
                sem = sems.at[len(copies)]
                copies.append(pltpu.make_async_copy(q_ref.at[block, chunk, :], q_hbm.at[block, chunk, :], sem))
                copies[-1].start()
    for copy in copies:
        copy.wait()


def body(start_block, sea_mask, depth_levels):
    x = start_block.reshape(B * LAT, LON)
    x, sea_mask, depth_levels = [pltpu.with_memory_space_constraint(v, pltpu.HBM) for v in (x, sea_mask, depth_levels)]
    edge = (RIM, B + 8, LON)
    anywhere = pl.BlockSpec(memory_space=pl.ANY)
    small = pltpu.VMEM((LAT, LON), jnp.int32)
    far, near, x, h = call(
        edge_rows,
        (edge, edge, (B * LAT, LON), (LAT, LON)),
        [small, small, pltpu.SemaphoreType.DMA((3,))],
        in_specs=[pl.BlockSpec(memory_space=pltpu.HBM)] * 3,
    )(x, sea_mask, depth_levels)
    far = lax.ppermute(far, ROW, [(i, ((i + 1) ^ 1) - 1) for i in range(1, 7)])
    near = lax.ppermute(near, ROW, [(i, i ^ 1) for i in range(8)])
    flat = (B + 8, FLAT)
    core, part_west, part_east = call(
        core_rows, ((LAT, B + 8, LON), flat, flat), flops=1 << 22, moved=1 << 20
    )(x, h)
    far, near, north, south, own_west, own_east = call(side_columns, (flat, flat, edge, edge, flat, flat))(
        far, near, part_west, part_east
    )
    far = lax.ppermute(far, COL, [(i, (((i + 1) ^ 1) - 1) % 32) for i in range(32)])
    near = lax.ppermute(near, COL, [(i, i ^ 1) for i in range(32)])
    wide = pltpu.VMEM((ROWS, B, LON), jnp.float32)
    thin = pltpu.VMEM((ROWS, 8, LON), jnp.float32)
    square = (ALL, ALL)
    s, own = call(
        inside, ((LAT, ALL, LON), square), [wide, wide, thin, thin, thin], flops=1 << 28, moved=1 << 23
    )(core, north, south)
    rim = (ALL - B, FLAT)
    gram, west, east = call(border, ((B, LON), rim, rim))(far, near, own_west, own_east, own)
    other = lax.ppermute(gram, ROW, [(i, i ^ 1) for i in range(8)])
    copies = call(join, ((16, B, LON),))(gram, other)[0]
    parts = lax.all_to_all(copies, ("x", "y"), 0, 0)
    copies = call(spread, ((8, B, LON),))(parts)[0]
    parts = lax.all_to_all(copies, "z", 0, 0)
    table = (ITERS, B, B)
    results = ((ALL, LAT, LON), table, table)
    return call(
        basis,
        results,
        [pltpu.VMEM(shape, jnp.float32) for shape in results]
        + [pltpu.VMEM((LAT // 2, ALL, 2 * LON), jnp.bfloat16)] * 3
        + [pltpu.SemaphoreType.DMA((2 + (LAT // 8) * (ALL // PIECE),))],
        out_specs=(anywhere,) * 3,
    )(parts, s, west, east)


def solution(mesh):
    torus = Mesh(mesh.devices.reshape(4, 2, 8, 4), ("x", "core", "z", "y"))
    in_specs = (P(None, ROW, COL), P(ROW, COL), P(ROW, COL))
    out_specs = (P(None, ROW, COL), P(), P())
    return jax.shard_map(body, mesh=torus, in_specs=in_specs, out_specs=out_specs, check_vma=False)
```

```python
import jax
import jax.numpy as jnp
from jax import lax
from jax.experimental import pallas as pl
from jax.experimental.pallas import tpu as pltpu
from jax.sharding import Mesh, PartitionSpec as P

ITERS = 3
LEVELS = 50.0
KAPPA = 1.5
CELLS = 1048576.0

B = 32
LAT = 32
LON = 128
RIM = 3
ROWS = LAT + 2 * RIM
STARTS = (0, RIM, LON - 2 * RIM, LON - RIM)
ALL = (ITERS + 1) * B
HALF = B // 2
PIECE = 64
HALVES = [(k, part) for k in range(ITERS) for part in range(2)]
HIGH = lax.Precision.HIGHEST
ROW, COL = ("x", "core"), ("z", "y")
NT = (((1,), (1,)), ((), ()))
TN = (((0,), (0,)), ((), ()))
PARAMS = pltpu.CompilerParams(vmem_limit_bytes=48 * 1024 * 1024)


def lanes_of(rows):
    return lax.broadcasted_iota(jnp.int32, (rows, LON), 1)


def call(kernel, outs, scratch=(), flops=0, moved=0, **specs):
    return pl.pallas_call(
        kernel,
        **specs,
        out_shape=tuple(jax.ShapeDtypeStruct(s, jnp.float32) for s in outs),
        scratch_shapes=list(scratch),
        compiler_params=PARAMS,
        cost_estimate=pl.CostEstimate(flops=flops, bytes_accessed=moved, transcendentals=0),
    )


def edge_rows(x_hbm, mask_hbm, depth_hbm, far_ref, near_ref, x_ref, h_ref, mask_ref, depth_ref, sems):
    pairs = ((x_hbm, x_ref), (mask_hbm, mask_ref), (depth_hbm, depth_ref))
    copies = [pltpu.make_async_copy(a, b, sems.at[i]) for i, (a, b) in enumerate(pairs)]
    for copy in copies:
        copy.start()
    for copy in copies[1:]:
        copy.wait()
    h_ref[...] = mask_ref[...].astype(jnp.float32) * depth_ref[...].astype(jnp.float32) / LEVELS
    copies[0].wait()
    odd = lax.axis_index("core") == 1
    for i in range(RIM):
        top = masked_row(i, x_ref, h_ref)
        bottom = masked_row(LAT - RIM + i, x_ref, h_ref)
        near_ref[i] = jnp.where(odd, top, bottom)
        far_ref[i] = jnp.where(odd, bottom, top)


def masked_row(lat, x_ref, h_ref):
    depth = h_ref[pl.ds(lat, 1), :]
    row = jnp.where(depth > 0.0, x_ref[pl.ds(lat, B, stride=LAT), :], 0.0)
    return jnp.concatenate([row, jnp.broadcast_to(depth, (8, LON))], axis=0)


def pack_sides(row, r, packed):
    lane = lanes_of(B + 8)
    here = (lane >= RIM * r) & (lane < RIM * r + RIM)
    return [jnp.where(here, pltpu.roll(row, (RIM * r - start) % LON, 1), p) for p, start in zip(packed, STARTS)]


def core_rows(x_ref, h_ref, core_ref, packed_ref):
    packed = [jnp.zeros((B + 8, LON), jnp.float32)] * len(STARTS)
    for i in range(LAT):
        row = masked_row(i, x_ref, h_ref)
        core_ref[i] = row
        packed = pack_sides(row, i + RIM, packed)
    for k, value in enumerate(packed):
        packed_ref[k] = value


def side_columns(far_ref, near_ref, part_ref, far_out, near_out, north_ref, south_ref, packed_ref):
    odd = lax.axis_index("core") == 1
    packed = [part_ref[k] for k in range(len(STARTS))]
    for i in range(RIM):
        north = jnp.where(odd, near_ref[i], far_ref[i])
        south = jnp.where(odd, far_ref[i], near_ref[i])
        north_ref[i] = north
        south_ref[i] = south
        packed = pack_sides(north, i, packed)
        packed = pack_sides(south, i + RIM + LAT, packed)
    for k, value in enumerate(packed):
        packed_ref[k] = value
    odd = lax.axis_index("y") % 2 == 1
    near_out[...] = jnp.where(odd, packed[0], packed[3])
    far_out[...] = jnp.where(odd, packed[3], packed[0])


def split(value):
    high = value.astype(jnp.bfloat16)
    rest = value - high.astype(jnp.float32)
    middle = rest.astype(jnp.bfloat16)
    low = (rest - middle.astype(jnp.float32)).astype(jnp.bfloat16)
    return high, middle, low


def four(field):
    return jnp.concatenate([field] * (B // 8), axis=0)


def outer(left, right):
    return lax.dot_general(left, right, NT, preferred_element_type=jnp.float32)


def products(value):
    high, middle, low = split(value)
    both = outer(high, jnp.concatenate([high, middle], axis=0))
    return both[:, :ALL] + outer(middle, middle), both[:, ALL:] + outer(high, low)


def inside(core_ref, north_ref, south_ref, s_ref, own_ref, k1_ref, k2_ref, down_ref, right_ref, centre_ref):
    def base(r):
        if r < RIM:
            return north_ref[r]
        return core_ref[r - RIM] if r < RIM + LAT else south_ref[r - RIM - LAT]

    for r in range(ROWS - 1):
        h = base(r)[B:]
        down_ref[r] = KAPPA * jnp.minimum(h, base(r + 1)[B:])
        right_ref[r] = KAPPA * jnp.minimum(h, pltpu.roll(h, LON - 1, 1))
        centre_ref[r] = jnp.where(h > 0.0, 0.0, -1.0)
    levels = (
        (lambda r: base(r)[:B], k1_ref),
        (lambda r: k1_ref[r], k2_ref),
        (lambda r: k2_ref[r], None),
    )
    for step, (source, target) in enumerate(levels):
        first, last = step + 1, ROWS - 2 - step
        v, after = source(first - 1), source(first)
        flux = four(down_ref[first - 1]) * (v - after)
        for r in range(first, last + 1):
            v, after = after, source(r + 1)
            down = four(down_ref[r]) * (v - after)
            right = four(right_ref[r]) * (v - pltpu.roll(v, LON - 1, 1))
            new = four(centre_ref[r]) * v + ((down - flux) + (right - pltpu.roll(right, 1, 1)))
            flux = down
            if target is not None:
                target[r] = new
            if RIM <= r < RIM + LAT:
                s_ref[r - RIM, (step + 1) * B:(step + 2) * B, :] = new
    lane = lanes_of(ALL)
    clean = (lane >= RIM) & (lane < LON - RIM)
    even = half = jnp.zeros((ALL, ALL), jnp.float32)
    for i in range(0, LAT, 2):
        rows = []
        for j in (i, i + 1):
            s_ref[j, :B, :] = core_ref[j, :B]
            rows.append(jnp.where(clean, s_ref[j], 0.0))
        one, two = products(jnp.concatenate(rows, axis=1))
        even += one
        half += two
    own_ref[...] = even + half + half.T


def border(far_ref, near_ref, packed_ref, own_ref, gram_ref, west_ref, east_ref):
    odd = lax.axis_index("y") % 2 == 1
    near, far = near_ref[...], far_ref[...]
    lane = lanes_of(B)
    line = (lane * 21846) >> 16
    place = lane - RIM * line
    first, last = place == 0, place == RIM - 1
    kept = (line[:1] >= RIM) & (line[:1] < RIM + LAT)
    move = lambda value, by: pltpu.roll(value, by % LON, 1)

    def rightward(values, i):
        inner = move(values[i], -1)
        return jnp.where(last[:inner.shape[0]], move(values[i + 1], RIM - 1), inner) if i < 2 else inner

    def leftward(values, i):
        inner = move(values[i], 1)
        return jnp.where(first[:inner.shape[0]], move(values[i - 1], 1 - RIM), inner) if i > 0 else inner

    fields = []
    for chain, out_ref in (
        ((jnp.where(odd, near, far), packed_ref[0], packed_ref[1]), west_ref),
        ((packed_ref[2], packed_ref[3], jnp.where(odd, far, near)), east_ref),
    ):
        h = [part[B:] for part in chain]
        south = [KAPPA * jnp.minimum(h[i], move(h[i], -RIM)) for i in range(3)]
        right = [KAPPA * jnp.minimum(h[i], rightward(h, i)) for i in range(3)]
        right[2] = jnp.where(last[:8], 0.0, right[2])
        left = [leftward(right, i) for i in range(3)]
        left[0] = jnp.where(first[:8], 0.0, left[0])
        north = [four(move(value, RIM)) for value in south]
        south, right, left = [[four(value) for value in values] for values in (south, right, left)]
        centre = [four(jnp.where(value > 0.0, 0.0, -1.0)) for value in h]
        v = [part[:B] for part in chain]
        found = [v[1]]
        for step in range(ITERS):
            v = [
                centre[i] * v[i]
                + (
                    (south[i] * (v[i] - move(v[i], -RIM)) + north[i] * (v[i] - move(v[i], RIM)))
                    + (right[i] * (v[i] - rightward(v, i)) + left[i] * (v[i] - leftward(v, i)))
                )
                for i in range(3)
            ]
            found.append(v[1])
        out_ref[...] = jnp.concatenate(found[1:], axis=0)
        fields.append(jnp.where(kept, jnp.concatenate(found, axis=0), 0.0))
    high, middle, low = split(jnp.concatenate(fields, axis=1))
    both = jnp.concatenate([high, middle], axis=0)
    both = outer(both, both)
    large, small = both[:ALL, :ALL], both[:ALL, ALL:] + both[ALL:, :ALL]
    gram = (own_ref[...] + large) + (small + (both[ALL:, ALL:] + (outer(high, low) + outer(low, high))))
    row = lax.broadcasted_iota(jnp.int32, (B, LON), 0)
    lane = lax.broadcasted_iota(jnp.int32, (B, LON), 1)
    packed = diagonal = jnp.zeros((B, LON), jnp.float32)
    for k in range(ITERS + 1):
        own = gram[k * B:(k + 1) * B]
        after = pltpu.roll(own, LON - B, 1)
        here = (lane >= k * B) & (lane < (k + 1) * B)
        packed = jnp.where(here, jnp.where(lane - k * B >= row, own, after), packed)
        diagonal = jnp.where(here & (lane - k * B == row), after, diagonal)
    line = jnp.sum(diagonal, axis=0, keepdims=True)
    for n, (k, part) in enumerate(HALVES):
        there = (row == B - 1 - n) & (lane >= ITERS * B) & (lane < ITERS * B + HALF)
        packed = jnp.where(there, pltpu.roll(line, (ITERS * B - k * B - part * HALF) % LON, 1), packed)
    gram_ref[...] = packed


def spread(parts_ref, out_ref):
    total = parts_ref[0]
    for i in range(1, parts_ref.shape[0]):
        total += parts_ref[i]
    for i in range(out_ref.shape[0]):
        out_ref[i] = total


def join(own_ref, other_ref, out_ref):
    total = own_ref[...] + other_ref[...]
    for i in range(out_ref.shape[0]):
        out_ref[i] = total


def unpack(total):
    row = lax.broadcasted_iota(jnp.int32, (B, LON), 0)
    lane = lax.broadcasted_iota(jnp.int32, (B, LON), 1)
    block, place = lane >> 5, lane & (B - 1)
    turned = jnp.concatenate([jnp.where(block == k, total, 0.0) for k in range(ITERS + 1)], axis=0).T
    mirror = (turned[:B] + turned[B:2 * B]) + (turned[2 * B:3 * B] + turned[3 * B:])
    even = jnp.where(place >= row, total, mirror)
    odd = jnp.where(place < row, total, mirror)
    line = jnp.zeros((1, LON), jnp.float32)
    for n, (k, part) in enumerate(HALVES):
        target = k * B + part * HALF
        moved = pltpu.roll(total[B - 1 - n:B - n], (target - ITERS * B) % LON, 1)
        line = jnp.where((lane[:1] >= target) & (lane[:1] < target + HALF), moved, line)
    odd = jnp.where(place == row, line, odd)
    move = lambda field, k: pltpu.roll(field, (k * B) % LON, 1)
    pick = lambda a, b, c, d: jnp.where(block == 0, a, jnp.where(block == 1, b, jnp.where(block == 2, c, d)))
    even_on, even_back, odd_on, odd_back = move(even, 1), move(even, -1), move(odd, 1), move(odd, -1)
    rows = [
        pick(even, odd_on, even_on, move(odd, 2)),
        pick(odd, even, odd_on, even_on),
        pick(even_back, odd, even, odd_on),
        pick(odd_back, even_back, odd, even),
    ]
    return even, jnp.concatenate(rows, axis=0)


def reciprocal(value):
    return 1.0 / value


def factor(first, gram):
    groups = ALL // 8
    lane = lax.broadcasted_iota(jnp.int32, (8, ALL), 1)
    sub = lax.broadcasted_iota(jnp.int32, (8, ALL), 0)
    full = lambda value: jnp.broadcast_to(value, (8, ALL))
    line = lambda value, t: full(value[t:t + 1])
    tree = lambda p: ((p[0] + p[1]) + (p[2] + p[3])) + ((p[4] + p[5]) + (p[6] + p[7]))
    weigh = lambda p, q: tree([p[t] * q[t] for t in range(8)])
    work = [gram[8 * g:8 * g + 8] for g in range(groups)]
    columns = lambda k, g: [full(work[k][:, 8 * g + t:8 * g + t + 1]) for t in range(8)] if k < groups else None
    diagonal = sum(jnp.where(lane == sub + 8 * g, work[g], 0.0) for g in range(groups))
    guess = full(reciprocal(jnp.sum(diagonal, axis=0, keepdims=True)))
    uppers, inverses = [], []
    own, after = [[full(first[8 * k:8 * k + 8, t:t + 1]) for t in range(8)] for k in range(2)]
    for g in range(groups):
        later, coming = columns(g + 2, g), columns(g + 1, g + 1)
        a = work[g]
        b = jnp.where(lane == sub + 8 * g, 1.0, jnp.where(lane < 8 * g, work[g], 0.0))
        recip, ratio, pivot = [None] * 8, {}, []
        for t in range(8):
            pivot.append(line(own[t], t))
            if recip[t] is None:
                recip[t] = reciprocal(pivot[t])
            if t % 2 == 0 and g > 0:
                unit = full(guess[:, 8 * g + t:8 * g + t + 1])
                near, cross = pivot[t] * unit, line(own[t], t + 1)
                recip[t + 1] = near * reciprocal(near * line(own[t + 1], t + 1) - cross * (cross * unit))
            column = jnp.where(sub > t, own[t] * recip[t], 0.0)
            for s in range(t + 1, 8):
                ratio[s, t] = line(column, s)
                own[s] = own[s] - column * line(own[t], s)
            if t < 7:
                a = a - column * line(a, t)
                b = b - column * line(b, t)
                for ahead in (after, later):
                    for s in range(t + 1, 8) if ahead else ():
                        ahead[s] = ahead[s] - ratio[s, t] * ahead[t]
        pivots = inverted = jnp.zeros((8, ALL), jnp.float32)
        for t in range(8):
            pivots = jnp.where(sub == t, pivot[t], pivots)
            inverted = jnp.where(sub == t, recip[t], inverted)
        scale = lax.rsqrt(pivots)
        uppers.append(jnp.where(lane >= sub + 8 * g, a * scale, 0.0))
        inverses.append(b * scale)
        if g + 1 == groups:
            break
        c = jnp.where(lane < 8 * g + 8, b, a) * inverted
        c = [line(c, t) for t in range(8)]
        scaled = [after[t] * recip[t] for t in range(8)]
        own = [coming[u] - weigh(after, [line(scaled[t], u) for t in range(8)]) for u in range(8)]
        block = (lane >= 8 * g) & (lane < 8 * g + 8)
        for k, ahead in ((g + 1, after), (g + 2, later)):
            if ahead:
                work[k] = jnp.where(block, 0.0, work[k]) - weigh(ahead, c)
        after = columns(g + 2, g + 1)
        for t in range(7, 0, -1):
            for s in range(t):
                c[s] = c[s] - ratio[t, s] * c[t]
        panel = 8 * g // B
        for k in range(g + 3, min((panel + 2) * B // 8, groups)):
            work[k] = jnp.where(block, 0.0, work[k]) - weigh(columns(k, g), c)
        if (8 * g + 8) % B == 0 and (panel + 2) * B < ALL:
            top = jnp.concatenate(uppers[-B // 8:], axis=0)
            wide = lax.broadcasted_iota(jnp.int32, (B, ALL), 1) < (panel + 1) * B
            rest = jnp.where(wide, jnp.concatenate(inverses[-B // 8:], axis=0), top)
            change = lax.dot_general(top, rest, TN, precision=HIGH, preferred_element_type=jnp.float32)
            block = (lane >= panel * B) & (lane < (panel + 1) * B)
            for k in range((panel + 2) * B // 8, groups):
                work[k] = jnp.where(block, 0.0, work[k]) - change[8 * k:8 * k + 8]
    return jnp.concatenate(inverses, axis=0), jnp.concatenate(uppers, axis=0)


def swap(rows, sub):
    for k in (4, 2, 1):
        low, new = (sub & k) == 0, list(rows)
        for i in range(8):
            if not i & k:
                new[i] = jnp.where(low, rows[i], pltpu.roll(rows[i | k], k, 0))
                new[i | k] = jnp.where(low, pltpu.roll(rows[i], 8 - k, 0), rows[i | k])
        rows = new
    return rows


def whole_row(i, s_ref, west_ref, east_ref):
    lane = lanes_of(ALL - B)
    row = s_ref[i, B:, :]
    for ref, target in ((west_ref, 0), (east_ref, LON - RIM)):
        side = pltpu.roll(ref[...], (target - RIM * (i + RIM)) % LON, 1)
        row = jnp.where((lane >= target) & (lane < target + RIM), side, row)
    return jnp.concatenate([s_ref[i, :B, :], row], axis=0)


def basis(parts_ref, s_ref, west_ref, east_ref, q_hbm, alpha_hbm, beta_hbm,
          q_ref, alpha_ref, beta_ref, high_ref, middle_ref, low_ref, sems):
    for i in range(0, LAT, 2):
        pair = [whole_row(j, s_ref, west_ref, east_ref) for j in (i, i + 1)]
        a, b, c = split(jnp.concatenate(pair, axis=1))
        high_ref[i // 2] = a
        middle_ref[i // 2] = b
        low_ref[i // 2] = c
    total = parts_ref[0]
    for i in range(1, parts_ref.shape[0]):
        total += parts_ref[i]
    inverse, upper = factor(*unpack(total * (1.0 / CELLS)))
    lane = lax.broadcasted_iota(jnp.int32, (ALL, ALL), 1)
    image = jnp.where(lane < ITERS * B, inverse, 0.0) + jnp.where(lane >= B, pltpu.roll(inverse, B, 1), 0.0)
    coeffs = lax.dot_general(upper, image, NT, precision=HIGH, preferred_element_type=jnp.float32)
    for k in range(ITERS):
        here, after = slice(k * B, (k + 1) * B), slice((k + 1) * B, (k + 2) * B)
        alpha_ref[k] = coeffs[here, here]
        beta_ref[k] = coeffs[after, here]
    copies = [
        pltpu.make_async_copy(alpha_ref, alpha_hbm, sems.at[0]),
        pltpu.make_async_copy(beta_ref, beta_hbm, sems.at[1]),
    ]
    for copy in copies:
        copy.start()
    high, middle, low = split(inverse)
    two = jnp.concatenate([high, middle], axis=1)
    three = jnp.concatenate([high, middle, low], axis=1)
    dot = lambda a, b: jnp.dot(a, b, preferred_element_type=jnp.float32)
    sub = lax.broadcasted_iota(jnp.int32, (8, LON), 0)
    for g in range(LAT // 8):
        rows = []
        for i in range(8 * g, 8 * g + 8, 2):
            a, b, c = high_ref[i // 2], middle_ref[i // 2], low_ref[i // 2]
            new = dot(three, jnp.concatenate([a, a, a], axis=0)) + dot(two, jnp.concatenate([b, b], axis=0)) + dot(high, c)
            rows += [new[:, :LON], new[:, LON:]]
        chunk = pl.ds(8 * g, 8)
        for v in range(0, ALL, 8):
            for t, tile in enumerate(swap([row[v:v + 8] for row in rows], sub)):
                q_ref[v + t, 8 * g:8 * g + 8, :] = tile
            if v % PIECE == PIECE - 8:
                block = pl.ds(v + 8 - PIECE, PIECE)
                sem = sems.at[len(copies)]
                copies.append(pltpu.make_async_copy(q_ref.at[block, chunk, :], q_hbm.at[block, chunk, :], sem))
                copies[-1].start()
    for copy in copies:
        copy.wait()


def body(start_block, sea_mask, depth_levels):
    x = start_block.reshape(B * LAT, LON)
    x, sea_mask, depth_levels = [pltpu.with_memory_space_constraint(v, pltpu.HBM) for v in (x, sea_mask, depth_levels)]
    edge = (RIM, B + 8, LON)
    anywhere = pl.BlockSpec(memory_space=pl.ANY)
    small = pltpu.VMEM((LAT, LON), jnp.int32)
    far, near, x, h = call(
        edge_rows,
        (edge, edge, (B * LAT, LON), (LAT, LON)),
        [small, small, pltpu.SemaphoreType.DMA((3,))],
        in_specs=[pl.BlockSpec(memory_space=pltpu.HBM)] * 3,
    )(x, sea_mask, depth_levels)
    far = lax.ppermute(far, ROW, [(i, ((i + 1) ^ 1) - 1) for i in range(1, 7)])
    near = lax.ppermute(near, ROW, [(i, i ^ 1) for i in range(8)])
    flat = (B + 8, LON)
    packs = (len(STARTS), B + 8, LON)
    core, part = call(core_rows, ((LAT, B + 8, LON), packs), flops=1 << 22, moved=1 << 20)(x, h)
    far, near, north, south, packed = call(side_columns, (flat, flat, edge, edge, packs))(far, near, part)
    far = lax.ppermute(far, COL, [(i, (((i + 1) ^ 1) - 1) % 32) for i in range(32)])
    near = lax.ppermute(near, COL, [(i, i ^ 1) for i in range(32)])
    wide = pltpu.VMEM((ROWS, B, LON), jnp.float32)
    thin = pltpu.VMEM((ROWS, 8, LON), jnp.float32)
    square = (ALL, ALL)
    s, own = call(
        inside, ((LAT, ALL, LON), square), [wide, wide, thin, thin, thin], flops=1 << 28, moved=1 << 23
    )(core, north, south)
    rim = (ALL - B, LON)
    gram, west, east = call(border, ((B, LON), rim, rim))(far, near, packed, own)
    other = lax.ppermute(gram, ROW, [(i, i ^ 1) for i in range(8)])
    copies = call(join, ((16, B, LON),))(gram, other)[0]
    parts = lax.all_to_all(copies, ("x", "y"), 0, 0)
    copies = call(spread, ((8, B, LON),))(parts)[0]
    parts = lax.all_to_all(copies, "z", 0, 0)
    table = (ITERS, B, B)
    results = ((ALL, LAT, LON), table, table)
    return call(
        basis,
        results,
        [pltpu.VMEM(shape, jnp.float32) for shape in results]
        + [pltpu.VMEM((LAT // 2, ALL, 2 * LON), jnp.bfloat16)] * 3
        + [pltpu.SemaphoreType.DMA((2 + (LAT // 8) * (ALL // PIECE),))],
        out_specs=(anywhere,) * 3,
    )(parts, s, west, east)


def solution(mesh):
    torus = Mesh(mesh.devices.reshape(4, 2, 8, 4), ("x", "core", "z", "y"))
    in_specs = (P(None, ROW, COL), P(ROW, COL), P(ROW, COL))
    out_specs = (P(None, ROW, COL), P(), P())
    return jax.shard_map(body, mesh=torus, in_specs=in_specs, out_specs=out_specs, check_vma=False)
```

```python
import jax
import jax.numpy as jnp
from jax import lax
from jax.experimental import pallas as pl
from jax.experimental.pallas import tpu as pltpu
from jax.sharding import Mesh, PartitionSpec as P

ITERS = 3
LEVELS = 50.0
KAPPA = 1.5
CELLS = 1048576.0

B = 32
LAT = 32
LON = 128
RIM = 3
ROWS = LAT + 2 * RIM
STARTS = (0, RIM, LON - 2 * RIM, LON - RIM)
ALL = (ITERS + 1) * B
HALF = B // 2
PIECE = 64
HALVES = [(k, part) for k in range(ITERS) for part in range(2)]
HIGH = lax.Precision.HIGHEST
ROW, COL = ("x", "core"), ("z", "y")
NT = (((1,), (1,)), ((), ()))
TN = (((0,), (0,)), ((), ()))
PARAMS = pltpu.CompilerParams(vmem_limit_bytes=48 * 1024 * 1024)


def lanes_of(rows):
    return lax.broadcasted_iota(jnp.int32, (rows, LON), 1)


def call(kernel, outs, scratch=(), flops=0, moved=0, **specs):
    return pl.pallas_call(
        kernel,
        **specs,
        out_shape=tuple(jax.ShapeDtypeStruct(s, jnp.float32) for s in outs),
        scratch_shapes=list(scratch),
        compiler_params=PARAMS,
        cost_estimate=pl.CostEstimate(flops=flops, bytes_accessed=moved, transcendentals=0),
    )


def edge_rows(x_hbm, mask_hbm, depth_hbm, far_ref, near_ref, x_ref, h_ref, mask_ref, depth_ref, sems):
    pairs = ((x_hbm, x_ref), (mask_hbm, mask_ref), (depth_hbm, depth_ref))
    copies = [pltpu.make_async_copy(a, b, sems.at[i]) for i, (a, b) in enumerate(pairs)]
    for copy in copies:
        copy.start()
    for copy in copies[1:]:
        copy.wait()
    h_ref[...] = mask_ref[...].astype(jnp.float32) * depth_ref[...].astype(jnp.float32) / LEVELS
    copies[0].wait()
    odd = lax.axis_index("core") == 1
    for i in range(RIM):
        top = masked_row(i, x_ref, h_ref)
        bottom = masked_row(LAT - RIM + i, x_ref, h_ref)
        near_ref[i] = jnp.where(odd, top, bottom)
        far_ref[i] = jnp.where(odd, bottom, top)


def masked_row(lat, x_ref, h_ref):
    depth = h_ref[pl.ds(lat, 1), :]
    row = jnp.where(depth > 0.0, x_ref[pl.ds(lat, B, stride=LAT), :], 0.0)
    return jnp.concatenate([row, jnp.broadcast_to(depth, (8, LON))], axis=0)


def pack_sides(row, r, packed):
    lane = lanes_of(B + 8)
    here = (lane >= RIM * r) & (lane < RIM * r + RIM)
    return [jnp.where(here, pltpu.roll(row, (RIM * r - start) % LON, 1), p) for p, start in zip(packed, STARTS)]


def core_rows(x_ref, h_ref, core_ref, packed_ref):
    packed = [jnp.zeros((B + 8, LON), jnp.float32)] * len(STARTS)
    for i in range(LAT):
        row = masked_row(i, x_ref, h_ref)
        core_ref[i] = row
        packed = pack_sides(row, i + RIM, packed)
    for k, value in enumerate(packed):
        packed_ref[k] = value


def side_columns(far_ref, near_ref, part_ref, far_out, near_out, north_ref, south_ref, packed_ref):
    odd = lax.axis_index("core") == 1
    packed = [part_ref[k] for k in range(len(STARTS))]
    for i in range(RIM):
        north = jnp.where(odd, near_ref[i], far_ref[i])
        south = jnp.where(odd, far_ref[i], near_ref[i])
        north_ref[i] = north
        south_ref[i] = south
        packed = pack_sides(north, i, packed)
        packed = pack_sides(south, i + RIM + LAT, packed)
    for k, value in enumerate(packed):
        packed_ref[k] = value
    odd = lax.axis_index("y") % 2 == 1
    near_out[...] = jnp.where(odd, packed[0], packed[3])
    far_out[...] = jnp.where(odd, packed[3], packed[0])


def split(value):
    high = value.astype(jnp.bfloat16)
    rest = value - high.astype(jnp.float32)
    middle = rest.astype(jnp.bfloat16)
    low = (rest - middle.astype(jnp.float32)).astype(jnp.bfloat16)
    return high, middle, low


def four(field):
    return jnp.concatenate([field] * (B // 8), axis=0)


def outer(left, right):
    return lax.dot_general(left, right, NT, preferred_element_type=jnp.float32)


def products(value):
    high, middle, low = split(value)
    both = outer(high, jnp.concatenate([high, middle], axis=0))
    return both[:, :ALL] + outer(middle, middle), both[:, ALL:] + outer(high, low)


def inside(core_ref, north_ref, south_ref, s_ref, own_ref, k1_ref, k2_ref, down_ref, right_ref, centre_ref):
    def base(r):
        if r < RIM:
            return north_ref[r]
        return core_ref[r - RIM] if r < RIM + LAT else south_ref[r - RIM - LAT]

    for r in range(ROWS - 1):
        h = base(r)[B:]
        down_ref[r] = KAPPA * jnp.minimum(h, base(r + 1)[B:])
        right_ref[r] = KAPPA * jnp.minimum(h, pltpu.roll(h, LON - 1, 1))
        centre_ref[r] = jnp.where(h > 0.0, 0.0, -1.0)
    levels = (
        (lambda r: base(r)[:B], k1_ref),
        (lambda r: k1_ref[r], k2_ref),
        (lambda r: k2_ref[r], None),
    )
    for step, (source, target) in enumerate(levels):
        first, last = step + 1, ROWS - 2 - step
        v, after = source(first - 1), source(first)
        flux = four(down_ref[first - 1]) * (v - after)
        for r in range(first, last + 1):
            v, after = after, source(r + 1)
            down = four(down_ref[r]) * (v - after)
            right = four(right_ref[r]) * (v - pltpu.roll(v, LON - 1, 1))
            new = four(centre_ref[r]) * v + ((down - flux) + (right - pltpu.roll(right, 1, 1)))
            flux = down
            if target is not None:
                target[r] = new
            if RIM <= r < RIM + LAT:
                s_ref[r - RIM, (step + 1) * B:(step + 2) * B, :] = new
    lane = lanes_of(ALL)
    clean = (lane >= RIM) & (lane < LON - RIM)
    even = half = jnp.zeros((ALL, ALL), jnp.float32)
    for i in range(0, LAT, 2):
        rows = []
        for j in (i, i + 1):
            s_ref[j, :B, :] = core_ref[j, :B]
            rows.append(jnp.where(clean, s_ref[j], 0.0))
        one, two = products(jnp.concatenate(rows, axis=1))
        even += one
        half += two
    own_ref[...] = even + half + half.T


def border(far_ref, near_ref, packed_ref, own_ref, gram_ref, west_ref, east_ref):
    odd = lax.axis_index("y") % 2 == 1
    near, far = near_ref[...], far_ref[...]
    lane = lanes_of(B)
    line = (lane * 21846) >> 16
    place = lane - RIM * line
    first, last = place == 0, place == RIM - 1
    kept = (line[:1] >= RIM) & (line[:1] < RIM + LAT)
    move = lambda value, by: pltpu.roll(value, by % LON, 1)

    def rightward(values, i):
        inner = move(values[i], -1)
        return jnp.where(last[:inner.shape[0]], move(values[i + 1], RIM - 1), inner) if i < 2 else inner

    def leftward(values, i):
        inner = move(values[i], 1)
        return jnp.where(first[:inner.shape[0]], move(values[i - 1], 1 - RIM), inner) if i > 0 else inner

    fields = []
    for chain, out_ref in (
        ((jnp.where(odd, near, far), packed_ref[0], packed_ref[1]), west_ref),
        ((packed_ref[2], packed_ref[3], jnp.where(odd, far, near)), east_ref),
    ):
        h = [part[B:] for part in chain]
        south = [KAPPA * jnp.minimum(h[i], move(h[i], -RIM)) for i in range(3)]
        right = [KAPPA * jnp.minimum(h[i], rightward(h, i)) for i in range(3)]
        right[2] = jnp.where(last[:8], 0.0, right[2])
        left = [leftward(right, i) for i in range(3)]
        left[0] = jnp.where(first[:8], 0.0, left[0])
        north = [four(move(value, RIM)) for value in south]
        south, right, left = [[four(value) for value in values] for values in (south, right, left)]
        centre = [four(jnp.where(value > 0.0, 0.0, -1.0)) for value in h]
        v = [part[:B] for part in chain]
        found = [v[1]]
        for step in range(ITERS):
            v = [
                centre[i] * v[i]
                + (
                    (south[i] * (v[i] - move(v[i], -RIM)) + north[i] * (v[i] - move(v[i], RIM)))
                    + (right[i] * (v[i] - rightward(v, i)) + left[i] * (v[i] - leftward(v, i)))
                )
                for i in range(3)
            ]
            found.append(v[1])
        out_ref[...] = jnp.concatenate(found[1:], axis=0)
        fields.append(jnp.where(kept, jnp.concatenate(found, axis=0), 0.0))
    high, middle, low = split(jnp.concatenate(fields, axis=1))
    both = jnp.concatenate([high, middle], axis=0)
    both = outer(both, both)
    large, small = both[:ALL, :ALL], both[:ALL, ALL:] + both[ALL:, :ALL]
    gram = (own_ref[...] + large) + (small + (both[ALL:, ALL:] + (outer(high, low) + outer(low, high))))
    row = lax.broadcasted_iota(jnp.int32, (B, LON), 0)
    lane = lax.broadcasted_iota(jnp.int32, (B, LON), 1)
    packed = diagonal = jnp.zeros((B, LON), jnp.float32)
    for k in range(ITERS + 1):
        own = gram[k * B:(k + 1) * B]
        after = pltpu.roll(own, LON - B, 1)
        here = (lane >= k * B) & (lane < (k + 1) * B)
        packed = jnp.where(here, jnp.where(lane - k * B >= row, own, after), packed)
        diagonal = jnp.where(here & (lane - k * B == row), after, diagonal)
    line = jnp.sum(diagonal, axis=0, keepdims=True)
    for n, (k, part) in enumerate(HALVES):
        there = (row == B - 1 - n) & (lane >= ITERS * B) & (lane < ITERS * B + HALF)
        packed = jnp.where(there, pltpu.roll(line, (ITERS * B - k * B - part * HALF) % LON, 1), packed)
    gram_ref[...] = packed


def spread(parts_ref, out_ref):
    total = parts_ref[0]
    for i in range(1, parts_ref.shape[0]):
        total += parts_ref[i]
    for i in range(out_ref.shape[0]):
        out_ref[i] = total


def join(own_ref, other_ref, out_ref):
    total = own_ref[...] + other_ref[...]
    for i in range(out_ref.shape[0]):
        out_ref[i] = total


def unpack(total):
    row = lax.broadcasted_iota(jnp.int32, (B, LON), 0)
    lane = lax.broadcasted_iota(jnp.int32, (B, LON), 1)
    block, place = lane >> 5, lane & (B - 1)
    turned = jnp.concatenate([jnp.where(block == k, total, 0.0) for k in range(ITERS + 1)], axis=0).T
    mirror = (turned[:B] + turned[B:2 * B]) + (turned[2 * B:3 * B] + turned[3 * B:])
    even = jnp.where(place >= row, total, mirror)
    odd = jnp.where(place < row, total, mirror)
    line = jnp.zeros((1, LON), jnp.float32)
    for n, (k, part) in enumerate(HALVES):
        target = k * B + part * HALF
        moved = pltpu.roll(total[B - 1 - n:B - n], (target - ITERS * B) % LON, 1)
        line = jnp.where((lane[:1] >= target) & (lane[:1] < target + HALF), moved, line)
    odd = jnp.where(place == row, line, odd)
    move = lambda field, k: pltpu.roll(field, (k * B) % LON, 1)
    pick = lambda a, b, c, d: jnp.where(block == 0, a, jnp.where(block == 1, b, jnp.where(block == 2, c, d)))
    even_on, even_back, odd_on, odd_back = move(even, 1), move(even, -1), move(odd, 1), move(odd, -1)
    rows = [
        pick(even, odd_on, even_on, move(odd, 2)),
        pick(odd, even, odd_on, even_on),
        pick(even_back, odd, even, odd_on),
        pick(odd_back, even_back, odd, even),
    ]
    return even, jnp.concatenate(rows, axis=0)


def reciprocal(value):
    return 1.0 / value


def factor(first, gram):
    groups = ALL // 8
    lane = lax.broadcasted_iota(jnp.int32, (8, ALL), 1)
    sub = lax.broadcasted_iota(jnp.int32, (8, ALL), 0)
    full = lambda value: jnp.broadcast_to(value, (8, ALL))
    line = lambda value, t: full(value[t:t + 1])
    tree = lambda p: ((p[0] + p[1]) + (p[2] + p[3])) + ((p[4] + p[5]) + (p[6] + p[7]))
    weigh = lambda p, q: tree([p[t] * q[t] for t in range(8)])
    work = [gram[8 * g:8 * g + 8] for g in range(groups)]
    columns = lambda k, g: [full(work[k][:, 8 * g + t:8 * g + t + 1]) for t in range(8)] if k < groups else None
    diagonal = sum(jnp.where(lane == sub + 8 * g, work[g], 0.0) for g in range(groups))
    guess = full(reciprocal(jnp.sum(diagonal, axis=0, keepdims=True)))
    uppers, inverses = [], []
    own, after = [[full(first[8 * k:8 * k + 8, t:t + 1]) for t in range(8)] for k in range(2)]
    for g in range(groups):
        later, coming = columns(g + 2, g), columns(g + 1, g + 1)
        a = work[g]
        b = jnp.where(lane == sub + 8 * g, 1.0, jnp.where(lane < 8 * g, work[g], 0.0))
        recip, ratio, pivot = [None] * 8, {}, []
        for t in range(8):
            pivot.append(line(own[t], t))
            if recip[t] is None:
                recip[t] = reciprocal(pivot[t])
            if t % 2 == 0 and g > 0:
                unit = full(guess[:, 8 * g + t:8 * g + t + 1])
                near, cross = pivot[t] * unit, line(own[t], t + 1)
                recip[t + 1] = near * reciprocal(near * line(own[t + 1], t + 1) - cross * (cross * unit))
            column = own[t] * recip[t]
            for s in range(t + 1, 8):
                ratio[s, t] = line(column, s)
                own[s] = own[s] - column * line(own[t], s)
            if t < 7:
                column = jnp.where(sub > t, column, 0.0)
                a = a - column * line(a, t)
                b = b - column * line(b, t)
                for ahead in (after, later):
                    for s in range(t + 1, 8) if ahead else ():
                        ahead[s] = ahead[s] - ratio[s, t] * ahead[t]
        pivots = inverted = jnp.zeros((8, ALL), jnp.float32)
        for t in range(8):
            pivots = jnp.where(sub == t, pivot[t], pivots)
            inverted = jnp.where(sub == t, recip[t], inverted)
        scale = lax.rsqrt(pivots)
        uppers.append(jnp.where(lane >= sub + 8 * g, a * scale, 0.0))
        inverses.append(b * scale)
        if g + 1 == groups:
            break
        c = jnp.where(lane < 8 * g + 8, b, a) * inverted
        c = [line(c, t) for t in range(8)]
        scaled = [after[t] * recip[t] for t in range(8)]
        own = []
        for u in range(8):
            p = [after[t] * line(scaled[t], u) for t in range(8)]
            own.append((coming[u] - (((p[0] + p[1]) + (p[2] + p[3])) + (p[4] + p[5]))) - (p[6] + p[7]))
        block = (lane >= 8 * g) & (lane < 8 * g + 8)
        for k, ahead in ((g + 1, after), (g + 2, later)):
            if ahead:
                work[k] = jnp.where(block, 0.0, work[k]) - weigh(ahead, c)
        after = columns(g + 2, g + 1)
        for t in range(7, 0, -1):
            for s in range(t):
                c[s] = c[s] - ratio[t, s] * c[t]
        panel = 8 * g // B
        for k in range(g + 3, min((panel + 2) * B // 8, groups)):
            work[k] = jnp.where(block, 0.0, work[k]) - weigh(columns(k, g), c)
        if (8 * g + 8) % B == 0 and (panel + 2) * B < ALL:
            top = jnp.concatenate(uppers[-B // 8:], axis=0)
            wide = lax.broadcasted_iota(jnp.int32, (B, ALL), 1) < (panel + 1) * B
            rest = jnp.where(wide, jnp.concatenate(inverses[-B // 8:], axis=0), top)
            change = lax.dot_general(top, rest, TN, precision=HIGH, preferred_element_type=jnp.float32)
            block = (lane >= panel * B) & (lane < (panel + 1) * B)
            for k in range((panel + 2) * B // 8, groups):
                work[k] = jnp.where(block, 0.0, work[k]) - change[8 * k:8 * k + 8]
    return jnp.concatenate(inverses, axis=0), jnp.concatenate(uppers, axis=0)


def swap(rows, sub):
    for k in (4, 2, 1):
        low, new = (sub & k) == 0, list(rows)
        for i in range(8):
            if not i & k:
                new[i] = jnp.where(low, rows[i], pltpu.roll(rows[i | k], k, 0))
                new[i | k] = jnp.where(low, pltpu.roll(rows[i], 8 - k, 0), rows[i | k])
        rows = new
    return rows


def whole_row(i, s_ref, west_ref, east_ref):
    lane = lanes_of(ALL - B)
    row = s_ref[i, B:, :]
    for ref, target in ((west_ref, 0), (east_ref, LON - RIM)):
        side = pltpu.roll(ref[...], (target - RIM * (i + RIM)) % LON, 1)
        row = jnp.where((lane >= target) & (lane < target + RIM), side, row)
    return jnp.concatenate([s_ref[i, :B, :], row], axis=0)


def basis(parts_ref, s_ref, west_ref, east_ref, q_hbm, alpha_hbm, beta_hbm,
          q_ref, alpha_ref, beta_ref, high_ref, middle_ref, low_ref, sems):
    for i in range(0, LAT, 2):
        pair = [whole_row(j, s_ref, west_ref, east_ref) for j in (i, i + 1)]
        a, b, c = split(jnp.concatenate(pair, axis=1))
        high_ref[i // 2] = a
        middle_ref[i // 2] = b
        low_ref[i // 2] = c
    total = parts_ref[0]
    for i in range(1, parts_ref.shape[0]):
        total += parts_ref[i]
    inverse, upper = factor(*unpack(total * (1.0 / CELLS)))
    lane = lax.broadcasted_iota(jnp.int32, (ALL, ALL), 1)
    image = jnp.where(lane < ITERS * B, inverse, 0.0) + jnp.where(lane >= B, pltpu.roll(inverse, B, 1), 0.0)
    coeffs = lax.dot_general(upper, image, NT, precision=HIGH, preferred_element_type=jnp.float32)
    for k in range(ITERS):
        here, after = slice(k * B, (k + 1) * B), slice((k + 1) * B, (k + 2) * B)
        alpha_ref[k] = coeffs[here, here]
        beta_ref[k] = coeffs[after, here]
    copies = [
        pltpu.make_async_copy(alpha_ref, alpha_hbm, sems.at[0]),
        pltpu.make_async_copy(beta_ref, beta_hbm, sems.at[1]),
    ]
    for copy in copies:
        copy.start()
    high, middle, low = split(inverse)
    two = jnp.concatenate([high, middle], axis=1)
    three = jnp.concatenate([high, middle, low], axis=1)
    dot = lambda a, b: jnp.dot(a, b, preferred_element_type=jnp.float32)
    sub = lax.broadcasted_iota(jnp.int32, (8, LON), 0)
    for g in range(LAT // 8):
        rows = []
        for i in range(8 * g, 8 * g + 8, 2):
            a, b, c = high_ref[i // 2], middle_ref[i // 2], low_ref[i // 2]
            new = dot(three, jnp.concatenate([a, a, a], axis=0)) + dot(two, jnp.concatenate([b, b], axis=0)) + dot(high, c)
            rows += [new[:, :LON], new[:, LON:]]
        chunk = pl.ds(8 * g, 8)
        for v in range(0, ALL, 8):
            for t, tile in enumerate(swap([row[v:v + 8] for row in rows], sub)):
                q_ref[v + t, 8 * g:8 * g + 8, :] = tile
            if v % PIECE == PIECE - 8:
                block = pl.ds(v + 8 - PIECE, PIECE)
                sem = sems.at[len(copies)]
                copies.append(pltpu.make_async_copy(q_ref.at[block, chunk, :], q_hbm.at[block, chunk, :], sem))
                copies[-1].start()
    for copy in copies:
        copy.wait()


def body(start_block, sea_mask, depth_levels):
    x = start_block.reshape(B * LAT, LON)
    x, sea_mask, depth_levels = [pltpu.with_memory_space_constraint(v, pltpu.HBM) for v in (x, sea_mask, depth_levels)]
    edge = (RIM, B + 8, LON)
    anywhere = pl.BlockSpec(memory_space=pl.ANY)
    small = pltpu.VMEM((LAT, LON), jnp.int32)
    far, near, x, h = call(
        edge_rows,
        (edge, edge, (B * LAT, LON), (LAT, LON)),
        [small, small, pltpu.SemaphoreType.DMA((3,))],
        in_specs=[pl.BlockSpec(memory_space=pltpu.HBM)] * 3,
    )(x, sea_mask, depth_levels)
    far = lax.ppermute(far, ROW, [(i, ((i + 1) ^ 1) - 1) for i in range(1, 7)])
    near = lax.ppermute(near, ROW, [(i, i ^ 1) for i in range(8)])
    flat = (B + 8, LON)
    packs = (len(STARTS), B + 8, LON)
    core, part = call(core_rows, ((LAT, B + 8, LON), packs), flops=1 << 22, moved=1 << 20)(x, h)
    far, near, north, south, packed = call(side_columns, (flat, flat, edge, edge, packs))(far, near, part)
    far = lax.ppermute(far, COL, [(i, (((i + 1) ^ 1) - 1) % 32) for i in range(32)])
    near = lax.ppermute(near, COL, [(i, i ^ 1) for i in range(32)])
    wide = pltpu.VMEM((ROWS, B, LON), jnp.float32)
    thin = pltpu.VMEM((ROWS, 8, LON), jnp.float32)
    square = (ALL, ALL)
    s, own = call(
        inside, ((LAT, ALL, LON), square), [wide, wide, thin, thin, thin], flops=1 << 28, moved=1 << 23
    )(core, north, south)
    rim = (ALL - B, LON)
    gram, west, east = call(border, ((B, LON), rim, rim))(far, near, packed, own)
    other = lax.ppermute(gram, ROW, [(i, i ^ 1) for i in range(8)])
    copies = call(join, ((16, B, LON),))(gram, other)[0]
    parts = lax.all_to_all(copies, ("x", "y"), 0, 0)
    copies = call(spread, ((8, B, LON),))(parts)[0]
    parts = lax.all_to_all(copies, "z", 0, 0)
    table = (ITERS, B, B)
    results = ((ALL, LAT, LON), table, table)
    return call(
        basis,
        results,
        [pltpu.VMEM(shape, jnp.float32) for shape in results]
        + [pltpu.VMEM((LAT // 2, ALL, 2 * LON), jnp.bfloat16)] * 3
        + [pltpu.SemaphoreType.DMA((2 + (LAT // 8) * (ALL // PIECE),))],
        out_specs=(anywhere,) * 3,
    )(parts, s, west, east)


def solution(mesh):
    torus = Mesh(mesh.devices.reshape(4, 2, 8, 4), ("x", "core", "z", "y"))
    in_specs = (P(None, ROW, COL), P(ROW, COL), P(ROW, COL))
    out_specs = (P(None, ROW, COL), P(), P())
    return jax.shard_map(body, mesh=torus, in_specs=in_specs, out_specs=out_specs, check_vma=False)
```

```python
import jax
import jax.numpy as jnp
from jax import lax
from jax.experimental import pallas as pl
from jax.experimental.pallas import tpu as pltpu
from jax.sharding import Mesh, PartitionSpec as P

ITERS = 3
LEVELS = 50.0
KAPPA = 1.5
CELLS = 1048576.0

B = 32
LAT = 32
LON = 128
RIM = 3
ROWS = LAT + 2 * RIM
STARTS = (0, RIM, LON - 2 * RIM, LON - RIM)
ALL = (ITERS + 1) * B
HALF = B // 2
PIECE = 64
HALVES = [(k, part) for k in range(ITERS) for part in range(2)]
HIGH = lax.Precision.HIGHEST
ROW, COL = ("x", "core"), ("z", "y")
NT = (((1,), (1,)), ((), ()))
TN = (((0,), (0,)), ((), ()))
PARAMS = pltpu.CompilerParams(vmem_limit_bytes=48 * 1024 * 1024)


def lanes_of(rows):
    return lax.broadcasted_iota(jnp.int32, (rows, LON), 1)


def call(kernel, outs, scratch=(), flops=0, moved=0, **specs):
    return pl.pallas_call(
        kernel,
        **specs,
        out_shape=tuple(jax.ShapeDtypeStruct(s, jnp.float32) for s in outs),
        scratch_shapes=list(scratch),
        compiler_params=PARAMS,
        cost_estimate=pl.CostEstimate(flops=flops, bytes_accessed=moved, transcendentals=0),
    )


def edge_rows(x_hbm, mask_hbm, depth_hbm, far_ref, near_ref, x_ref, h_ref, mask_ref, depth_ref, sems):
    pairs = ((x_hbm, x_ref), (mask_hbm, mask_ref), (depth_hbm, depth_ref))
    copies = [pltpu.make_async_copy(a, b, sems.at[i]) for i, (a, b) in enumerate(pairs)]
    for copy in copies:
        copy.start()
    for copy in copies[1:]:
        copy.wait()
    h_ref[...] = mask_ref[...].astype(jnp.float32) * depth_ref[...].astype(jnp.float32) / LEVELS
    copies[0].wait()
    odd = lax.axis_index("core") == 1
    for i in range(RIM):
        top = masked_row(i, x_ref, h_ref)
        bottom = masked_row(LAT - RIM + i, x_ref, h_ref)
        near_ref[i] = jnp.where(odd, top, bottom)
        far_ref[i] = jnp.where(odd, bottom, top)


def masked_row(lat, x_ref, h_ref):
    depth = h_ref[pl.ds(lat, 1), :]
    row = jnp.where(depth > 0.0, x_ref[pl.ds(lat, B, stride=LAT), :], 0.0)
    return jnp.concatenate([row, jnp.broadcast_to(depth, (8, LON))], axis=0)


def pack_sides(row, r, packed):
    lane = lanes_of(B + 8)
    here = (lane >= RIM * r) & (lane < RIM * r + RIM)
    return [jnp.where(here, pltpu.roll(row, (RIM * r - start) % LON, 1), p) for p, start in zip(packed, STARTS)]


def core_rows(x_ref, h_ref, core_ref, packed_ref):
    packed = [jnp.zeros((B + 8, LON), jnp.float32)] * len(STARTS)
    for i in range(LAT):
        row = masked_row(i, x_ref, h_ref)
        core_ref[i] = row
        packed = pack_sides(row, i + RIM, packed)
    for k, value in enumerate(packed):
        packed_ref[k] = value


def side_columns(far_ref, near_ref, part_ref, far_out, near_out, north_ref, south_ref, packed_ref):
    odd = lax.axis_index("core") == 1
    packed = [part_ref[k] for k in range(len(STARTS))]
    for i in range(RIM):
        north = jnp.where(odd, near_ref[i], far_ref[i])
        south = jnp.where(odd, far_ref[i], near_ref[i])
        north_ref[i] = north
        south_ref[i] = south
        packed = pack_sides(north, i, packed)
        packed = pack_sides(south, i + RIM + LAT, packed)
    for k, value in enumerate(packed):
        packed_ref[k] = value
    odd = lax.axis_index("y") % 2 == 1
    near_out[...] = jnp.where(odd, packed[0], packed[3])
    far_out[...] = jnp.where(odd, packed[3], packed[0])


def split(value):
    high = value.astype(jnp.bfloat16)
    rest = value - high.astype(jnp.float32)
    middle = rest.astype(jnp.bfloat16)
    low = (rest - middle.astype(jnp.float32)).astype(jnp.bfloat16)
    return high, middle, low


def four(field):
    return jnp.concatenate([field] * (B // 8), axis=0)


def outer(left, right):
    return lax.dot_general(left, right, NT, preferred_element_type=jnp.float32)


def products(value):
    high, middle, low = split(value)
    both = outer(high, jnp.concatenate([high, middle], axis=0))
    return both[:, :ALL] + outer(middle, middle), both[:, ALL:] + outer(high, low)


def inside(core_ref, north_ref, south_ref, s_ref, own_ref, k1_ref, k2_ref, down_ref, right_ref, centre_ref):
    def base(r):
        if r < RIM:
            return north_ref[r]
        return core_ref[r - RIM] if r < RIM + LAT else south_ref[r - RIM - LAT]

    for r in range(ROWS - 1):
        h = base(r)[B:]
        down_ref[r] = KAPPA * jnp.minimum(h, base(r + 1)[B:])
        right_ref[r] = KAPPA * jnp.minimum(h, pltpu.roll(h, LON - 1, 1))
        centre_ref[r] = jnp.where(h > 0.0, 0.0, -1.0)
    levels = (
        (lambda r: base(r)[:B], k1_ref),
        (lambda r: k1_ref[r], k2_ref),
        (lambda r: k2_ref[r], None),
    )
    for step, (source, target) in enumerate(levels):
        first, last = step + 1, ROWS - 2 - step
        v, after = source(first - 1), source(first)
        flux = four(down_ref[first - 1]) * (v - after)
        for r in range(first, last + 1):
            v, after = after, source(r + 1)
            down = four(down_ref[r]) * (v - after)
            right = four(right_ref[r]) * (v - pltpu.roll(v, LON - 1, 1))
            new = four(centre_ref[r]) * v + ((down - flux) + (right - pltpu.roll(right, 1, 1)))
            flux = down
            if target is not None:
                target[r] = new
            if RIM <= r < RIM + LAT:
                s_ref[r - RIM, (step + 1) * B:(step + 2) * B, :] = new
    lane = lanes_of(ALL)
    clean = (lane >= RIM) & (lane < LON - RIM)
    even = half = jnp.zeros((ALL, ALL), jnp.float32)
    for i in range(0, LAT, 2):
        rows = []
        for j in (i, i + 1):
            s_ref[j, :B, :] = core_ref[j, :B]
            rows.append(jnp.where(clean, s_ref[j], 0.0))
        one, two = products(jnp.concatenate(rows, axis=1))
        even += one
        half += two
    own_ref[...] = even + half + half.T


def border(far_ref, near_ref, packed_ref, own_ref, gram_ref, west_ref, east_ref):
    odd = lax.axis_index("y") % 2 == 1
    near, far = near_ref[...], far_ref[...]
    lane = lanes_of(B)
    line = (lane * 21846) >> 16
    place = lane - RIM * line
    first, last = place == 0, place == RIM - 1
    kept = (line[:1] >= RIM) & (line[:1] < RIM + LAT)
    move = lambda value, by: pltpu.roll(value, by % LON, 1)

    def rightward(values, i):
        inner = move(values[i], -1)
        return jnp.where(last[:inner.shape[0]], move(values[i + 1], RIM - 1), inner) if i < 2 else inner

    def leftward(values, i):
        inner = move(values[i], 1)
        return jnp.where(first[:inner.shape[0]], move(values[i - 1], 1 - RIM), inner) if i > 0 else inner

    fields = []
    for chain, out_ref in (
        ((jnp.where(odd, near, far), packed_ref[0], packed_ref[1]), west_ref),
        ((packed_ref[2], packed_ref[3], jnp.where(odd, far, near)), east_ref),
    ):
        h = [part[B:] for part in chain]
        south = [KAPPA * jnp.minimum(h[i], move(h[i], -RIM)) for i in range(3)]
        right = [KAPPA * jnp.minimum(h[i], rightward(h, i)) for i in range(3)]
        right[2] = jnp.where(last[:8], 0.0, right[2])
        left = [KAPPA * jnp.minimum(h[i], leftward(h, i)) for i in range(3)]
        left[0] = jnp.where(first[:8], 0.0, left[0])
        north = [four(KAPPA * jnp.minimum(value, move(value, RIM))) for value in h]
        south, right, left = [[four(value) for value in values] for values in (south, right, left)]
        centre = [four(jnp.where(value > 0.0, 0.0, -1.0)) for value in h]
        v = [part[:B] for part in chain]
        found = [v[1]]
        for step in range(ITERS):
            v = [
                centre[i] * v[i]
                + (
                    (south[i] * (v[i] - move(v[i], -RIM)) + north[i] * (v[i] - move(v[i], RIM)))
                    + (right[i] * (v[i] - rightward(v, i)) + left[i] * (v[i] - leftward(v, i)))
                )
                for i in range(3)
            ]
            found.append(v[1])
        out_ref[...] = jnp.concatenate(found[1:], axis=0)
        fields.append(jnp.where(kept, jnp.concatenate(found, axis=0), 0.0))
    high, middle, low = split(jnp.concatenate(fields, axis=1))
    both = jnp.concatenate([high, middle], axis=0)
    both = outer(both, both)
    large, small = both[:ALL, :ALL], both[:ALL, ALL:] + both[ALL:, :ALL]
    gram = (own_ref[...] + large) + (small + (both[ALL:, ALL:] + (outer(high, low) + outer(low, high))))
    row = lax.broadcasted_iota(jnp.int32, (B, LON), 0)
    lane = lax.broadcasted_iota(jnp.int32, (B, LON), 1)
    packed = diagonal = jnp.zeros((B, LON), jnp.float32)
    for k in range(ITERS + 1):
        own = gram[k * B:(k + 1) * B]
        after = pltpu.roll(own, LON - B, 1)
        here = (lane >= k * B) & (lane < (k + 1) * B)
        packed = jnp.where(here, jnp.where(lane - k * B >= row, own, after), packed)
        diagonal = jnp.where(lane - (k + 1) * B == row, own, diagonal)
    line = jnp.sum(diagonal, axis=0, keepdims=True)
    for n, (k, part) in enumerate(HALVES):
        there = (row == B - 1 - n) & (lane >= ITERS * B) & (lane < ITERS * B + HALF)
        packed = jnp.where(there, pltpu.roll(line, (ITERS * B - (k + 1) * B - part * HALF) % LON, 1), packed)
    gram_ref[...] = packed


def spread(parts_ref, out_ref):
    total = parts_ref[0]
    for i in range(1, parts_ref.shape[0]):
        total += parts_ref[i]
    for i in range(out_ref.shape[0]):
        out_ref[i] = total


def join(own_ref, other_ref, out_ref):
    total = own_ref[...] + other_ref[...]
    for i in range(out_ref.shape[0]):
        out_ref[i] = total


def unpack(total):
    row = lax.broadcasted_iota(jnp.int32, (B, LON), 0)
    lane = lax.broadcasted_iota(jnp.int32, (B, LON), 1)
    block, place = lane >> 5, lane & (B - 1)
    turned = jnp.concatenate([jnp.where(block == k, total, 0.0) for k in range(ITERS + 1)], axis=0).T
    mirror = (turned[:B] + turned[B:2 * B]) + (turned[2 * B:3 * B] + turned[3 * B:])
    even = jnp.where(place >= row, total, mirror)
    odd = jnp.where(place < row, total, mirror)
    line = jnp.zeros((1, LON), jnp.float32)
    for n, (k, part) in enumerate(HALVES):
        target = k * B + part * HALF
        moved = pltpu.roll(total[B - 1 - n:B - n], (target - ITERS * B) % LON, 1)
        line = jnp.where((lane[:1] >= target) & (lane[:1] < target + HALF), moved, line)
    odd = jnp.where(place == row, line, odd)
    move = lambda field, k: pltpu.roll(field, (k * B) % LON, 1)
    pick = lambda a, b, c, d: jnp.where(block == 0, a, jnp.where(block == 1, b, jnp.where(block == 2, c, d)))
    even_on, even_back, odd_on, odd_back = move(even, 1), move(even, -1), move(odd, 1), move(odd, -1)
    rows = [
        pick(even, odd_on, even_on, move(odd, 2)),
        pick(odd, even, odd_on, even_on),
        pick(even_back, odd, even, odd_on),
        pick(odd_back, even_back, odd, even),
    ]
    return even, jnp.concatenate(rows, axis=0)


def reciprocal(value):
    return 1.0 / value


def factor(first, gram):
    groups = ALL // 8
    lane = lax.broadcasted_iota(jnp.int32, (8, ALL), 1)
    sub = lax.broadcasted_iota(jnp.int32, (8, ALL), 0)
    full = lambda value: jnp.broadcast_to(value, (8, ALL))
    line = lambda value, t: full(value[t:t + 1])
    tree = lambda p: ((p[0] + p[1]) + (p[2] + p[3])) + ((p[4] + p[5]) + (p[6] + p[7]))
    weigh = lambda p, q: tree([p[t] * q[t] for t in range(8)])
    work = [gram[8 * g:8 * g + 8] for g in range(groups)]
    columns = lambda k, g: [full(work[k][:, 8 * g + t:8 * g + t + 1]) for t in range(8)] if k < groups else None
    diagonal = sum(jnp.where(lane == sub + 8 * g, work[g], 0.0) for g in range(groups))
    guess = full(reciprocal(jnp.sum(diagonal, axis=0, keepdims=True)))
    uppers, inverses = [], []
    own, after = [[full(first[8 * k:8 * k + 8, t:t + 1]) for t in range(8)] for k in range(2)]
    for g in range(groups):
        later, coming = columns(g + 2, g), columns(g + 1, g + 1)
        a = work[g]
        b = jnp.where(lane == sub + 8 * g, 1.0, jnp.where(lane < 8 * g, work[g], 0.0))
        recip, ratio, pivot = [None] * 8, {}, []
        for t in range(8):
            pivot.append(line(own[t], t))
            if recip[t] is None:
                recip[t] = reciprocal(pivot[t])
            if t % 2 == 0 and g > 0:
                unit = full(guess[:, 8 * g + t:8 * g + t + 1])
                near, cross = pivot[t] * unit, line(own[t], t + 1)
                recip[t + 1] = near * reciprocal(near * line(own[t + 1], t + 1) - cross * (cross * unit))
            column = jnp.where(sub > t, own[t] * recip[t], 0.0)
            for s in range(t + 1, 8):
                ratio[s, t] = line(column, s)
                own[s] = own[s] - column * line(own[t], s)
            if t < 7:
                a = a - column * line(a, t)
                b = b - column * line(b, t)
                for ahead in (after, later):
                    for s in range(t + 1, 8) if ahead else ():
                        ahead[s] = ahead[s] - ratio[s, t] * ahead[t]
        pivots = inverted = jnp.zeros((8, ALL), jnp.float32)
        for t in range(8):
            pivots = jnp.where(sub == t, pivot[t], pivots)
            inverted = jnp.where(sub == t, recip[t], inverted)
        scale = lax.rsqrt(pivots)
        uppers.append(jnp.where(lane >= sub + 8 * g, a * scale, 0.0))
        inverses.append(b * scale)
        if g + 1 == groups:
            break
        c = jnp.where(lane < 8 * g + 8, b, a) * inverted
        c = [line(c, t) for t in range(8)]
        scaled = [after[t] * recip[t] for t in range(8)]
        own = [coming[u] - weigh(after, [line(scaled[t], u) for t in range(8)]) for u in range(8)]
        block = (lane >= 8 * g) & (lane < 8 * g + 8)
        for k, ahead in ((g + 1, after), (g + 2, later)):
            if ahead:
                work[k] = jnp.where(block, 0.0, work[k]) - weigh(ahead, c)
        after = columns(g + 2, g + 1)
        for t in range(7, 0, -1):
            for s in range(t):
                c[s] = c[s] - ratio[t, s] * c[t]
        panel = 8 * g // B
        for k in range(g + 3, min((panel + 2) * B // 8, groups)):
            work[k] = jnp.where(block, 0.0, work[k]) - weigh(columns(k, g), c)
        if (8 * g + 8) % B == 0 and (panel + 2) * B < ALL:
            top = jnp.concatenate(uppers[-B // 8:], axis=0)
            wide = lax.broadcasted_iota(jnp.int32, (B, ALL), 1) < (panel + 1) * B
            rest = jnp.where(wide, jnp.concatenate(inverses[-B // 8:], axis=0), top)
            change = lax.dot_general(top, rest, TN, precision=HIGH, preferred_element_type=jnp.float32)
            block = (lane >= panel * B) & (lane < (panel + 1) * B)
            for k in range((panel + 2) * B // 8, groups):
                work[k] = jnp.where(block, 0.0, work[k]) - change[8 * k:8 * k + 8]
    return jnp.concatenate(inverses, axis=0), jnp.concatenate(uppers, axis=0)


def swap(rows, sub):
    for k in (4, 2, 1):
        low, new = (sub & k) == 0, list(rows)
        for i in range(8):
            if not i & k:
                new[i] = jnp.where(low, rows[i], pltpu.roll(rows[i | k], k, 0))
                new[i | k] = jnp.where(low, pltpu.roll(rows[i], 8 - k, 0), rows[i | k])
        rows = new
    return rows


def whole_row(i, s_ref, west_ref, east_ref):
    lane = lanes_of(ALL - B)
    row = s_ref[i, B:, :]
    for ref, target in ((west_ref, 0), (east_ref, LON - RIM)):
        side = pltpu.roll(ref[...], (target - RIM * (i + RIM)) % LON, 1)
        row = jnp.where((lane >= target) & (lane < target + RIM), side, row)
    return jnp.concatenate([s_ref[i, :B, :], row], axis=0)


def basis(parts_ref, s_ref, west_ref, east_ref, q_hbm, alpha_hbm, beta_hbm,
          q_ref, alpha_ref, beta_ref, high_ref, middle_ref, low_ref, sems):
    for i in range(0, LAT, 2):
        pair = [whole_row(j, s_ref, west_ref, east_ref) for j in (i, i + 1)]
        a, b, c = split(jnp.concatenate(pair, axis=1))
        high_ref[i // 2] = a
        middle_ref[i // 2] = b
        low_ref[i // 2] = c
    total = parts_ref[0]
    for i in range(1, parts_ref.shape[0]):
        total += parts_ref[i]
    inverse, upper = factor(*unpack(total * (1.0 / CELLS)))
    lane = lax.broadcasted_iota(jnp.int32, (ALL, ALL), 1)
    image = jnp.where(lane < ITERS * B, inverse, 0.0) + jnp.where(lane >= B, pltpu.roll(inverse, B, 1), 0.0)
    coeffs = lax.dot_general(upper, image, NT, precision=HIGH, preferred_element_type=jnp.float32)
    for k in range(ITERS):
        here, after = slice(k * B, (k + 1) * B), slice((k + 1) * B, (k + 2) * B)
        alpha_ref[k] = coeffs[here, here]
        beta_ref[k] = coeffs[after, here]
    copies = [
        pltpu.make_async_copy(alpha_ref, alpha_hbm, sems.at[0]),
        pltpu.make_async_copy(beta_ref, beta_hbm, sems.at[1]),
    ]
    for copy in copies:
        copy.start()
    high, middle, low = split(inverse)
    two = jnp.concatenate([high, middle], axis=1)
    three = jnp.concatenate([high, middle, low], axis=1)
    dot = lambda a, b: jnp.dot(a, b, preferred_element_type=jnp.float32)
    sub = lax.broadcasted_iota(jnp.int32, (8, LON), 0)
    for g in range(LAT // 8):
        rows = []
        for i in range(8 * g, 8 * g + 8, 2):
            a, b, c = high_ref[i // 2], middle_ref[i // 2], low_ref[i // 2]
            new = dot(three, jnp.concatenate([a, a, a], axis=0)) + dot(two, jnp.concatenate([b, b], axis=0)) + dot(high, c)
            rows += [new[:, :LON], new[:, LON:]]
        chunk = pl.ds(8 * g, 8)
        for v in range(0, ALL, 8):
            for t, tile in enumerate(swap([row[v:v + 8] for row in rows], sub)):
                q_ref[v + t, 8 * g:8 * g + 8, :] = tile
            if v % PIECE == PIECE - 8:
                block = pl.ds(v + 8 - PIECE, PIECE)
                sem = sems.at[len(copies)]
                copies.append(pltpu.make_async_copy(q_ref.at[block, chunk, :], q_hbm.at[block, chunk, :], sem))
                copies[-1].start()
    for copy in copies:
        copy.wait()


def body(start_block, sea_mask, depth_levels):
    x = start_block.reshape(B * LAT, LON)
    x, sea_mask, depth_levels = [pltpu.with_memory_space_constraint(v, pltpu.HBM) for v in (x, sea_mask, depth_levels)]
    edge = (RIM, B + 8, LON)
    anywhere = pl.BlockSpec(memory_space=pl.ANY)
    small = pltpu.VMEM((LAT, LON), jnp.int32)
    far, near, x, h = call(
        edge_rows,
        (edge, edge, (B * LAT, LON), (LAT, LON)),
        [small, small, pltpu.SemaphoreType.DMA((3,))],
        in_specs=[pl.BlockSpec(memory_space=pltpu.HBM)] * 3,
    )(x, sea_mask, depth_levels)
    far = lax.ppermute(far, ROW, [(i, ((i + 1) ^ 1) - 1) for i in range(1, 7)])
    near = lax.ppermute(near, ROW, [(i, i ^ 1) for i in range(8)])
    flat = (B + 8, LON)
    packs = (len(STARTS), B + 8, LON)
    core, part = call(core_rows, ((LAT, B + 8, LON), packs), flops=1 << 22, moved=1 << 20)(x, h)
    far, near, north, south, packed = call(side_columns, (flat, flat, edge, edge, packs))(far, near, part)
    far = lax.ppermute(far, COL, [(i, (((i + 1) ^ 1) - 1) % 32) for i in range(32)])
    near = lax.ppermute(near, COL, [(i, i ^ 1) for i in range(32)])
    wide = pltpu.VMEM((ROWS, B, LON), jnp.float32)
    thin = pltpu.VMEM((ROWS, 8, LON), jnp.float32)
    square = (ALL, ALL)
    s, own = call(
        inside, ((LAT, ALL, LON), square), [wide, wide, thin, thin, thin], flops=1 << 28, moved=1 << 23
    )(core, north, south)
    rim = (ALL - B, LON)
    gram, west, east = call(border, ((B, LON), rim, rim))(far, near, packed, own)
    other = lax.ppermute(gram, ROW, [(i, i ^ 1) for i in range(8)])
    copies = call(join, ((16, B, LON),))(gram, other)[0]
    parts = lax.all_to_all(copies, ("x", "y"), 0, 0)
    copies = call(spread, ((8, B, LON),))(parts)[0]
    parts = lax.all_to_all(copies, "z", 0, 0)
    table = (ITERS, B, B)
    results = ((ALL, LAT, LON), table, table)
    return call(
        basis,
        results,
        [pltpu.VMEM(shape, jnp.float32) for shape in results]
        + [pltpu.VMEM((LAT // 2, ALL, 2 * LON), jnp.bfloat16)] * 3
        + [pltpu.SemaphoreType.DMA((2 + (LAT // 8) * (ALL // PIECE),))],
        out_specs=(anywhere,) * 3,
    )(parts, s, west, east)


def solution(mesh):
    torus = Mesh(mesh.devices.reshape(4, 2, 8, 4), ("x", "core", "z", "y"))
    in_specs = (P(None, ROW, COL), P(ROW, COL), P(ROW, COL))
    out_specs = (P(None, ROW, COL), P(), P())
    return jax.shard_map(body, mesh=torus, in_specs=in_specs, out_specs=out_specs, check_vma=False)
```

```python
import jax
import jax.numpy as jnp
from jax import lax
from jax.experimental import pallas as pl
from jax.experimental.pallas import tpu as pltpu
from jax.sharding import Mesh, PartitionSpec as P

ITERS = 3
LEVELS = 50.0
KAPPA = 1.5
CELLS = 1048576.0

B = 32
LAT = 32
LON = 128
RIM = 3
ROWS = LAT + 2 * RIM
STARTS = (0, RIM, LON - 2 * RIM, LON - RIM)
ALL = (ITERS + 1) * B
HALF = B // 2
PIECE = 64
HALVES = [(k, part) for k in range(ITERS) for part in range(2)]
HIGH = lax.Precision.HIGHEST
ROW, COL = ("x", "core"), ("z", "y")
NT = (((1,), (1,)), ((), ()))
TN = (((0,), (0,)), ((), ()))
PARAMS = pltpu.CompilerParams(vmem_limit_bytes=48 * 1024 * 1024)


def lanes_of(rows):
    return lax.broadcasted_iota(jnp.int32, (rows, LON), 1)


def call(kernel, outs, scratch=(), flops=0, moved=0, **specs):
    return pl.pallas_call(
        kernel,
        **specs,
        out_shape=tuple(jax.ShapeDtypeStruct(s, jnp.float32) for s in outs),
        scratch_shapes=list(scratch),
        compiler_params=PARAMS,
        cost_estimate=pl.CostEstimate(flops=flops, bytes_accessed=moved, transcendentals=0),
    )


def edge_rows(x_hbm, mask_hbm, depth_hbm, far_ref, near_ref, x_ref, h_ref, mask_ref, depth_ref, sems):
    pairs = ((x_hbm, x_ref), (mask_hbm, mask_ref), (depth_hbm, depth_ref))
    copies = [pltpu.make_async_copy(a, b, sems.at[i]) for i, (a, b) in enumerate(pairs)]
    for copy in copies:
        copy.start()
    for copy in copies[1:]:
        copy.wait()
    h_ref[...] = mask_ref[...].astype(jnp.float32) * depth_ref[...].astype(jnp.float32) / LEVELS
    copies[0].wait()
    odd = lax.axis_index("core") == 1
    for i in range(RIM):
        top = masked_row(i, x_ref, h_ref)
        bottom = masked_row(LAT - RIM + i, x_ref, h_ref)
        near_ref[i] = jnp.where(odd, top, bottom)
        far_ref[i] = jnp.where(odd, bottom, top)


def masked_row(lat, x_ref, h_ref):
    depth = h_ref[pl.ds(lat, 1), :]
    row = jnp.where(depth > 0.0, x_ref[pl.ds(lat, B, stride=LAT), :], 0.0)
    return jnp.concatenate([row, jnp.broadcast_to(depth, (8, LON))], axis=0)


def pack_sides(row, r, packed):
    lane = lanes_of(B + 8)
    here = (lane >= RIM * r) & (lane < RIM * r + RIM)
    return [jnp.where(here, pltpu.roll(row, (RIM * r - start) % LON, 1), p) for p, start in zip(packed, STARTS)]


def core_rows(x_ref, h_ref, core_ref, packed_ref):
    packed = [jnp.zeros((B + 8, LON), jnp.float32)] * len(STARTS)
    for i in range(LAT):
        row = masked_row(i, x_ref, h_ref)
        core_ref[i] = row
        packed = pack_sides(row, i + RIM, packed)
    for k, value in enumerate(packed):
        packed_ref[k] = value


def side_columns(far_ref, near_ref, part_ref, far_out, near_out, north_ref, south_ref, packed_ref):
    odd = lax.axis_index("core") == 1
    packed = [part_ref[k] for k in range(len(STARTS))]
    for i in range(RIM):
        north = jnp.where(odd, near_ref[i], far_ref[i])
        south = jnp.where(odd, far_ref[i], near_ref[i])
        north_ref[i] = north
        south_ref[i] = south
        packed = pack_sides(north, i, packed)
        packed = pack_sides(south, i + RIM + LAT, packed)
    for k, value in enumerate(packed):
        packed_ref[k] = value
    odd = lax.axis_index("y") % 2 == 1
    near_out[...] = jnp.where(odd, packed[0], packed[3])
    far_out[...] = jnp.where(odd, packed[3], packed[0])


def split(value):
    high = value.astype(jnp.bfloat16)
    rest = value - high.astype(jnp.float32)
    middle = rest.astype(jnp.bfloat16)
    low = (rest - middle.astype(jnp.float32)).astype(jnp.bfloat16)
    return high, middle, low


def four(field):
    return jnp.concatenate([field] * (B // 8), axis=0)


def outer(left, right):
    return lax.dot_general(left, right, NT, preferred_element_type=jnp.float32)


def products(value):
    high, middle, low = split(value)
    both = outer(high, jnp.concatenate([high, middle], axis=0))
    return both[:, :ALL] + outer(middle, middle), both[:, ALL:] + outer(high, low)


def inside(core_ref, north_ref, south_ref, s_ref, own_ref, k1_ref, k2_ref, down_ref, right_ref, centre_ref):
    def base(r):
        if r < RIM:
            return north_ref[r]
        return core_ref[r - RIM] if r < RIM + LAT else south_ref[r - RIM - LAT]

    for r in range(ROWS - 1):
        h = base(r)[B:]
        down_ref[r] = KAPPA * jnp.minimum(h, base(r + 1)[B:])
        right_ref[r] = KAPPA * jnp.minimum(h, pltpu.roll(h, LON - 1, 1))
        centre_ref[r] = jnp.where(h > 0.0, 0.0, -1.0)
    levels = (
        (lambda r: base(r)[:B], k1_ref),
        (lambda r: k1_ref[r], k2_ref),
        (lambda r: k2_ref[r], None),
    )
    for step, (source, target) in enumerate(levels):
        first, last = step + 1, ROWS - 2 - step
        v, after = source(first - 1), source(first)
        flux = four(down_ref[first - 1]) * (v - after)
        for r in range(first, last + 1):
            v, after = after, source(r + 1)
            down = four(down_ref[r]) * (v - after)
            right = four(right_ref[r]) * (v - pltpu.roll(v, LON - 1, 1))
            new = four(centre_ref[r]) * v + ((down - flux) + (right - pltpu.roll(right, 1, 1)))
            flux = down
            if target is not None:
                target[r] = new
            if RIM <= r < RIM + LAT:
                s_ref[r - RIM, (step + 1) * B:(step + 2) * B, :] = new
    lane = lanes_of(ALL)
    clean = (lane >= RIM) & (lane < LON - RIM)
    even = half = jnp.zeros((ALL, ALL), jnp.float32)
    for i in range(0, LAT, 2):
        rows = []
        for j in (i, i + 1):
            s_ref[j, :B, :] = core_ref[j, :B]
            rows.append(jnp.where(clean, s_ref[j], 0.0))
        one, two = products(jnp.concatenate(rows, axis=1))
        even += one
        half += two
    own_ref[...] = even + half + half.T


def border(far_ref, near_ref, packed_ref, own_ref, gram_ref, west_ref, east_ref):
    odd = lax.axis_index("y") % 2 == 1
    near, far = near_ref[...], far_ref[...]
    lane = lanes_of(B)
    line = (lane * 21846) >> 16
    place = lane - RIM * line
    first, last = place == 0, place == RIM - 1
    kept = (line[:1] >= RIM) & (line[:1] < RIM + LAT)
    move = lambda value, by: pltpu.roll(value, by % LON, 1)

    def rightward(values, i):
        inner = move(values[i], -1)
        return jnp.where(last[:inner.shape[0]], move(values[i + 1], RIM - 1), inner) if i < 2 else inner

    def leftward(values, i):
        inner = move(values[i], 1)
        return jnp.where(first[:inner.shape[0]], move(values[i - 1], 1 - RIM), inner) if i > 0 else inner

    fields = []
    for chain, out_ref in (
        ((jnp.where(odd, near, far), packed_ref[0], packed_ref[1]), west_ref),
        ((packed_ref[2], packed_ref[3], jnp.where(odd, far, near)), east_ref),
    ):
        h = [part[B:] for part in chain]
        south = [KAPPA * jnp.minimum(h[i], move(h[i], -RIM)) for i in range(3)]
        right = [KAPPA * jnp.minimum(h[i], rightward(h, i)) for i in range(3)]
        right[2] = jnp.where(last[:8], 0.0, right[2])
        left = [KAPPA * jnp.minimum(h[i], leftward(h, i)) for i in range(3)]
        left[0] = jnp.where(first[:8], 0.0, left[0])
        north = [four(KAPPA * jnp.minimum(value, move(value, RIM))) for value in h]
        south, right, left = [[four(value) for value in values] for values in (south, right, left)]
        centre = [four(jnp.where(value > 0.0, 0.0, -1.0)) for value in h]
        v = [part[:B] for part in chain]
        found = [v[1]]
        for step in range(ITERS):
            v = [
                centre[i] * v[i]
                + (
                    (south[i] * (v[i] - move(v[i], -RIM)) + north[i] * (v[i] - move(v[i], RIM)))
                    + (right[i] * (v[i] - rightward(v, i)) + left[i] * (v[i] - leftward(v, i)))
                )
                for i in range(3)
            ]
            found.append(v[1])
        out_ref[...] = jnp.concatenate(found[1:], axis=0)
        fields.append(jnp.where(kept, jnp.concatenate(found, axis=0), 0.0))
    high, middle, low = split(jnp.concatenate(fields, axis=1))
    both = jnp.concatenate([high, middle], axis=0)
    both = outer(both, both)
    large, small = both[:ALL, :ALL], both[:ALL, ALL:] + both[ALL:, :ALL]
    gram = (own_ref[...] + large) + (small + (both[ALL:, ALL:] + (outer(high, low) + outer(low, high))))
    row = lax.broadcasted_iota(jnp.int32, (B, LON), 0)
    lane = lax.broadcasted_iota(jnp.int32, (B, LON), 1)
    packed = diagonal = jnp.zeros((B, LON), jnp.float32)
    for k in range(ITERS + 1):
        own = gram[k * B:(k + 1) * B]
        after = pltpu.roll(own, LON - B, 1)
        here = (lane >= k * B) & (lane < (k + 1) * B)
        packed = jnp.where(here, jnp.where(lane - k * B <= row, own, after), packed)
        diagonal = jnp.where(lane - (k + 1) * B == row, own, diagonal)
    line = jnp.sum(diagonal, axis=0, keepdims=True)
    for n, (k, part) in enumerate(HALVES):
        there = (row == n) & (lane >= ITERS * B + HALF)
        packed = jnp.where(there, pltpu.roll(line, (ITERS * B + HALF - (k + 1) * B - part * HALF) % LON, 1), packed)
    gram_ref[...] = packed


def spread(parts_ref, out_ref):
    total = parts_ref[0]
    for i in range(1, parts_ref.shape[0]):
        total += parts_ref[i]
    for i in range(out_ref.shape[0]):
        out_ref[i] = total


def join(own_ref, other_ref, out_ref):
    total = own_ref[...] + other_ref[...]
    for i in range(out_ref.shape[0]):
        out_ref[i] = total


def unpack(total):
    row = lax.broadcasted_iota(jnp.int32, (B, LON), 0)
    lane = lax.broadcasted_iota(jnp.int32, (B, LON), 1)
    block, place = lane >> 5, lane & (B - 1)
    turned = jnp.concatenate([jnp.where(block == k, total, 0.0) for k in range(ITERS + 1)], axis=0).T
    mirror = (turned[:B] + turned[B:2 * B]) + (turned[2 * B:3 * B] + turned[3 * B:])
    even = jnp.where(place <= row, total, mirror)
    odd = jnp.where(place > row, total, mirror)
    line = jnp.zeros((1, LON), jnp.float32)
    for n, (k, part) in enumerate(HALVES):
        target = k * B + part * HALF
        moved = pltpu.roll(total[n:n + 1], (target - ITERS * B - HALF) % LON, 1)
        line = jnp.where((lane[:1] >= target) & (lane[:1] < target + HALF), moved, line)
    odd = jnp.where(place == row, line, odd)
    move = lambda field, k: pltpu.roll(field, (k * B) % LON, 1)
    pick = lambda a, b, c, d: jnp.where(block == 0, a, jnp.where(block == 1, b, jnp.where(block == 2, c, d)))
    even_on, even_back, odd_on, odd_back = move(even, 1), move(even, -1), move(odd, 1), move(odd, -1)
    rows = [
        pick(even, odd_on, even_on, move(odd, 2)),
        pick(odd, even, odd_on, even_on),
        pick(even_back, odd, even, odd_on),
        pick(odd_back, even_back, odd, even),
    ]
    return total, jnp.concatenate(rows, axis=0)


def reciprocal(value):
    return 1.0 / value


def factor(first, gram):
    groups = ALL // 8
    lane = lax.broadcasted_iota(jnp.int32, (8, ALL), 1)
    sub = lax.broadcasted_iota(jnp.int32, (8, ALL), 0)
    full = lambda value: jnp.broadcast_to(value, (8, ALL))
    line = lambda value, t: full(value[t:t + 1])
    tree = lambda p: ((p[0] + p[1]) + (p[2] + p[3])) + ((p[4] + p[5]) + (p[6] + p[7]))
    weigh = lambda p, q: tree([p[t] * q[t] for t in range(8)])
    work = [gram[8 * g:8 * g + 8] for g in range(groups)]
    columns = lambda k, g: [full(work[k][:, 8 * g + t:8 * g + t + 1]) for t in range(8)] if k < groups else None
    diagonal = sum(jnp.where(lane == sub + 8 * g, work[g], 0.0) for g in range(groups))
    guess = full(reciprocal(jnp.sum(diagonal, axis=0, keepdims=True)))
    uppers, inverses = [], []
    own, after = [[full(first[8 * k:8 * k + 8, t:t + 1]) for t in range(8)] for k in range(2)]
    for g in range(groups):
        later, coming = columns(g + 2, g), columns(g + 1, g + 1)
        a = work[g]
        b = jnp.where(lane == sub + 8 * g, 1.0, jnp.where(lane < 8 * g, work[g], 0.0))
        recip, ratio, pivot = [None] * 8, {}, []
        for t in range(8):
            pivot.append(line(own[t], t))
            if recip[t] is None:
                recip[t] = reciprocal(pivot[t])
            if t % 2 == 0 and g > 0:
                unit = full(guess[:, 8 * g + t:8 * g + t + 1])
                near, cross = pivot[t] * unit, line(own[t], t + 1)
                recip[t + 1] = near * reciprocal(near * line(own[t + 1], t + 1) - cross * (cross * unit))
            column = jnp.where(sub > t, own[t] * recip[t], 0.0)
            for s in range(t + 1, 8):
                ratio[s, t] = line(column, s)
                own[s] = own[s] - column * line(own[t], s)
            if t < 7:
                a = a - column * line(a, t)
                b = b - column * line(b, t)
                for ahead in (after, later):
                    for s in range(t + 1, 8) if ahead else ():
                        ahead[s] = ahead[s] - ratio[s, t] * ahead[t]
        pivots = inverted = jnp.zeros((8, ALL), jnp.float32)
        for t in range(8):
            pivots = jnp.where(sub == t, pivot[t], pivots)
            inverted = jnp.where(sub == t, recip[t], inverted)
        scale = lax.rsqrt(pivots)
        uppers.append(jnp.where(lane >= sub + 8 * g, a * scale, 0.0))
        inverses.append(b * scale)
        if g + 1 == groups:
            break
        c = jnp.where(lane < 8 * g + 8, b, a) * inverted
        c = [line(c, t) for t in range(8)]
        scaled = [after[t] * recip[t] for t in range(8)]
        own = [coming[u] - weigh(after, [line(scaled[t], u) for t in range(8)]) for u in range(8)]
        block = (lane >= 8 * g) & (lane < 8 * g + 8)
        for k, ahead in ((g + 1, after), (g + 2, later)):
            if ahead:
                work[k] = jnp.where(block, 0.0, work[k]) - weigh(ahead, c)
        after = columns(g + 2, g + 1)
        for t in range(7, 0, -1):
            for s in range(t):
                c[s] = c[s] - ratio[t, s] * c[t]
        panel = 8 * g // B
        for k in range(g + 3, min((panel + 2) * B // 8, groups)):
            work[k] = jnp.where(block, 0.0, work[k]) - weigh(columns(k, g), c)
        if (8 * g + 8) % B == 0 and (panel + 2) * B < ALL:
            top = jnp.concatenate(uppers[-B // 8:], axis=0)
            wide = lax.broadcasted_iota(jnp.int32, (B, ALL), 1) < (panel + 1) * B
            rest = jnp.where(wide, jnp.concatenate(inverses[-B // 8:], axis=0), top)
            change = lax.dot_general(top, rest, TN, precision=HIGH, preferred_element_type=jnp.float32)
            block = (lane >= panel * B) & (lane < (panel + 1) * B)
            for k in range((panel + 2) * B // 8, groups):
                work[k] = jnp.where(block, 0.0, work[k]) - change[8 * k:8 * k + 8]
    return jnp.concatenate(inverses, axis=0), jnp.concatenate(uppers, axis=0)


def swap(rows, sub):
    for k in (4, 2, 1):
        low, new = (sub & k) == 0, list(rows)
        for i in range(8):
            if not i & k:
                new[i] = jnp.where(low, rows[i], pltpu.roll(rows[i | k], k, 0))
                new[i | k] = jnp.where(low, pltpu.roll(rows[i], 8 - k, 0), rows[i | k])
        rows = new
    return rows


def whole_row(i, s_ref, west_ref, east_ref):
    lane = lanes_of(ALL - B)
    row = s_ref[i, B:, :]
    for ref, target in ((west_ref, 0), (east_ref, LON - RIM)):
        side = pltpu.roll(ref[...], (target - RIM * (i + RIM)) % LON, 1)
        row = jnp.where((lane >= target) & (lane < target + RIM), side, row)
    return jnp.concatenate([s_ref[i, :B, :], row], axis=0)


def basis(parts_ref, s_ref, west_ref, east_ref, q_hbm, alpha_hbm, beta_hbm,
          q_ref, alpha_ref, beta_ref, high_ref, middle_ref, low_ref, sems):
    for i in range(0, LAT, 2):
        pair = [whole_row(j, s_ref, west_ref, east_ref) for j in (i, i + 1)]
        a, b, c = split(jnp.concatenate(pair, axis=1))
        high_ref[i // 2] = a
        middle_ref[i // 2] = b
        low_ref[i // 2] = c
    total = parts_ref[0]
    for i in range(1, parts_ref.shape[0]):
        total += parts_ref[i]
    inverse, upper = factor(*unpack(total * (1.0 / CELLS)))
    lane = lax.broadcasted_iota(jnp.int32, (ALL, ALL), 1)
    image = jnp.where(lane < ITERS * B, inverse, 0.0) + jnp.where(lane >= B, pltpu.roll(inverse, B, 1), 0.0)
    coeffs = lax.dot_general(upper, image, NT, precision=HIGH, preferred_element_type=jnp.float32)
    for k in range(ITERS):
        here, after = slice(k * B, (k + 1) * B), slice((k + 1) * B, (k + 2) * B)
        alpha_ref[k] = coeffs[here, here]
        beta_ref[k] = coeffs[after, here]
    copies = [
        pltpu.make_async_copy(alpha_ref, alpha_hbm, sems.at[0]),
        pltpu.make_async_copy(beta_ref, beta_hbm, sems.at[1]),
    ]
    for copy in copies:
        copy.start()
    high, middle, low = split(inverse)
    two = jnp.concatenate([high, middle], axis=1)
    three = jnp.concatenate([high, middle, low], axis=1)
    dot = lambda a, b: jnp.dot(a, b, preferred_element_type=jnp.float32)
    sub = lax.broadcasted_iota(jnp.int32, (8, LON), 0)
    for g in range(LAT // 8):
        rows = []
        for i in range(8 * g, 8 * g + 8, 2):
            a, b, c = high_ref[i // 2], middle_ref[i // 2], low_ref[i // 2]
            new = dot(three, jnp.concatenate([a, a, a], axis=0)) + dot(two, jnp.concatenate([b, b], axis=0)) + dot(high, c)
            rows += [new[:, :LON], new[:, LON:]]
        chunk = pl.ds(8 * g, 8)
        for v in range(0, ALL, 8):
            for t, tile in enumerate(swap([row[v:v + 8] for row in rows], sub)):
                q_ref[v + t, 8 * g:8 * g + 8, :] = tile
            if v % PIECE == PIECE - 8:
                block = pl.ds(v + 8 - PIECE, PIECE)
                sem = sems.at[len(copies)]
                copies.append(pltpu.make_async_copy(q_ref.at[block, chunk, :], q_hbm.at[block, chunk, :], sem))
                copies[-1].start()
    for copy in copies:
        copy.wait()


def body(start_block, sea_mask, depth_levels):
    x = start_block.reshape(B * LAT, LON)
    x, sea_mask, depth_levels = [pltpu.with_memory_space_constraint(v, pltpu.HBM) for v in (x, sea_mask, depth_levels)]
    edge = (RIM, B + 8, LON)
    anywhere = pl.BlockSpec(memory_space=pl.ANY)
    small = pltpu.VMEM((LAT, LON), jnp.int32)
    far, near, x, h = call(
        edge_rows,
        (edge, edge, (B * LAT, LON), (LAT, LON)),
        [small, small, pltpu.SemaphoreType.DMA((3,))],
        in_specs=[pl.BlockSpec(memory_space=pltpu.HBM)] * 3,
    )(x, sea_mask, depth_levels)
    far = lax.ppermute(far, ROW, [(i, ((i + 1) ^ 1) - 1) for i in range(1, 7)])
    near = lax.ppermute(near, ROW, [(i, i ^ 1) for i in range(8)])
    flat = (B + 8, LON)
    packs = (len(STARTS), B + 8, LON)
    core, part = call(core_rows, ((LAT, B + 8, LON), packs), flops=1 << 22, moved=1 << 20)(x, h)
    far, near, north, south, packed = call(side_columns, (flat, flat, edge, edge, packs))(far, near, part)
    far = lax.ppermute(far, COL, [(i, (((i + 1) ^ 1) - 1) % 32) for i in range(32)])
    near = lax.ppermute(near, COL, [(i, i ^ 1) for i in range(32)])
    wide = pltpu.VMEM((ROWS, B, LON), jnp.float32)
    thin = pltpu.VMEM((ROWS, 8, LON), jnp.float32)
    square = (ALL, ALL)
    s, own = call(
        inside, ((LAT, ALL, LON), square), [wide, wide, thin, thin, thin], flops=1 << 28, moved=1 << 23
    )(core, north, south)
    rim = (ALL - B, LON)
    gram, west, east = call(border, ((B, LON), rim, rim))(far, near, packed, own)
    other = lax.ppermute(gram, ROW, [(i, i ^ 1) for i in range(8)])
    copies = call(join, ((16, B, LON),))(gram, other)[0]
    parts = lax.all_to_all(copies, ("x", "y"), 0, 0)
    copies = call(spread, ((8, B, LON),))(parts)[0]
    parts = lax.all_to_all(copies, "z", 0, 0)
    table = (ITERS, B, B)
    results = ((ALL, LAT, LON), table, table)
    return call(
        basis,
        results,
        [pltpu.VMEM(shape, jnp.float32) for shape in results]
        + [pltpu.VMEM((LAT // 2, ALL, 2 * LON), jnp.bfloat16)] * 3
        + [pltpu.SemaphoreType.DMA((2 + (LAT // 8) * (ALL // PIECE),))],
        out_specs=(anywhere,) * 3,
    )(parts, s, west, east)


def solution(mesh):
    torus = Mesh(mesh.devices.reshape(4, 2, 8, 4), ("x", "core", "z", "y"))
    in_specs = (P(None, ROW, COL), P(ROW, COL), P(ROW, COL))
    out_specs = (P(None, ROW, COL), P(), P())
    return jax.shard_map(body, mesh=torus, in_specs=in_specs, out_specs=out_specs, check_vma=False)
```

```python
import jax
import jax.numpy as jnp
from jax import lax
from jax.experimental import pallas as pl
from jax.experimental.pallas import tpu as pltpu
from jax.sharding import Mesh, PartitionSpec as P

ITERS = 3
LEVELS = 50.0
KAPPA = 1.5
CELLS = 1048576.0

B = 32
LAT = 32
LON = 128
RIM = 3
ROWS = LAT + 2 * RIM
STARTS = (0, RIM, LON - 2 * RIM, LON - RIM)
ALL = (ITERS + 1) * B
HALF = B // 2
PIECE = 64
HALVES = [(k, part) for k in range(ITERS) for part in range(2)]
HIGH = lax.Precision.HIGHEST
ROW, COL = ("x", "core"), ("z", "y")
NT = (((1,), (1,)), ((), ()))
TN = (((0,), (0,)), ((), ()))
PARAMS = pltpu.CompilerParams(vmem_limit_bytes=48 * 1024 * 1024)


def lanes_of(rows):
    return lax.broadcasted_iota(jnp.int32, (rows, LON), 1)


def call(kernel, outs, scratch=(), flops=0, moved=0, **specs):
    return pl.pallas_call(
        kernel,
        **specs,
        out_shape=tuple(jax.ShapeDtypeStruct(s, jnp.float32) for s in outs),
        scratch_shapes=list(scratch),
        compiler_params=PARAMS,
        cost_estimate=pl.CostEstimate(flops=flops, bytes_accessed=moved, transcendentals=0),
    )


def edge_rows(x_hbm, mask_hbm, depth_hbm, far_ref, near_ref, x_ref, h_ref, mask_ref, depth_ref, sems):
    pairs = ((x_hbm, x_ref), (mask_hbm, mask_ref), (depth_hbm, depth_ref))
    copies = [pltpu.make_async_copy(a, b, sems.at[i]) for i, (a, b) in enumerate(pairs)]
    for copy in copies:
        copy.start()
    for copy in copies[1:]:
        copy.wait()
    h_ref[...] = mask_ref[...].astype(jnp.float32) * depth_ref[...].astype(jnp.float32) / LEVELS
    copies[0].wait()
    odd = lax.axis_index("core") == 1
    for i in range(RIM):
        top = masked_row(i, x_ref, h_ref)
        bottom = masked_row(LAT - RIM + i, x_ref, h_ref)
        near_ref[i] = jnp.where(odd, top, bottom)
        far_ref[i] = jnp.where(odd, bottom, top)


def masked_row(lat, x_ref, h_ref):
    depth = h_ref[pl.ds(lat, 1), :]
    row = jnp.where(depth > 0.0, x_ref[pl.ds(lat, B, stride=LAT), :], 0.0)
    return jnp.concatenate([row, jnp.broadcast_to(depth, (8, LON))], axis=0)


def pack_sides(row, r, packed):
    lane = lanes_of(B + 8)
    here = (lane >= RIM * r) & (lane < RIM * r + RIM)
    return [jnp.where(here, pltpu.roll(row, (RIM * r - start) % LON, 1), p) for p, start in zip(packed, STARTS)]


def core_rows(x_ref, h_ref, core_ref, packed_ref):
    packed = [jnp.zeros((B + 8, LON), jnp.float32)] * len(STARTS)
    for i in range(LAT):
        row = masked_row(i, x_ref, h_ref)
        core_ref[i] = row
        packed = pack_sides(row, i + RIM, packed)
    for k, value in enumerate(packed):
        packed_ref[k] = value


def side_columns(far_ref, near_ref, part_ref, far_out, near_out, north_ref, south_ref, packed_ref):
    odd = lax.axis_index("core") == 1
    packed = [part_ref[k] for k in range(len(STARTS))]
    for i in range(RIM):
        north = jnp.where(odd, near_ref[i], far_ref[i])
        south = jnp.where(odd, far_ref[i], near_ref[i])
        north_ref[i] = north
        south_ref[i] = south
        packed = pack_sides(north, i, packed)
        packed = pack_sides(south, i + RIM + LAT, packed)
    for k, value in enumerate(packed):
        packed_ref[k] = value
    odd = lax.axis_index("y") % 2 == 1
    near_out[...] = jnp.where(odd, packed[0], packed[3])
    far_out[...] = jnp.where(odd, packed[3], packed[0])


def split(value):
    high = value.astype(jnp.bfloat16)
    rest = value - high.astype(jnp.float32)
    middle = rest.astype(jnp.bfloat16)
    low = (rest - middle.astype(jnp.float32)).astype(jnp.bfloat16)
    return high, middle, low


def four(field):
    return jnp.concatenate([field] * (B // 8), axis=0)


def outer(left, right):
    return lax.dot_general(left, right, NT, preferred_element_type=jnp.float32)


def products(value):
    high, middle, low = split(value)
    both = outer(high, jnp.concatenate([high, middle], axis=0))
    return both[:, :ALL] + outer(middle, middle), both[:, ALL:] + outer(high, low)


def inside(core_ref, north_ref, south_ref, s_ref, own_ref, k1_ref, k2_ref, down_ref, right_ref, centre_ref):
    def base(r):
        if r < RIM:
            return north_ref[r]
        return core_ref[r - RIM] if r < RIM + LAT else south_ref[r - RIM - LAT]

    for r in range(ROWS - 1):
        h = base(r)[B:]
        down_ref[r] = KAPPA * jnp.minimum(h, base(r + 1)[B:])
        right_ref[r] = KAPPA * jnp.minimum(h, pltpu.roll(h, LON - 1, 1))
        centre_ref[r] = jnp.where(h > 0.0, 0.0, -1.0)
    levels = (
        (lambda r: base(r)[:B], k1_ref),
        (lambda r: k1_ref[r], k2_ref),
        (lambda r: k2_ref[r], None),
    )
    for step, (source, target) in enumerate(levels):
        first, last = step + 1, ROWS - 2 - step
        v, after = source(first - 1), source(first)
        flux = four(down_ref[first - 1]) * (v - after)
        for r in range(first, last + 1):
            v, after = after, source(r + 1)
            down = four(down_ref[r]) * (v - after)
            right = four(right_ref[r]) * (v - pltpu.roll(v, LON - 1, 1))
            new = four(centre_ref[r]) * v + ((down - flux) + (right - pltpu.roll(right, 1, 1)))
            flux = down
            if target is not None:
                target[r] = new
            if RIM <= r < RIM + LAT:
                s_ref[r - RIM, (step + 1) * B:(step + 2) * B, :] = new
    lane = lanes_of(ALL)
    clean = (lane >= RIM) & (lane < LON - RIM)
    even = half = jnp.zeros((ALL, ALL), jnp.float32)
    for i in range(0, LAT, 2):
        rows = []
        for j in (i, i + 1):
            s_ref[j, :B, :] = core_ref[j, :B]
            rows.append(jnp.where(clean, s_ref[j], 0.0))
        one, two = products(jnp.concatenate(rows, axis=1))
        even += one
        half += two
    own_ref[...] = even + half + half.T


def border(far_ref, near_ref, packed_ref, own_ref, gram_ref, west_ref, east_ref):
    odd = lax.axis_index("y") % 2 == 1
    near, far = near_ref[...], far_ref[...]
    lane = lanes_of(B)
    line = (lane * 21846) >> 16
    place = lane - RIM * line
    first, last = place == 0, place == RIM - 1
    kept = (line[:1] >= RIM) & (line[:1] < RIM + LAT)
    move = lambda value, by: pltpu.roll(value, by % LON, 1)

    def rightward(values, i):
        inner = move(values[i], -1)
        return jnp.where(last[:inner.shape[0]], move(values[i + 1], RIM - 1), inner) if i < 2 else inner

    def leftward(values, i):
        inner = move(values[i], 1)
        return jnp.where(first[:inner.shape[0]], move(values[i - 1], 1 - RIM), inner) if i > 0 else inner

    fields = []
    for chain, out_ref in (
        ((jnp.where(odd, near, far), packed_ref[0], packed_ref[1]), west_ref),
        ((packed_ref[2], packed_ref[3], jnp.where(odd, far, near)), east_ref),
    ):
        h = [part[B:] for part in chain]
        south = [KAPPA * jnp.minimum(h[i], move(h[i], -RIM)) for i in range(3)]
        right = [KAPPA * jnp.minimum(h[i], rightward(h, i)) for i in range(3)]
        right[2] = jnp.where(last[:8], 0.0, right[2])
        left = [KAPPA * jnp.minimum(h[i], leftward(h, i)) for i in range(3)]
        left[0] = jnp.where(first[:8], 0.0, left[0])
        north = [four(KAPPA * jnp.minimum(value, move(value, RIM))) for value in h]
        south, right, left = [[four(value) for value in values] for values in (south, right, left)]
        centre = [four(jnp.where(value > 0.0, 0.0, -1.0)) for value in h]
        v = [part[:B] for part in chain]
        found = [v[1]]
        for step in range(ITERS):
            v = [
                centre[i] * v[i]
                + (
                    (south[i] * (v[i] - move(v[i], -RIM)) + north[i] * (v[i] - move(v[i], RIM)))
                    + (right[i] * (v[i] - rightward(v, i)) + left[i] * (v[i] - leftward(v, i)))
                )
                for i in range(3)
            ]
            found.append(v[1])
        out_ref[...] = jnp.concatenate(found[1:], axis=0)
        fields.append(jnp.where(kept, jnp.concatenate(found, axis=0), 0.0))
    high, middle, low = split(jnp.concatenate(fields, axis=1))
    both = jnp.concatenate([high, middle], axis=0)
    both = outer(both, both)
    large, small = both[:ALL, :ALL], both[:ALL, ALL:] + both[ALL:, :ALL]
    gram = (own_ref[...] + large) + (small + (both[ALL:, ALL:] + (outer(high, low) + outer(low, high))))
    row = lax.broadcasted_iota(jnp.int32, (B, LON), 0)
    lane = lax.broadcasted_iota(jnp.int32, (B, LON), 1)
    packed = diagonal = jnp.zeros((B, LON), jnp.float32)
    for k in range(ITERS + 1):
        own = gram[k * B:(k + 1) * B]
        after = pltpu.roll(own, LON - B, 1)
        here = (lane >= k * B) & (lane < (k + 1) * B)
        packed = jnp.where(here, jnp.where(lane - k * B <= row, own, after), packed)
        diagonal = jnp.where(lane - (k + 1) * B == row, own, diagonal)
    line = jnp.sum(diagonal, axis=0, keepdims=True)
    for n, (k, part) in enumerate(HALVES):
        there = (row == n) & (lane >= ITERS * B + HALF)
        packed = jnp.where(there, pltpu.roll(line, (ITERS * B + HALF - (k + 1) * B - part * HALF) % LON, 1), packed)
    gram_ref[...] = packed


def spread(parts_ref, out_ref):
    total = parts_ref[0]
    for i in range(1, parts_ref.shape[0]):
        total += parts_ref[i]
    for i in range(out_ref.shape[0]):
        out_ref[i] = total


def join(own_ref, other_ref, out_ref):
    total = own_ref[...] + other_ref[...]
    for i in range(out_ref.shape[0]):
        out_ref[i] = total


def unpack(total):
    row = lax.broadcasted_iota(jnp.int32, (B, LON), 0)
    lane = lax.broadcasted_iota(jnp.int32, (B, LON), 1)
    block, place = lane >> 5, lane & (B - 1)
    turned = jnp.concatenate([jnp.where(block == k, total, 0.0) for k in range(ITERS + 1)], axis=0).T
    mirror = (turned[:B] + turned[B:2 * B]) + (turned[2 * B:3 * B] + turned[3 * B:])
    even = jnp.where(place <= row, total, mirror)
    odd = jnp.where(place > row, total, mirror)
    line = jnp.zeros((1, LON), jnp.float32)
    for n, (k, part) in enumerate(HALVES):
        target = k * B + part * HALF
        moved = pltpu.roll(total[n:n + 1], (target - ITERS * B - HALF) % LON, 1)
        line = jnp.where((lane[:1] >= target) & (lane[:1] < target + HALF), moved, line)
    odd = jnp.where(place == row, line, odd)
    move = lambda field, k: pltpu.roll(field, (k * B) % LON, 1)
    pick = lambda a, b, c, d: jnp.where(block == 0, a, jnp.where(block == 1, b, jnp.where(block == 2, c, d)))
    even_on, even_back, odd_on, odd_back = move(even, 1), move(even, -1), move(odd, 1), move(odd, -1)
    rows = [
        pick(even, odd_on, even_on, move(odd, 2)),
        pick(odd, even, odd_on, even_on),
        pick(even_back, odd, even, odd_on),
        pick(odd_back, even_back, odd, even),
    ]
    return total, jnp.concatenate(rows, axis=0)


def reciprocal(value):
    return 1.0 / value


def factor(first, gram):
    groups = ALL // 8
    lane = lax.broadcasted_iota(jnp.int32, (8, ALL), 1)
    sub = lax.broadcasted_iota(jnp.int32, (8, ALL), 0)
    full = lambda value: jnp.broadcast_to(value, (8, ALL))
    line = lambda value, t: full(value[t:t + 1])
    tree = lambda p: ((p[0] + p[1]) + (p[2] + p[3])) + ((p[4] + p[5]) + (p[6] + p[7]))
    weigh = lambda p, q: tree([p[t] * q[t] for t in range(8)])
    work = [gram[8 * g:8 * g + 8] for g in range(groups)]
    columns = lambda k, g: [full(work[k][:, 8 * g + t:8 * g + t + 1]) for t in range(8)] if k < groups else None
    diagonal = sum(jnp.where(lane == sub + 8 * g, work[g], 0.0) for g in range(groups))
    guess = full(reciprocal(jnp.sum(diagonal, axis=0, keepdims=True)))
    uppers, inverses = [], []
    own, after = [[full(first[8 * k:8 * k + 8, t:t + 1]) for t in range(8)] for k in range(2)]
    for g in range(groups):
        later, coming = columns(g + 2, g), columns(g + 1, g + 1)
        a = work[g]
        b = jnp.where(lane == sub + 8 * g, 1.0, jnp.where(lane < 8 * g, work[g], 0.0))
        recip, ratio, pivot = [None] * 8, {}, []
        for t in range(8):
            pivot.append(line(own[t], t))
            if recip[t] is None:
                recip[t] = reciprocal(pivot[t])
            if t % 2 == 0 and g > 0:
                unit = full(guess[:, 8 * g + t:8 * g + t + 1])
                near, cross = pivot[t] * unit, line(own[t], t + 1)
                recip[t + 1] = near * reciprocal(near * line(own[t + 1], t + 1) - cross * (cross * unit))
            column = own[t] * recip[t]
            for s in range(t + 1, 8):
                ratio[s, t] = line(column, s)
                own[s] = own[s] - column * line(own[t], s)
            if t < 7:
                column = jnp.where(sub > t, column, 0.0)
                a = a - column * line(a, t)
                b = b - column * line(b, t)
                for ahead in (after, later):
                    for s in range(t + 1, 8) if ahead else ():
                        ahead[s] = ahead[s] - ratio[s, t] * ahead[t]
        pivots = inverted = jnp.zeros((8, ALL), jnp.float32)
        for t in range(8):
            pivots = jnp.where(sub == t, pivot[t], pivots)
            inverted = jnp.where(sub == t, recip[t], inverted)
        scale = lax.rsqrt(pivots)
        uppers.append(jnp.where(lane >= sub + 8 * g, a * scale, 0.0))
        inverses.append(b * scale)
        if g + 1 == groups:
            break
        c = jnp.where(lane < 8 * g + 8, b, a) * inverted
        c = [line(c, t) for t in range(8)]
        scaled = [after[t] * recip[t] for t in range(8)]
        own = [coming[u] - weigh(after, [line(scaled[t], u) for t in range(8)]) for u in range(8)]
        block = (lane >= 8 * g) & (lane < 8 * g + 8)
        for k, ahead in ((g + 1, after), (g + 2, later)):
            if ahead:
                work[k] = jnp.where(block, 0.0, work[k]) - weigh(ahead, c)
        after = columns(g + 2, g + 1)
        for t in range(7, 0, -1):
            for s in range(t):
                c[s] = c[s] - ratio[t, s] * c[t]
        panel = 8 * g // B
        for k in range(g + 3, min((panel + 2) * B // 8, groups)):
            work[k] = jnp.where(block, 0.0, work[k]) - weigh(columns(k, g), c)
        if (8 * g + 8) % B == 0 and (panel + 2) * B < ALL:
            top = jnp.concatenate(uppers[-B // 8:], axis=0)
            wide = lax.broadcasted_iota(jnp.int32, (B, ALL), 1) < (panel + 1) * B
            rest = jnp.where(wide, jnp.concatenate(inverses[-B // 8:], axis=0), top)
            change = lax.dot_general(top, rest, TN, precision=HIGH, preferred_element_type=jnp.float32)
            block = (lane >= panel * B) & (lane < (panel + 1) * B)
            for k in range((panel + 2) * B // 8, groups):
                work[k] = jnp.where(block, 0.0, work[k]) - change[8 * k:8 * k + 8]
    return jnp.concatenate(inverses, axis=0), jnp.concatenate(uppers, axis=0)


def swap(rows, sub):
    for k in (4, 2, 1):
        low, new = (sub & k) == 0, list(rows)
        for i in range(8):
            if not i & k:
                new[i] = jnp.where(low, rows[i], pltpu.roll(rows[i | k], k, 0))
                new[i | k] = jnp.where(low, pltpu.roll(rows[i], 8 - k, 0), rows[i | k])
        rows = new
    return rows


def whole_row(i, s_ref, west_ref, east_ref):
    lane = lanes_of(ALL - B)
    row = s_ref[i, B:, :]
    for ref, target in ((west_ref, 0), (east_ref, LON - RIM)):
        side = pltpu.roll(ref[...], (target - RIM * (i + RIM)) % LON, 1)
        row = jnp.where((lane >= target) & (lane < target + RIM), side, row)
    return jnp.concatenate([s_ref[i, :B, :], row], axis=0)


def basis(parts_ref, s_ref, west_ref, east_ref, q_hbm, alpha_hbm, beta_hbm,
          q_ref, alpha_ref, beta_ref, high_ref, middle_ref, low_ref, sems):
    for i in range(0, LAT, 2):
        pair = [whole_row(j, s_ref, west_ref, east_ref) for j in (i, i + 1)]
        a, b, c = split(jnp.concatenate(pair, axis=1))
        high_ref[i // 2] = a
        middle_ref[i // 2] = b
        low_ref[i // 2] = c
    total = parts_ref[0]
    for i in range(1, parts_ref.shape[0]):
        total += parts_ref[i]
    inverse, upper = factor(*unpack(total * (1.0 / CELLS)))
    lane = lax.broadcasted_iota(jnp.int32, (ALL, ALL), 1)
    image = jnp.where(lane < ITERS * B, inverse, 0.0) + jnp.where(lane >= B, pltpu.roll(inverse, B, 1), 0.0)
    coeffs = lax.dot_general(upper, image, NT, precision=HIGH, preferred_element_type=jnp.float32)
    for k in range(ITERS):
        here, after = slice(k * B, (k + 1) * B), slice((k + 1) * B, (k + 2) * B)
        alpha_ref[k] = coeffs[here, here]
        beta_ref[k] = coeffs[after, here]
    copies = [
        pltpu.make_async_copy(alpha_ref, alpha_hbm, sems.at[0]),
        pltpu.make_async_copy(beta_ref, beta_hbm, sems.at[1]),
    ]
    for copy in copies:
        copy.start()
    high, middle, low = split(inverse)
    two = jnp.concatenate([high, middle], axis=1)
    three = jnp.concatenate([high, middle, low], axis=1)
    dot = lambda a, b: jnp.dot(a, b, preferred_element_type=jnp.float32)
    sub = lax.broadcasted_iota(jnp.int32, (8, LON), 0)
    for g in range(LAT // 8):
        rows = []
        for i in range(8 * g, 8 * g + 8, 2):
            a, b, c = high_ref[i // 2], middle_ref[i // 2], low_ref[i // 2]
            new = dot(three, jnp.concatenate([a, a, a], axis=0)) + dot(two, jnp.concatenate([b, b], axis=0)) + dot(high, c)
            rows += [new[:, :LON], new[:, LON:]]
        chunk = pl.ds(8 * g, 8)
        for v in range(0, ALL, 8):
            for t, tile in enumerate(swap([row[v:v + 8] for row in rows], sub)):
                q_ref[v + t, 8 * g:8 * g + 8, :] = tile
            if v % PIECE == PIECE - 8:
                block = pl.ds(v + 8 - PIECE, PIECE)
                sem = sems.at[len(copies)]
                copies.append(pltpu.make_async_copy(q_ref.at[block, chunk, :], q_hbm.at[block, chunk, :], sem))
                copies[-1].start()
    for copy in copies:
        copy.wait()


def body(start_block, sea_mask, depth_levels):
    x = start_block.reshape(B * LAT, LON)
    x, sea_mask, depth_levels = [pltpu.with_memory_space_constraint(v, pltpu.HBM) for v in (x, sea_mask, depth_levels)]
    edge = (RIM, B + 8, LON)
    anywhere = pl.BlockSpec(memory_space=pl.ANY)
    small = pltpu.VMEM((LAT, LON), jnp.int32)
    far, near, x, h = call(
        edge_rows,
        (edge, edge, (B * LAT, LON), (LAT, LON)),
        [small, small, pltpu.SemaphoreType.DMA((3,))],
        in_specs=[pl.BlockSpec(memory_space=pltpu.HBM)] * 3,
    )(x, sea_mask, depth_levels)
    far = lax.ppermute(far, ROW, [(i, ((i + 1) ^ 1) - 1) for i in range(1, 7)])
    near = lax.ppermute(near, ROW, [(i, i ^ 1) for i in range(8)])
    flat = (B + 8, LON)
    packs = (len(STARTS), B + 8, LON)
    core, part = call(core_rows, ((LAT, B + 8, LON), packs), flops=1 << 22, moved=1 << 20)(x, h)
    far, near, north, south, packed = call(side_columns, (flat, flat, edge, edge, packs))(far, near, part)
    far = lax.ppermute(far, COL, [(i, (((i + 1) ^ 1) - 1) % 32) for i in range(32)])
    near = lax.ppermute(near, COL, [(i, i ^ 1) for i in range(32)])
    wide = pltpu.VMEM((ROWS, B, LON), jnp.float32)
    thin = pltpu.VMEM((ROWS, 8, LON), jnp.float32)
    square = (ALL, ALL)
    s, own = call(
        inside, ((LAT, ALL, LON), square), [wide, wide, thin, thin, thin], flops=1 << 28, moved=1 << 23
    )(core, north, south)
    rim = (ALL - B, LON)
    gram, west, east = call(border, ((B, LON), rim, rim))(far, near, packed, own)
    other = lax.ppermute(gram, ROW, [(i, i ^ 1) for i in range(8)])
    copies = call(join, ((16, B, LON),))(gram, other)[0]
    parts = lax.all_to_all(copies, ("x", "y"), 0, 0)
    copies = call(spread, ((8, B, LON),))(parts)[0]
    parts = lax.all_to_all(copies, "z", 0, 0)
    table = (ITERS, B, B)
    results = ((ALL, LAT, LON), table, table)
    return call(
        basis,
        results,
        [pltpu.VMEM(shape, jnp.float32) for shape in results]
        + [pltpu.VMEM((LAT // 2, ALL, 2 * LON), jnp.bfloat16)] * 3
        + [pltpu.SemaphoreType.DMA((2 + (LAT // 8) * (ALL // PIECE),))],
        out_specs=(anywhere,) * 3,
    )(parts, s, west, east)


def solution(mesh):
    torus = Mesh(mesh.devices.reshape(4, 2, 8, 4), ("x", "core", "z", "y"))
    in_specs = (P(None, ROW, COL), P(ROW, COL), P(ROW, COL))
    out_specs = (P(None, ROW, COL), P(), P())
    return jax.shard_map(body, mesh=torus, in_specs=in_specs, out_specs=out_specs, check_vma=False)
```
